128 devices in a mesh: dp: 32 (over z, x, core), hid: 4 (over y).
Axes of the slice: x: 4, y: 4, z: 4, core: 2. Of those that a mesh axis runs over, the one named last changes fastest.
Arguments:
- features: bfloat16 [16384, 80], P('dp'), may hold values from -6 to 6
- lengths: int32 [32], P('dp'), may hold values from 128 to 512, as said below
- routes: int32 [2, 16384, 1], P(None, 'dp'), may hold values from 0 to 31; in each aligned block of 512 rows (0 to 511, 512 to 1023, ..., all dimensions but the last counted through in order) at most 24 rows name the same one
- alignments: int32 [16384], P('dp'), may hold values from 0 to 4095
- input_weight: float32 [80, 512], P(None, 'dp'), may hold values from -0.625 to 0.625
- attention_in: float32 [512, 1536], P('dp'), may hold values from -0.25 to 0.25
- branch_out: float32 [2, 512, 512], P(None, 'dp'), may hold values from -0.5 to 0.5
- pointwise_in: float32 [512, 1024], P('dp'), may hold values from -0.25 to 0.25
- depthwise: float32 [15, 512], P(None, 'dp'), may hold values from -1.5 to 1.5
- router: float32 [2, 512, 32], P(None, 'dp'), may hold values from -0.19887379 to 0.19887379
- senone_table: float32 [512, 4096], P('dp', 'hid')
- norm_scales: float32 [7, 512], P(None, 'dp'), may hold values from 0.5 to 1.5
- expert_weights: float32 [2, 2, 32, 512, 2048], P(None, None, 'dp', None, 'hid')
- input_first: float32 [80, 512], P(None, 'dp'), may hold values from -5.722046e-06 to 5.722046e-06
- input_second: float32 [80, 512], P(None, 'dp'), may hold values from 6.589491e-14 to 2.6357963e-13
- attention_first: float32 [512, 1536], P('dp'), may hold values from -5.722046e-06 to 5.722046e-06
- attention_second: float32 [512, 1536], P('dp'), may hold values from 6.589491e-14 to 2.6357963e-13
- branch_first: float32 [2, 512, 512], P(None, 'dp'), may hold values from -5.722046e-06 to 5.722046e-06
- branch_second: float32 [2, 512, 512], P(None, 'dp'), may hold values from 6.589491e-14 to 2.6357963e-13
- pointwise_first: float32 [512, 1024], P('dp'), may hold values from -5.722046e-06 to 5.722046e-06
- pointwise_second: float32 [512, 1024], P('dp'), may hold values from 6.589491e-14 to 2.6357963e-13
- depthwise_first: float32 [15, 512], P(None, 'dp'), may hold values from -1.1444092e-05 to 1.1444092e-05
- depthwise_second: float32 [15, 512], P(None, 'dp'), may hold values from 2.6357963e-13 to 1.0543185e-12
- router_first: float32 [2, 512, 32], P(None, 'dp'), may hold values from -5.722046e-06 to 5.722046e-06
- router_second: float32 [2, 512, 32], P(None, 'dp'), may hold values from 6.589491e-14 to 2.6357963e-13
- senone_first: float32 [512, 4096], P('dp', 'hid'), may hold values from -5.722046e-06 to 5.722046e-06
- senone_second: float32 [512, 4096], P('dp', 'hid'), may hold values from 6.589491e-14 to 2.6357963e-13
- scales_first: float32 [7, 512], P(None, 'dp'), may hold values from -1.1444092e-05 to 1.1444092e-05
- scales_second: float32 [7, 512], P(None, 'dp'), may hold values from 2.6357963e-13 to 1.0543185e-12
- expert_momentum: float32 [2, 2, 32, 512, 2048], P(None, None, 'dp', None, 'hid')
Outputs:
- loss_sum: float32 [], replicated
- frame_count: float32 [], replicated
- grad_norm: float32 [], replicated
- input_first_new: float32 [80, 512], P(None, 'dp')
- input_second_new: float32 [80, 512], P(None, 'dp')
- input_new: float32 [80, 512], P(None, 'dp')
- attention_first_new: float32 [512, 1536], P('dp')
- attention_second_new: float32 [512, 1536], P('dp')
- attention_new: float32 [512, 1536], P('dp')
- branch_first_new: float32 [2, 512, 512], P(None, 'dp')
- branch_second_new: float32 [2, 512, 512], P(None, 'dp')
- branch_new: float32 [2, 512, 512], P(None, 'dp')
- pointwise_first_new: float32 [512, 1024], P('dp')
- pointwise_second_new: float32 [512, 1024], P('dp')
- pointwise_new: float32 [512, 1024], P('dp')
- depthwise_first_new: float32 [15, 512], P(None, 'dp')
- depthwise_second_new: float32 [15, 512], P(None, 'dp')
- depthwise_new: float32 [15, 512], P(None, 'dp')
- router_first_new: float32 [2, 512, 32], P(None, 'dp')
- router_second_new: float32 [2, 512, 32], P(None, 'dp')
- router_new: float32 [2, 512, 32], P(None, 'dp')
- senone_first_new: float32 [512, 4096], P('dp', 'hid')
- senone_second_new: float32 [512, 4096], P('dp', 'hid')
- senone_new: float32 [512, 4096], P('dp', 'hid')
- scales_first_new: float32 [7, 512], P(None, 'dp')
- scales_second_new: float32 [7, 512], P(None, 'dp')
- scales_new: float32 [7, 512], P(None, 'dp')
- momentum_new: float32 [2, 2, 32, 512, 2048], P(None, None, 'dp', None, 'hid')
- experts_new: float32 [2, 2, 32, 512, 2048], P(None, None, 'dp', None, 'hid')
The draws below stay inside these ranges and needn't reach their ends.
Inputs may be any that keep to these rules, and one draw needn't show every extreme that they name: `lengths`: each utterance has at least a quarter of its 512 padded frames; the last utterance fills all 512. `routes`: within one utterance's frames of one feed-forward no expert is named more than 24 times, a bound that some block reaches.
All inputs are finite; a program needn't handle non-finite values.
Results may differ from the reference program's by a relative error of at most 0.015.
Values may be sent and summed in bfloat16 or wider, within the bound.
No kernel may reach another device: no remote copies, remote signals or barrier semaphores. Data moves between devices by JAX's collectives and lax.ppermute only.
A program may use at most 192 MiB of HBM per device.

```python
import math
import jax
import jax.numpy as jnp
import numpy as np
from jax import lax

D = 512
HEADS = 8
HEAD_DIM = 64
FF = 2048
V = 4096
F = 80
KERNEL = 15
STEP = 10
TOK_DEV = 512
UTTS = 32
EXPERTS = 32
TOKENS = 16384
CAP = 24
DENSE = 3973120
PARAMS = 138234880


def draw_lengths(key, part):
    key = jax.random.fold_in(key, 11)
    index = jnp.arange(UTTS, dtype=jnp.int32)
    base = TOK_DEV // 3 + 2 * TOK_DEV // 3 * index // max(UTTS - 1, 1)
    jitter = jax.random.randint(key, (UTTS,), 0, TOK_DEV // 8 + 1)
    drawn = jnp.maximum(base - jitter, TOK_DEV // 4)
    return jnp.where(index == UTTS - 1, TOK_DEV, drawn).astype(jnp.int32)


def draw_senone_table(key, part):
    key = jax.random.fold_in(key, 12)
    columns = jnp.arange(V, dtype=jnp.float32) / (V - 1)
    noise = jax.random.normal(key, (D, V), jnp.float32)
    spread = 1.0 + 2.0 * columns
    return noise * spread[None, :] * D ** (-0.5)


def draw_expert_weights(key, part):
    key = jax.random.fold_in(key, 13)
    shape = (2, 2, EXPERTS, D, FF)
    noise = jax.random.normal(key, shape, jnp.float32)
    kind_scale = jnp.array([D ** (-0.5), 3.0 * EXPERTS * FF ** (-0.5)], jnp.float32)
    return noise * kind_scale[None, :, None, None, None]


def draw_expert_momentum(key, part):
    key = jax.random.fold_in(key, 14)
    shape = (2, 2, EXPERTS, D, FF)
    noise = jax.random.normal(key, shape, jnp.float32)
    kind_scale = jnp.array([1.0, 1.0 / EXPERTS], jnp.float32) * (0.02 * PARAMS ** (-0.5))
    return noise * kind_scale[None, :, None, None, None]


def touch_ends(values, key, least, high):
    spot = [jax.random.randint(jax.random.fold_in(key, axis), (), 0, length) for axis, length in enumerate(values.shape)]
    longest = values.shape.index(max(values.shape))
    beside = spot[:longest] + [(spot[longest] + 1) % values.shape[longest]] + spot[longest + 1:]
    return values.at[tuple(spot)].set(least).at[tuple(beside)].set(high)


def levels(rng, dims, cuts, least, top_value):
    factor_of, own = 1.0, jax.random.fold_in(rng, 6)
    for dim, parts in cuts:
        draws = jnp.exp(jax.random.uniform(jax.random.fold_in(own, dim), (parts,), jnp.float32, least / len(cuts), top_value / len(cuts)))
        factor_of = factor_of * jnp.repeat(draws, dims[dim] // parts).reshape([-1 if axis == dim else 1 for axis in range(len(dims))])
    return factor_of


def cumulative_ranks(number_of, lean):
    portions = [(1 << 20) // math.isqrt(grade ** lean) + 1 for grade in range(1, number_of + 1)]
    scale = 1 + sum(portions) // (1 << 30)
    return np.cumsum(np.array([max(1, weight // scale) for weight in portions]))


def skewed_ids(stream_key, shape, count, slope):
    listing = cumulative_ranks(count, slope)
    lot = jax.random.randint(jax.random.fold_in(stream_key, 1), shape, 0, int(listing[count - 1]))
    rank = jnp.searchsorted(jnp.asarray(listing, jnp.int32), lot, side="right")
    return jax.random.permutation(jax.random.fold_in(stream_key, 2), count)[rank].astype(jnp.int32)


def assign_block(stream_key, own, number, rows, amount, top, bound, slope):
    order = jax.random.permutation(stream_key, amount)
    packed, common = shares(amount, rows * top, bound, slope, True), shares(amount, rows * top, bound, slope, False)
    places = jnp.arange(amount)

    def named(tallies, rotation):
        used = int((tallies > 0).sum())
        fixed = max(1, used // 4)
        moved = fixed + (places - fixed + rotation * (used - fixed)) % max(1, amount - fixed)
        return jnp.zeros((amount,), jnp.int32).at[order[jnp.where(places < fixed, places, moved)]].set(jnp.asarray(tallies, jnp.int32))

    tallies = jnp.where(number % 4 == 0, named(packed, number // 4), named(common, number - number // 4 - 1))
    mixed = jax.random.permutation(jax.random.fold_in(own, 3), amount)
    source_of, sink = mixed[0:amount // 2 * 2:2], mixed[1:amount // 2 * 2:2]
    slack = jnp.minimum(tallies[source_of] - 1, bound - tallies[sink]) // 2
    slack = jnp.where((source_of == order[0]) | (sink == order[0]) | (tallies[sink] == 0), 0, jnp.maximum(slack, 0))
    moved = jax.random.randint(jax.random.fold_in(own, 4), (amount // 2,), 0, 1 << 20) % (slack + 1)
    tallies = tallies.at[source_of].add(-moved).at[sink].add(moved)
    labels = jnp.searchsorted(jnp.cumsum(tallies), jnp.arange(rows * top), side="right").astype(jnp.int32)
    grid = labels.reshape(top, rows).T
    grid = grid[jax.random.permutation(jax.random.fold_in(own, 1), rows)]
    rotation = jax.random.randint(jax.random.fold_in(own, 2), (rows, 1), 0, top)
    return jnp.take_along_axis(grid, (jnp.arange(top)[None, :] + rotation) % top, axis=1)


def shares(amount, total, bound, skew, full):
    portions = [(1 << 20) // math.isqrt(rank ** skew) + 1 for rank in range(1, amount + 1)]
    largest = bound if full else min(bound, max(-(-total // amount), total * portions[0] // sum(portions)))
    least = 1 if total - largest >= amount - 1 else 0
    given, spare = [largest] + [least] * (amount - 1), total - largest - least * (amount - 1)
    while spare > 0:
        free = [i for i in range(1, amount) if given[i] < largest] or [i for i in range(1, amount) if given[i] < bound]
        mass, budget = sum([portions[i] for i in free]), spare
        for i in free:
            addition = min(bound - given[i], max(1, budget * portions[i] // mass), spare)
            given[i] = given[i] + addition
            spare = spare - addition
    return np.array(given)


def centred(stream_key, dims, scale, bound, split=(), kind=jnp.bfloat16):
    result = scale * jax.random.normal(stream_key, dims, jnp.float32)
    if split:
        result = result * levels(stream_key, dims, split, -0.22, 0.18)
    return jnp.clip(result, -bound, bound).astype(kind)


def setup_inputs(seed: int = 0) -> dict:
    arg_keys = jax.random.split(jax.random.key(seed), 31)
    features = centred(arg_keys[0], (TOKENS, F), 1.0, 6.0, ((0, 32),))
    lengths = draw_lengths(jax.random.fold_in(arg_keys[30], 71), 0)
    routes_keys = jax.random.split(jax.random.fold_in(arg_keys[2], 1), 2 * TOKENS // TOK_DEV)
    routes_turns = jax.random.permutation(jax.random.fold_in(arg_keys[2], 3), 2 * TOKENS // TOK_DEV)
    routes = jax.vmap(lambda own, number: assign_block(jax.random.fold_in(arg_keys[2], 2), own, number, TOK_DEV, EXPERTS, 1, CAP, 1))(routes_keys, routes_turns).reshape((2, TOKENS, 1))
    alignments = touch_ends(skewed_ids(arg_keys[3], (TOKENS,), V, 2), jax.random.fold_in(arg_keys[3], 3), 0, V - 1).astype(jnp.int32)
    input_weight = centred(arg_keys[4], (F, D), F ** -0.5, 0.625, ((1, 32),), jnp.float32)
    attention_in = centred(arg_keys[5], (D, 3 * D), D ** -0.5, 0.25, ((0, 32),), jnp.float32)
    branch_out = centred(arg_keys[6], (2, D, D), (D // 4) ** -0.5, 0.5, ((1, 32),), jnp.float32)
    pointwise_in = centred(arg_keys[7], (D, 2 * D), D ** -0.5, 0.25, ((0, 32),), jnp.float32)
    depthwise = centred(arg_keys[8], (KERNEL, D), KERNEL ** -0.5, 1.5, ((1, 32),), jnp.float32)
    router = centred(arg_keys[9], (2, D, EXPERTS), (0.75 * D ** -0.5), 0.19887379, ((1, 32),), jnp.float32)
    senone_table = draw_senone_table(jax.random.fold_in(arg_keys[30], 71), 0)
    norm_scales = jnp.clip(1.0 + 0.1 * jax.random.normal(arg_keys[11], (7, D), jnp.float32), 0.5, 1.5)
    expert_weights = draw_expert_weights(jax.random.fold_in(arg_keys[30], 71), 0)
    input_first = centred(arg_keys[13], (F, D), (0.0022 * (DENSE + 2 * D * FF) ** -0.5), 5.7220458984375e-06, ((1, 32),), jnp.float32)
    input_second = jnp.clip(jnp.exp(math.log(2.6357963121143024e-13) - 1.3862944 * jax.random.uniform(arg_keys[14], (F, D), jnp.float32) ** levels(arg_keys[14], (F, D), ((1, 32),), -0.2, 0.2)), 6.589490780285756e-14, 2.6357963121143024e-13)
    attention_first = centred(arg_keys[15], (D, 3 * D), (0.0022 * (DENSE + 2 * D * FF) ** -0.5), 5.7220458984375e-06, ((0, 32),), jnp.float32)
    attention_second = jnp.clip(jnp.exp(math.log(2.6357963121143024e-13) - 1.3862944 * jax.random.uniform(arg_keys[16], (D, 3 * D), jnp.float32) ** levels(arg_keys[16], (D, 3 * D), ((0, 32),), -0.2, 0.2)), 6.589490780285756e-14, 2.6357963121143024e-13)
    branch_first = centred(arg_keys[17], (2, D, D), (0.0022 * (DENSE + 2 * D * FF) ** -0.5), 5.7220458984375e-06, ((1, 32),), jnp.float32)
    branch_second = jnp.clip(jnp.exp(math.log(2.6357963121143024e-13) - 1.3862944 * jax.random.uniform(arg_keys[18], (2, D, D), jnp.float32) ** levels(arg_keys[18], (2, D, D), ((1, 32),), -0.2, 0.2)), 6.589490780285756e-14, 2.6357963121143024e-13)
    pointwise_first = centred(arg_keys[19], (D, 2 * D), (0.0022 * (DENSE + 2 * D * FF) ** -0.5), 5.7220458984375e-06, ((0, 32),), jnp.float32)
    pointwise_second = jnp.clip(jnp.exp(math.log(2.6357963121143024e-13) - 1.3862944 * jax.random.uniform(arg_keys[20], (D, 2 * D), jnp.float32) ** levels(arg_keys[20], (D, 2 * D), ((0, 32),), -0.2, 0.2)), 6.589490780285756e-14, 2.6357963121143024e-13)
    depthwise_first = centred(arg_keys[21], (KERNEL, D), (0.0044 * (DENSE + 2 * D * FF) ** -0.5), 1.1444091796875e-05, ((1, 32),), jnp.float32)
    depthwise_second = jnp.clip(jnp.exp(math.log(1.054318524845721e-12) - 1.3862944 * jax.random.uniform(arg_keys[22], (KERNEL, D), jnp.float32) ** levels(arg_keys[22], (KERNEL, D), ((1, 32),), -0.2, 0.2)), 2.6357963121143024e-13, 1.054318524845721e-12)
    router_first = centred(arg_keys[23], (2, D, EXPERTS), (0.0022 * (DENSE + 2 * D * FF) ** -0.5), 5.7220458984375e-06, ((1, 32),), jnp.float32)
    router_second = jnp.clip(jnp.exp(math.log(2.6357963121143024e-13) - 1.3862944 * jax.random.uniform(arg_keys[24], (2, D, EXPERTS), jnp.float32) ** levels(arg_keys[24], (2, D, EXPERTS), ((1, 32),), -0.2, 0.2)), 6.589490780285756e-14, 2.6357963121143024e-13)
    senone_first = centred(arg_keys[25], (D, V), (0.0022 * (DENSE + 2 * D * FF) ** -0.5), 5.7220458984375e-06, ((0, 32), (1, 4)), jnp.float32)
    senone_second = jnp.clip(jnp.exp(math.log(2.6357963121143024e-13) - 1.3862944 * jax.random.uniform(arg_keys[26], (D, V), jnp.float32) ** levels(arg_keys[26], (D, V), ((0, 32), (1, 4)), -0.2, 0.2)), 6.589490780285756e-14, 2.6357963121143024e-13)
    scales_first = centred(arg_keys[27], (7, D), (0.0044 * (DENSE + 2 * D * FF) ** -0.5), 1.1444091796875e-05, ((1, 32),), jnp.float32)
    scales_second = jnp.clip(jnp.exp(math.log(1.054318524845721e-12) - 1.3862944 * jax.random.uniform(arg_keys[28], (7, D), jnp.float32) ** levels(arg_keys[28], (7, D), ((1, 32),), -0.2, 0.2)), 2.6357963121143024e-13, 1.054318524845721e-12)
    expert_momentum = draw_expert_momentum(jax.random.fold_in(arg_keys[30], 71), 0)
    return dict(features=features, lengths=lengths, routes=routes, alignments=alignments, input_weight=input_weight, attention_in=attention_in, branch_out=branch_out, pointwise_in=pointwise_in, depthwise=depthwise, router=router, senone_table=senone_table, norm_scales=norm_scales, expert_weights=expert_weights, input_first=input_first, input_second=input_second, attention_first=attention_first, attention_second=attention_second, branch_first=branch_first, branch_second=branch_second, pointwise_first=pointwise_first, pointwise_second=pointwise_second, depthwise_first=depthwise_first, depthwise_second=depthwise_second, router_first=router_first, router_second=router_second, senone_first=senone_first, senone_second=senone_second, scales_first=scales_first, scales_second=scales_second, expert_momentum=expert_momentum)


@jax.custom_vjp
def low(v):
    return lax.optimization_barrier(v.astype(jnp.bfloat16)).astype(jnp.float32)

@jax.custom_vjp
def low_back(v):
    return v

def low_keep(v):
    return (low(v), None)

def low_pass(kept, grad):
    return (grad,)

def back_keep(v):
    return (v, None)

def back_low(kept, grad):
    return (low(grad),)
low.defvjp(low_keep, low_pass)
low_back.defvjp(back_keep, back_low)
clip_limit = 0.02
beta_one = 0.9
beta_two = 0.999
adam_epsilon = 1e-08
adam_rate = 0.2
gain_rate = 0.6
weight_decay = 0.01
muon_beta = 0.95
muon_rate = 1.0
muon_decay = 0.01
newton_first = 3.4445
newton_second = -4.775
newton_third = 2.0315

def product(left, right):
    return jnp.dot(left, right, precision=lax.Precision.HIGHEST)

def layer_norm(values, gain):
    centered = values - lax.optimization_barrier(jnp.mean(values, -1, keepdims=True))
    return centered * lax.rsqrt(lax.optimization_barrier(jnp.mean(centered * centered, -1, keepdims=True)) + 1e-05) * gain

def slot_positions(route_rows):
    table = route_rows.reshape(UTTS, TOK_DEV)
    onehot = (table[:, :, None] == jnp.arange(EXPERTS, dtype=jnp.int32)).astype(jnp.int32)
    earlier = jnp.cumsum(onehot, 1) - onehot
    slot = lax.optimization_barrier(jnp.sum(earlier * onehot, -1))
    owner = jnp.arange(UTTS, dtype=jnp.int32)[:, None]
    return (table * (UTTS * CAP) + owner * CAP + slot).reshape(-1).astype(jnp.int32)

def mixture(values, gain, router_part, expert_part, route_rows):
    normed = layer_norm(values, gain)
    chances = jax.nn.softmax(product(normed, router_part), -1)
    onehot = (route_rows[:, None] == jnp.arange(EXPERTS, dtype=jnp.int32)).astype(jnp.float32)
    gate = lax.optimization_barrier(jnp.sum(chances * onehot, -1))
    position = slot_positions(route_rows)
    buffer = jnp.zeros((EXPERTS * UTTS * CAP, D), jnp.float32).at[position].set(low(normed))
    buffer = low_back(buffer).reshape(EXPERTS, UTTS * CAP, D)
    matrices = low(expert_part)
    active = low_back(jnp.einsum('erd,edf->erf', buffer, matrices[0], precision=lax.Precision.HIGHEST))
    hidden = low(jax.nn.silu(active))
    output = jnp.einsum('erf,edf->erd', hidden, matrices[1], precision=lax.Precision.HIGHEST)
    output = low(low_back(output)).reshape(-1, D)
    return gate[:, None] * output[position]

def attention(values, gain, weight_in, weight_out, valid):
    normed = layer_norm(values, gain)
    project = low_back(product(low(normed), low(weight_in)))
    shaped = project.reshape(UTTS, TOK_DEV, 3, HEADS, HEAD_DIM)
    queries = low(shaped[:, :, 0])
    keys = low(shaped[:, :, 1])
    contents = low(shaped[:, :, 2])
    scores = jnp.einsum('uqhd,ukhd->uhqk', queries, keys, precision=lax.Precision.HIGHEST)
    scores = low_back(scores * HEAD_DIM ** (-0.5))
    scores = jnp.where(valid[:, None, None, :] > 0, scores, -1e+30)
    weights = jax.nn.softmax(scores, -1)
    context = jnp.einsum('uhqk,ukhd->uqhd', low(weights), contents, precision=lax.Precision.HIGHEST)
    context = low_back(context).reshape(-1, D)
    return low_back(product(low(context), low(weight_out)))

def convolution(values, gains, weight_in, depth, weight_out, valid):
    normed = layer_norm(values, gains[2])
    project = low_back(product(low(normed), low(weight_in)))
    mixed = project[:, :D] * jax.nn.sigmoid(project[:, D:]) * valid.reshape(-1)[:, None]
    reach = (KERNEL - 1) // 2
    padded = jnp.pad(mixed.reshape(UTTS, TOK_DEV, D), ((0, 0), (reach, reach), (0, 0)))
    deep = jnp.zeros((UTTS, TOK_DEV, D), jnp.float32)
    for offset in range(KERNEL):
        deep = deep + depth[offset] * padded[:, offset:offset + TOK_DEV]
    count = lax.optimization_barrier(jnp.sum(valid, 1))[:, None, None]
    mask = valid[:, :, None]
    mean = lax.optimization_barrier(jnp.sum(mask * deep, 1, keepdims=True)) / count
    spread = lax.optimization_barrier(jnp.sum(mask * deep * deep, 1, keepdims=True)) / count - mean * mean
    shifted = (deep - mean) * lax.rsqrt(spread + 1e-05) * gains[5] + gains[6]
    activated = jax.nn.silu(shifted).reshape(-1, D)
    return low_back(product(low(activated), low(weight_out)))

def senone_loss(values, gain, table, targets, valid):
    normed = layer_norm(values, gain)
    logits = low_back(product(low(normed), low(table)))
    top = lax.optimization_barrier(jnp.max(logits, -1, keepdims=True))
    log_total = top[:, 0] + jnp.log(lax.optimization_barrier(jnp.sum(jnp.exp(logits - top), -1)))
    target = jnp.take_along_axis(logits, targets[:, None], -1)[:, 0]
    return jnp.sum(valid.reshape(-1) * (log_total - target))

def orthogonal(matrix):
    current = matrix / (jnp.sqrt(jnp.sum(matrix * matrix)) + 1e-07)
    for turn in range(5):
        gram = product(current, current.T)
        poly = newton_second * gram + newton_third * product(gram, gram)
        current = newton_first * current + product(poly, current)
    return current

def adam_update(weight, grad, first, second, rate, decay):
    first_new = beta_one * first + (1.0 - beta_one) * grad
    second_new = beta_two * second + (1.0 - beta_two) * grad * grad
    corrected = first_new / (1.0 - beta_one ** STEP) / (jnp.sqrt(second_new / (1.0 - beta_two ** STEP)) + adam_epsilon)
    return (first_new, second_new, weight - rate * (corrected + decay * weight))

def reference(features, lengths, routes, alignments, input_weight, attention_in, branch_out, pointwise_in, depthwise, router, senone_table, norm_scales, expert_weights, input_first, input_second, attention_first, attention_second, branch_first, branch_second, pointwise_first, pointwise_second, depthwise_first, depthwise_second, router_first, router_second, senone_first, senone_second, scales_first, scales_second, expert_momentum):
    valid = (jnp.arange(TOK_DEV, dtype=jnp.int32)[None, :] < lengths[:, None]).astype(jnp.float32)
    inputs = features.astype(jnp.float32)
    route_rows = routes[:, :, 0]

    def forward(w_input, w_attention, w_branch, w_pointwise, w_depth, w_router, w_senone, w_scales, w_experts):
        start = low_back(product(low(inputs), low(w_input)))
        first = start + 0.5 * mixture(start, w_scales[0], w_router[0], w_experts[0], route_rows[0])
        second = first + attention(first, w_scales[1], w_attention, w_branch[0], valid)
        third = second + convolution(second, w_scales, w_pointwise, w_depth, w_branch[1], valid)
        fourth = third + 0.5 * mixture(third, w_scales[3], w_router[1], w_experts[1], route_rows[1])
        return senone_loss(fourth, w_scales[4], w_senone, alignments, valid)
    loss_sum, pull = jax.vjp(forward, input_weight, attention_in, branch_out, pointwise_in, depthwise, router, senone_table, norm_scales, expert_weights)
    grads = pull(jnp.float32(1.0))
    count = jnp.sum(valid)
    scaled = [grad / count for grad in grads]
    norm = jnp.sqrt(sum((jnp.sum(grad * grad) for grad in scaled)))
    factor = jnp.minimum(1.0, clip_limit / (norm + 1e-06))
    input_first_new, input_second_new, input_new = adam_update(input_weight, scaled[0] * factor, input_first, input_second, adam_rate, weight_decay)
    attention_first_new, attention_second_new, attention_new = adam_update(attention_in, scaled[1] * factor, attention_first, attention_second, adam_rate, weight_decay)
    branch_first_new, branch_second_new, branch_new = adam_update(branch_out, scaled[2] * factor, branch_first, branch_second, adam_rate, weight_decay)
    pointwise_first_new, pointwise_second_new, pointwise_new = adam_update(pointwise_in, scaled[3] * factor, pointwise_first, pointwise_second, adam_rate, weight_decay)
    depthwise_first_new, depthwise_second_new, depthwise_new = adam_update(depthwise, scaled[4] * factor, depthwise_first, depthwise_second, adam_rate, weight_decay)
    router_first_new, router_second_new, router_new = adam_update(router, scaled[5] * factor, router_first, router_second, adam_rate, weight_decay)
    senone_first_new, senone_second_new, senone_new = adam_update(senone_table, scaled[6] * factor, senone_first, senone_second, adam_rate, weight_decay)
    scales_first_new, scales_second_new, scales_new = adam_update(norm_scales, scaled[7] * factor, scales_first, scales_second, gain_rate, 0.0)
    momentum_new = muon_beta * expert_momentum + scaled[8] * factor
    orth = lax.map(orthogonal, momentum_new.reshape(-1, D, FF)).reshape(momentum_new.shape)
    kind_scale = jnp.array([D ** (-0.5), 3 * EXPERTS * FF ** (-0.5)], jnp.float32) * (muon_rate * FF ** 0.5)
    experts_new = (1.0 - muon_decay) * expert_weights - kind_scale[None, :, None, None, None] * orth
    return (loss_sum, count, norm, input_first_new, input_second_new, input_new, attention_first_new, attention_second_new, attention_new, branch_first_new, branch_second_new, branch_new, pointwise_first_new, pointwise_second_new, pointwise_new, depthwise_first_new, depthwise_second_new, depthwise_new, router_first_new, router_second_new, router_new, senone_first_new, senone_second_new, senone_new, scales_first_new, scales_second_new, scales_new, momentum_new, experts_new)
```

```python
import jax
import jax.numpy as jnp
from jax import lax
from jax.experimental import pallas as pl
from jax.experimental.pallas import tpu as pltpu
from jax.sharding import PartitionSpec as P

D = 512
HEADS = 8
HEAD_DIM = 64
FF = 2048
STEP = 10


clip_limit = 0.02
beta_one = 0.9
beta_two = 0.999
adam_epsilon = 1e-08
adam_rate = 0.2
gain_rate = 0.6
weight_decay = 0.01
muon_beta = 0.95
muon_rate = 1.0
muon_decay = 0.01
newton_first = 3.4445
newton_second = -4.775
newton_third = 2.0315


def shift(values, step):
    size = lax.axis_size("hid")
    return lax.ppermute(values, "hid", [(i, (i + step) % size) for i in range(size)])


def gather_near(values):
    return [values] + [shift(values, step) for step in range(1, lax.axis_size("hid"))]


def gather_far(values):
    half = values.shape[0] // 2
    before, after = shift(values, 1), shift(values, -1)
    across = jnp.concatenate([shift(before[:half], 1), shift(after[half:], -1)])
    return [values, before, across, after]


def in_order(blocks, axis):
    size = len(blocks)
    width = blocks[0].shape[axis]
    rising = [blocks[(-1 - place) % size] for place in range(size)]
    doubled = jnp.concatenate(rising + rising[:-1], axis)
    begin = (size - 1 - lax.axis_index("hid")) % size
    return lax.dynamic_slice_in_dim(doubled, begin * width, size * width, axis)


def own_part(values, axis):
    width = values.shape[axis] // lax.axis_size("hid")
    return lax.dynamic_slice_in_dim(values, lax.axis_index("hid") * width, width, axis)


def exchange_rows(values):
    return lax.all_to_all(values, "dp", split_axis=0, concat_axis=0, tiled=True)


def summed_shares(values):
    owners = lax.axis_size("dp")
    moved = exchange_rows(to_low(values).reshape(owners, values.shape[0] // owners, -1))
    return jnp.sum(moved.astype(jnp.float32), 0)


def to_low(values):
    return values.astype(jnp.bfloat16)


def dot_low(left, right):
    return jnp.dot(left, right, preferred_element_type=jnp.float32)


def dot_left(left, right):
    return lax.dot_general(
        left, right, (((0,), (0,)), ((), ())), preferred_element_type=jnp.float32
    )


def dot_right(left, right):
    return lax.dot_general(
        left, right, (((1,), (1,)), ((), ())), preferred_element_type=jnp.float32
    )


def exact_dot(left, right):
    return jnp.dot(left, right, precision=lax.Precision.HIGHEST)


def norm_forward(values, gain):
    centered = values - jnp.mean(values, -1, keepdims=True)
    inverse = lax.rsqrt(jnp.mean(centered * centered, -1, keepdims=True) + 1e-05)
    unit = centered * inverse
    return (unit * gain, unit, inverse)


def norm_backward(grad, unit, inverse, gain):
    scaled = grad * gain
    back = inverse * (
        scaled
        - jnp.mean(scaled, -1, keepdims=True)
        - unit * jnp.mean(scaled * unit, -1, keepdims=True)
    )
    return (back, jnp.sum(grad * unit, 0))


def silu_slope(values):
    sigma = jax.nn.sigmoid(values)
    return sigma * (1.0 + values * (1.0 - sigma))


def two_parts(values):
    high = to_low(values)
    return high, to_low(values - high.astype(jnp.float32))


def close_dot(left, right):
    return dot_low(left[0], right[0]) + (dot_low(left[0], right[1]) + dot_low(left[1], right[0]))


def orthogonal_kernel(factor_ref, momentum_ref, grad_ref, out_ref, matrix_ref):
    pieces = momentum_ref.shape[0]
    gram = jnp.zeros((D, D), jnp.float32)
    for piece in range(pieces):
        current = muon_beta * momentum_ref[piece] + factor_ref[0] * grad_ref[piece].astype(
            jnp.float32
        )
        matrix_ref[piece] = current
        high, low = two_parts(current)
        cross = dot_right(high, low)
        gram = gram + (dot_right(high, high) + (cross + cross.T))
    row = lax.broadcasted_iota(jnp.int32, (D, D), 0)
    column = lax.broadcasted_iota(jnp.int32, (D, D), 1)
    square = jnp.sum(jnp.where(row == column, gram, 0.0))
    inverse = 1.0 / (jnp.sqrt(square) + 1e-07)
    gram = gram * (inverse * inverse)
    identity = jnp.where(row == column, newton_first, 0.0)
    total = None
    for turn in range(5):
        parts = two_parts(gram)
        poly = identity + newton_second * gram + newton_third * close_dot(parts, parts)
        poly_parts = two_parts(poly)
        total = poly if total is None else close_dot(poly_parts, two_parts(total))
        if turn < 4:
            gram = close_dot(poly_parts, two_parts(close_dot(poly_parts, parts)))
    total_parts = two_parts(total * (inverse * factor_ref[1]))
    for piece in range(pieces):
        out_ref[piece] = to_low(close_dot(total_parts, two_parts(matrix_ref[piece])))


def orthogonal(scalars, momentum, grad):
    return pl.pallas_call(
        orthogonal_kernel,
        out_shape=jax.ShapeDtypeStruct(momentum.shape, jnp.bfloat16),
        in_specs=[
            pl.BlockSpec(memory_space=pltpu.SMEM),
            pl.BlockSpec(memory_space=pltpu.VMEM),
            pl.BlockSpec(memory_space=pltpu.VMEM),
        ],
        out_specs=pl.BlockSpec(memory_space=pltpu.VMEM),
        scratch_shapes=[pltpu.VMEM(momentum.shape, jnp.float32)],
        compiler_params=pltpu.CompilerParams(vmem_limit_bytes=48 * 1024 * 1024),
        cost_estimate=pl.CostEstimate(
            flops=30_000_000_000, bytes_accessed=10_000_000, transcendentals=0
        ),
    )(scalars, momentum, grad)


def adam_update(weight, grad, first, second, rate, decay):
    first_new = beta_one * first + (1.0 - beta_one) * grad
    second_new = beta_two * second + (1.0 - beta_two) * grad * grad
    corrected = (
        first_new
        / (1.0 - beta_one**STEP)
        / (jnp.sqrt(second_new / (1.0 - beta_two**STEP)) + adam_epsilon)
    )
    return (first_new, second_new, weight - rate * (corrected + decay * weight))


def mixture_forward(values, gain, router_part, weights_in, weights_out, route_rows):
    experts, splits = lax.axis_size("dp"), lax.axis_size("hid")
    capacity = 3 * values.shape[0] // (2 * experts)
    share = capacity // splits
    normed, unit, inverse = norm_forward(values, gain)
    onehot_int = (route_rows[:, None] == jnp.arange(experts, dtype=jnp.int32)[None, :]).astype(
        jnp.int32
    )
    earlier = jnp.cumsum(onehot_int, 0) - onehot_int
    slot = jnp.sum(earlier * onehot_int, 1)
    turned = (lax.axis_index("hid") - slot // share) % splits
    position = (turned * experts + route_rows) * share + slot % share
    dispatch = (
        jnp.arange(experts * capacity, dtype=jnp.int32)[:, None] == position[None, :]
    ).astype(jnp.bfloat16)
    onehot = onehot_int.astype(jnp.float32)
    own = dispatch[: experts * share]
    rows = exchange_rows(to_low(dot_low(own, to_low(normed))))
    chances = jax.nn.softmax(exact_dot(normed, router_part), -1)
    gate = jnp.sum(chances * onehot, 1)
    active = [dot_low(rows, weight) for weight in weights_in]
    hidden = [to_low(jax.nn.silu(part)) for part in active]
    returned = sum(dot_right(part, weight) for part, weight in zip(hidden, weights_out))
    back = jnp.concatenate(gather_near(exchange_rows(to_low(returned))))
    expert_out = dot_left(dispatch, back)
    kept = (
        unit,
        inverse,
        normed,
        chances,
        onehot,
        gate,
        dispatch,
        rows,
        active,
        hidden,
        expert_out,
    )
    return (0.5 * gate[:, None] * expert_out, kept)


def feature_pieces(rows, parts):
    splits = lax.axis_size("hid")
    return (
        jnp.concatenate(gather_near(rows)),
        jnp.concatenate(
            [parts[0]] + [shift(parts[splits - step], step) for step in range(1, splits)]
        ),
    )


def mixture_backward(grad, gain, router_part, weights_in, weights_out, kept):
    unit, inverse, normed, chances, onehot, gate, dispatch, rows, active, hidden, expert_out = kept
    experts, splits = lax.axis_size("dp"), lax.axis_size("hid")
    own = dispatch[: dispatch.shape[0] // splits]
    branch = 0.5 * grad
    rows_grad = exchange_rows(to_low(dot_low(own, to_low(gate[:, None] * branch))))
    active_grad = [
        to_low(dot_low(rows_grad, weight) * silu_slope(part))
        for weight, part in zip(weights_out, active)
    ]
    returned = sum(dot_right(part, weight) for part, weight in zip(active_grad, weights_in))
    back = jnp.concatenate(gather_near(exchange_rows(to_low(returned))))
    all_rows, all_active_grad = feature_pieces(rows, active_grad)
    all_rows_grad, all_hidden = feature_pieces(rows_grad, hidden)
    in_grad = dot_left(all_rows, all_active_grad)
    out_grad = dot_left(all_rows_grad, all_hidden)
    gate_grad = jnp.sum(branch * expert_out, 1)
    logit_grad = (gate * gate_grad)[:, None] * (onehot - chances)
    router_grad = exact_dot(normed.T, logit_grad)
    normed_grad = exact_dot(logit_grad, router_part.T) + dot_left(dispatch, back)
    values_grad, gain_grad = norm_backward(normed_grad, unit, inverse, gain)
    return (grad + values_grad, gain_grad, router_grad, in_grad, out_grad)


def attention_scores(queries, keys, valid):
    scores = jnp.einsum(
        "qhd,khd->hqk", queries, keys, preferred_element_type=jnp.float32
    ) * HEAD_DIM ** (-0.5)
    return jnp.where(valid[None, None, :] > 0, scores, -1e30)


def attention_forward(values, gain, weight_in, weight_out, valid):
    tokens = values.shape[0]
    normed, unit, inverse = norm_forward(values, gain)
    low_normed = to_low(normed)
    shaped = to_low(dot_low(low_normed, weight_in)).reshape(tokens, 3, HEADS, HEAD_DIM)
    queries, keys, contents = (shaped[:, 0], shaped[:, 1], shaped[:, 2])
    scores = attention_scores(queries, keys, valid)
    top = jnp.max(scores, -1, keepdims=True)
    raised = jnp.exp(scores - top)
    total = jnp.sum(raised, -1, keepdims=True)
    log_total = top + jnp.log(total)
    mixed = jnp.einsum(
        "hqk,khd->qhd", to_low(raised / total), contents, preferred_element_type=jnp.float32
    )
    context = to_low(mixed.reshape(tokens, -1))
    kept = (unit, inverse, low_normed, queries, keys, contents, log_total, context)
    return (dot_low(context, weight_out), kept)


def attention_backward(grad, gain, weight_in, weight_out, valid, kept):
    unit, inverse, low_normed, queries, keys, contents, log_total, context = kept
    tokens = grad.shape[0]
    low_grad = to_low(grad)
    out_grad = dot_left(context, own_part(low_grad, 1))
    context_grad = to_low(dot_right(low_grad, weight_out)).reshape(tokens, HEADS, HEAD_DIM)
    weights = jnp.exp(attention_scores(queries, keys, valid) - log_total)
    weight_grad = jnp.einsum(
        "qhd,khd->hqk", context_grad, contents, preferred_element_type=jnp.float32
    )
    content_grad = jnp.einsum(
        "hqk,qhd->khd", to_low(weights), context_grad, preferred_element_type=jnp.float32
    )
    score_grad = to_low(weights * (weight_grad - jnp.sum(weight_grad * weights, -1, keepdims=True)))
    query_grad = jnp.einsum(
        "hqk,khd->qhd", score_grad, keys, preferred_element_type=jnp.float32
    ) * HEAD_DIM ** (-0.5)
    key_grad = jnp.einsum(
        "hqk,qhd->khd", score_grad, queries, preferred_element_type=jnp.float32
    ) * HEAD_DIM ** (-0.5)
    project_grad = to_low(jnp.stack([query_grad, key_grad, content_grad], 1).reshape(tokens, -1))
    in_grad = dot_left(low_normed, own_part(project_grad, 1))
    values_grad, gain_grad = norm_backward(dot_right(project_grad, weight_in), unit, inverse, gain)
    return (grad + values_grad, gain_grad, in_grad, out_grad)


def convolution_forward(values, gains, weight_in, depth, weight_out, valid):
    tokens = values.shape[0]
    normed, unit, inverse = norm_forward(values, gains[2])
    low_normed = to_low(normed)
    project = dot_low(low_normed, weight_in)
    width = project.shape[1] // 2
    linear = project[:, :width]
    gating = jax.nn.sigmoid(project[:, width:])
    mixed = linear * gating * valid[:, None]
    reach = (depth.shape[0] - 1) // 2
    padded = jnp.pad(mixed, ((reach, reach), (0, 0)))
    deep = jnp.zeros_like(mixed)
    for offset in range(depth.shape[0]):
        deep = deep + depth[offset] * padded[offset : offset + tokens]
    count = jnp.sum(valid)
    mask = valid[:, None]
    mean = jnp.sum(mask * deep, 0) / count
    spread = jnp.sum(mask * deep * deep, 0) / count - mean * mean
    scale = lax.rsqrt(spread + 1e-05)
    unit_batch = (deep - mean) * scale
    shifted = unit_batch * gains[5] + gains[6]
    activated = to_low(jax.nn.silu(shifted))
    kept = (
        unit,
        inverse,
        low_normed,
        linear,
        gating,
        padded,
        scale,
        unit_batch,
        shifted,
        activated,
    )
    return (dot_low(activated, weight_out), kept)


def convolution_backward(grad, gains, weight_in, depth, weight_out, valid, kept):
    unit, inverse, low_normed, linear, gating, padded, scale, unit_batch, shifted, activated = kept
    tokens = grad.shape[0]
    low_grad = to_low(grad)
    out_grad = dot_left(activated, own_part(low_grad, 1))
    shifted_grad = dot_right(low_grad, weight_out) * silu_slope(shifted)
    gamma_grad = jnp.sum(shifted_grad * unit_batch, 0)
    beta_grad = jnp.sum(shifted_grad, 0)
    unit_grad = shifted_grad * gains[5]
    count = jnp.sum(valid)
    mask = valid[:, None]
    first_sum = jnp.sum(mask * unit_grad, 0) / count
    second_sum = jnp.sum(mask * unit_grad * unit_batch, 0) / count
    deep_grad = scale * (unit_grad - mask * (first_sum + unit_batch * second_sum))
    reach = (depth.shape[0] - 1) // 2
    padded_grad = jnp.pad(deep_grad, ((reach, reach), (0, 0)))
    mixed_grad = jnp.zeros_like(deep_grad)
    depth_rows = []
    for offset in range(depth.shape[0]):
        begin = 2 * reach - offset
        mixed_grad = mixed_grad + depth[offset] * padded_grad[begin : begin + tokens]
        depth_rows.append(jnp.sum(deep_grad * padded[offset : offset + tokens], 0))
    mixed_grad = mixed_grad * mask
    project_grad = to_low(
        jnp.concatenate([mixed_grad * gating, mixed_grad * linear * gating * (1.0 - gating)], 1)
    )
    in_grad = dot_left(low_normed, own_part(project_grad, 1))
    values_grad, gain_grad = norm_backward(
        dot_right(project_grad, weight_in), unit, inverse, gains[2]
    )
    return (
        grad + values_grad,
        gain_grad,
        gamma_grad,
        beta_grad,
        in_grad,
        jnp.stack(depth_rows),
        out_grad,
    )


def senone_step(values, gain, tables, targets, valid):
    splits, place = lax.axis_size("hid"), lax.axis_index("hid")
    normed, unit, inverse = norm_forward(values, gain)
    low_normed = to_low(normed)
    own_rows, own_unit, own_inverse = (own_part(part, 0) for part in (low_normed, unit, inverse))
    own_targets, own_valid = own_part(targets, 0), own_part(valid, 0)
    logits = [dot_low(own_rows, table) for table in tables]
    width = logits[0].shape[1]
    picked = [
        own_targets[:, None]
        == jnp.arange(width, dtype=jnp.int32)[None, :] + (place - step) % splits * width
        for step in range(splits)
    ]
    top = jnp.max(jnp.stack([jnp.max(part, 1) for part in logits]), 0)
    total = sum(jnp.sum(jnp.exp(part - top[:, None]), 1) for part in logits)
    target = sum(
        jnp.sum(jnp.where(chosen, part, 0.0), 1) for chosen, part in zip(picked, logits)
    )
    log_total = top + jnp.log(total)
    loss = jnp.sum(own_valid * log_total) - jnp.sum(own_valid * target)
    logit_grad = [
        to_low(
            own_valid[:, None]
            * (jnp.exp(part - log_total[:, None]) - chosen.astype(jnp.float32))
        )
        for chosen, part in zip(picked, logits)
    ]
    normed_grad = sum(dot_right(part, table) for part, table in zip(logit_grad, tables))
    own_grad, own_gain_grad = norm_backward(normed_grad, own_unit, own_inverse, gain)
    values_grad = in_order(gather_near(to_low(own_grad)), 0).astype(jnp.float32)
    gain_grad = sum(gather_near(own_gain_grad))
    moved = [logit_grad[0]] + [shift(logit_grad[splits - step], step) for step in range(1, splits)]
    table_grad = dot_left(low_normed, in_order(moved, 0))
    return (loss, values_grad, gain_grad, table_grad)


def on_device(
    features,
    lengths,
    routes,
    alignments,
    input_weight,
    attention_in,
    branch_out,
    pointwise_in,
    depthwise,
    router,
    senone_table,
    norm_scales,
    expert_weights,
    input_first,
    input_second,
    attention_first,
    attention_second,
    branch_first,
    branch_second,
    pointwise_first,
    pointwise_second,
    depthwise_first,
    depthwise_second,
    router_first,
    router_second,
    senone_first,
    senone_second,
    scales_first,
    scales_second,
    expert_momentum,
):
    owners, splits = lax.axis_size("dp"), lax.axis_size("hid")
    place = lax.axis_index("hid")
    tokens = features.shape[0]
    bands, taps, gains = input_weight.shape[0], depthwise.shape[0], norm_scales.shape[0]
    own_width = input_weight.shape[1]

    small = jnp.concatenate(
        [
            jnp.pad(input_weight.T, ((0, 0), (0, 128 - bands))),
            router[0],
            router[1],
            depthwise.T,
            norm_scales.T,
            jnp.zeros((own_width, 128 - 2 * owners - taps - gains), jnp.float32),
        ],
        1,
    )
    small = exchange_rows(jnp.broadcast_to(small[None], (owners,) + small.shape))
    small = small.reshape(owners * own_width, -1)
    input_full = to_low(small[:, :bands])
    router_full = [small[:, 128 : 128 + owners], small[:, 128 + owners : 128 + 2 * owners]]
    begin = 128 + 2 * owners
    depth_full = small[:, begin : begin + taps].T
    scales_full = small[:, begin + taps : begin + taps + gains].T

    dense = to_low(jnp.concatenate([attention_in, branch_out[0], branch_out[1], pointwise_in], 1))
    dense = lax.all_gather(dense, "dp", axis=0, tiled=True)
    senone_own = lax.all_gather(to_low(senone_table), "dp", axis=0, tiled=True)
    attention_full, dense = dense[:, : 3 * D], dense[:, 3 * D :]
    branch_full, pointwise_full = (dense[:, :D], dense[:, D : 2 * D]), dense[:, 2 * D :]
    senone_full = gather_far(senone_own)
    expert_low = to_low(expert_weights[:, :, 0])
    expert_full = [[gather_far(expert_low[k, part]) for part in range(2)] for k in range(2)]
    momentum_pieces = expert_momentum.reshape((2 * 2,) + expert_momentum.shape[3:])

    def to_owners(pieces):
        return jnp.stack(
            [
                pieces[place] if step == 0 else shift(pieces[(place + step) % splits], step)
                for step in range(splits)
            ]
        )

    owned_momentum = to_owners(momentum_pieces)

    valid = (jnp.arange(tokens, dtype=jnp.int32) < lengths[0]).astype(jnp.float32)
    start = dot_right(features, input_full)
    mixed_one, kept_one = mixture_forward(
        start, scales_full[0], router_full[0], *expert_full[0], routes[0, :, 0]
    )
    first = start + mixed_one
    attended, kept_attend = attention_forward(
        first, scales_full[1], attention_full, branch_full[0], valid
    )
    second = first + attended
    convolved, kept_convolve = convolution_forward(
        second, scales_full, pointwise_full, depth_full, branch_full[1], valid
    )
    third = second + convolved
    mixed_two, kept_two = mixture_forward(
        third, scales_full[3], router_full[1], *expert_full[1], routes[1, :, 0]
    )
    fourth = third + mixed_two
    loss_local, grad, gain_five, senone_grad = senone_step(
        fourth, scales_full[4], senone_full, alignments, valid
    )
    senone_share = summed_shares(senone_grad)
    grad, gain_four, router_two, in_two, out_two = mixture_backward(
        grad, scales_full[3], router_full[1], *expert_full[1], kept_two
    )
    grad, gain_three, gamma_grad, beta_grad, pointwise_grad, depth_grad, conv_out_grad = (
        convolution_backward(
            grad, scales_full, pointwise_full, depth_full, branch_full[1], valid, kept_convolve
        )
    )
    grad, gain_two, attention_grad, attend_out_grad = attention_backward(
        grad, scales_full[1], attention_full, branch_full[0], valid, kept_attend
    )
    dense_share = summed_shares(
        jnp.concatenate([attention_grad, attend_out_grad, conv_out_grad, pointwise_grad], 1)
    )
    grad, gain_one, router_one, in_one, out_one = mixture_backward(
        grad, scales_full[0], router_full[0], *expert_full[0], kept_one
    )
    scales_grad = jnp.stack(
        [gain_one, gain_two, gain_three, gain_four, gain_five, gamma_grad, beta_grad]
    )
    expert_grad = jnp.stack([in_one, out_one, in_two, out_two])
    input_grad = dot_left(to_low(grad), features)
    small_share = summed_shares(
        jnp.concatenate(
            [
                jnp.pad(input_grad, ((0, 0), (0, 128 - bands))),
                router_one,
                router_two,
                depth_grad.T,
                scales_grad.T,
                jnp.zeros((D, 128 - 2 * owners - taps - gains), jnp.float32),
            ],
            1,
        )
    )
    leading = (place == 0).astype(jnp.float32)
    square = (
        leading * jnp.sum(small_share * small_share)
        + jnp.sum(dense_share * dense_share)
        + jnp.sum(senone_share * senone_share)
        + jnp.sum(expert_grad * expert_grad)
    )
    scalars = jnp.stack([square, leading * lengths[0].astype(jnp.float32), loss_local])
    scalars = jnp.broadcast_to(
        jnp.pad(scalars, (0, 125))[None, None], (owners * splits, 1, 128)
    )
    scalars = jnp.sum(
        lax.all_to_all(scalars, ("dp", "hid"), split_axis=0, concat_axis=0, tiled=True), (0, 1)
    )
    square, count, loss_sum = scalars[0], scalars[1], scalars[2]
    norm = jnp.sqrt(square) / count
    factor = jnp.minimum(1.0, clip_limit / (norm + 1e-06))

    owned_grad = to_owners(to_low(expert_grad))
    kind_scale = jnp.where(place % 2 == 0, D ** (-0.5), 3 * owners * FF ** (-0.5)) * (
        muon_rate * FF**0.5
    )
    expert_scale = factor / count
    orth = orthogonal(
        jnp.stack([expert_scale, kind_scale]), owned_momentum, owned_grad
    )
    momentum_new = muon_beta * expert_momentum + expert_scale * expert_grad.reshape(
        expert_momentum.shape
    )
    returned = [orth[0]] + [shift(orth[step], -step) for step in range(1, splits)]
    turned = [returned[0]] + returned[:0:-1]
    update = in_order(turned, 0).reshape(expert_weights.shape).astype(jnp.float32)
    experts_new = (1.0 - muon_decay) * expert_weights - update

    dense_share = gather_near(dense_share)
    quarter = D // splits
    parts = [
        in_order([block[:, begin : begin + width] for block in dense_share], 1)
        for begin, width in (
            (0, 3 * quarter),
            (3 * quarter, quarter),
            (4 * quarter, quarter),
            (5 * quarter, 2 * quarter),
        )
    ]
    begin = 128 + 2 * owners
    shares = (
        small_share[:, :bands].T,
        parts[0],
        jnp.stack(parts[1:3]),
        parts[3],
        senone_share,
        small_share[:, begin : begin + taps].T,
        jnp.stack([small_share[:, 128 : 128 + owners], small_share[:, 128 + owners : begin]]),
        small_share[:, begin + taps : begin + taps + gains].T,
    )
    input_first_new, input_second_new, input_new = adam_update(
        input_weight, shares[0] / count * factor, input_first, input_second, adam_rate, weight_decay
    )
    attention_first_new, attention_second_new, attention_new = adam_update(
        attention_in,
        shares[1] / count * factor,
        attention_first,
        attention_second,
        adam_rate,
        weight_decay,
    )
    branch_first_new, branch_second_new, branch_new = adam_update(
        branch_out, shares[2] / count * factor, branch_first, branch_second, adam_rate, weight_decay
    )
    pointwise_first_new, pointwise_second_new, pointwise_new = adam_update(
        pointwise_in,
        shares[3] / count * factor,
        pointwise_first,
        pointwise_second,
        adam_rate,
        weight_decay,
    )
    senone_first_new, senone_second_new, senone_new = adam_update(
        senone_table,
        shares[4] / count * factor,
        senone_first,
        senone_second,
        adam_rate,
        weight_decay,
    )
    depthwise_first_new, depthwise_second_new, depthwise_new = adam_update(
        depthwise,
        shares[5] / count * factor,
        depthwise_first,
        depthwise_second,
        adam_rate,
        weight_decay,
    )
    router_first_new, router_second_new, router_new = adam_update(
        router, shares[6] / count * factor, router_first, router_second, adam_rate, weight_decay
    )
    scales_first_new, scales_second_new, scales_new = adam_update(
        norm_scales, shares[7] / count * factor, scales_first, scales_second, gain_rate, 0.0
    )
    return (
        loss_sum,
        count,
        norm,
        input_first_new,
        input_second_new,
        input_new,
        attention_first_new,
        attention_second_new,
        attention_new,
        branch_first_new,
        branch_second_new,
        branch_new,
        pointwise_first_new,
        pointwise_second_new,
        pointwise_new,
        depthwise_first_new,
        depthwise_second_new,
        depthwise_new,
        router_first_new,
        router_second_new,
        router_new,
        senone_first_new,
        senone_second_new,
        senone_new,
        scales_first_new,
        scales_second_new,
        scales_new,
        momentum_new,
        experts_new,
    )


def solution(mesh):
    return jax.shard_map(
        on_device,
        mesh=mesh,
        in_specs=(
            P("dp", None),
            P("dp"),
            P(None, "dp", None),
            P("dp"),
            P(None, "dp"),
            P("dp", None),
            P(None, "dp", None),
            P("dp", None),
            P(None, "dp"),
            P(None, "dp", None),
            P("dp", "hid"),
            P(None, "dp"),
            P(None, None, "dp", None, "hid"),
            P(None, "dp"),
            P(None, "dp"),
            P("dp", None),
            P("dp", None),
            P(None, "dp", None),
            P(None, "dp", None),
            P("dp", None),
            P("dp", None),
            P(None, "dp"),
            P(None, "dp"),
            P(None, "dp", None),
            P(None, "dp", None),
            P("dp", "hid"),
            P("dp", "hid"),
            P(None, "dp"),
            P(None, "dp"),
            P(None, None, "dp", None, "hid"),
        ),
        out_specs=(
            P(),
            P(),
            P(),
            P(None, "dp"),
            P(None, "dp"),
            P(None, "dp"),
            P("dp", None),
            P("dp", None),
            P("dp", None),
            P(None, "dp", None),
            P(None, "dp", None),
            P(None, "dp", None),
            P("dp", None),
            P("dp", None),
            P("dp", None),
            P(None, "dp"),
            P(None, "dp"),
            P(None, "dp"),
            P(None, "dp", None),
            P(None, "dp", None),
            P(None, "dp", None),
            P("dp", "hid"),
            P("dp", "hid"),
            P("dp", "hid"),
            P(None, "dp"),
            P(None, "dp"),
            P(None, "dp"),
            P(None, None, "dp", None, "hid"),
            P(None, None, "dp", None, "hid"),
        ),
        check_vma=False,
    )
```

```python
import functools

import jax
import jax.numpy as jnp
from jax import lax
from jax.experimental import pallas as pl
from jax.experimental.pallas import tpu as pltpu
from jax.sharding import PartitionSpec as P

D = 512
HEADS = 8
HEAD_DIM = 64
FF = 2048
STEP = 10
LANES = 128


clip_limit = 0.02
beta_one = 0.9
beta_two = 0.999
adam_epsilon = 1e-08
adam_rate = 0.2
gain_rate = 0.6
weight_decay = 0.01
muon_beta = 0.95
muon_rate = 1.0
muon_decay = 0.01
newton_first = 3.4445
newton_second = -4.775
newton_third = 2.0315


def shift(values, step):
    size = lax.axis_size("hid")
    return lax.ppermute(values, "hid", [(i, (i + step) % size) for i in range(size)])


def gather_near(values):
    return [values] + [shift(values, step) for step in range(1, lax.axis_size("hid"))]


def after(values, *earlier):
    return lax.optimization_barrier((values,) + earlier)[0]


def spread(pieces, *earlier):
    pieces = after(tuple(pieces), *earlier)
    return [pieces[0]] + [shift(pieces[step], step) for step in range(1, len(pieces))]


def own_part(values, axis):
    width = values.shape[axis] // lax.axis_size("hid")
    return lax.dynamic_slice_in_dim(values, lax.axis_index("hid") * width, width, axis)


def exchange_rows(values):
    owners = lax.axis_size("dp")
    shape = values.shape
    shaped_rows = values.reshape((owners, shape[0] // owners) + shape[1:])
    moved = lax.all_to_all(shaped_rows, "dp", split_axis=0, concat_axis=0, tiled=True)
    return moved.reshape(shape)


def to_low(values):
    return values.astype(jnp.bfloat16)


def dot_low(left, right):
    return jnp.dot(left, right, preferred_element_type=jnp.float32)


def dot_left(left, right):
    return lax.dot_general(
        left, right, (((0,), (0,)), ((), ())), preferred_element_type=jnp.float32
    )


def dot_right(left, right):
    return lax.dot_general(
        left, right, (((1,), (1,)), ((), ())), preferred_element_type=jnp.float32
    )


def exact_dot(left, right, dims=((1,), (0,))):
    return lax.dot_general(
        left,
        right,
        (dims, ((), ())),
        precision=lax.Precision.HIGHEST,
        preferred_element_type=jnp.float32,
    )


def two_parts(values):
    high = to_low(values)
    return high, to_low(values - high.astype(jnp.float32))


def close_dot(left, right):
    return dot_low(left[0], right[0]) + (dot_low(left[0], right[1]) + dot_low(left[1], right[0]))


def norm_forward(values, gain):
    centered = values - jnp.mean(values, -1, keepdims=True)
    inverse = lax.rsqrt(jnp.mean(centered * centered, -1, keepdims=True) + 1e-05)
    unit = centered * inverse
    return (unit * gain, unit, inverse)


def norm_backward(grad, unit, inverse, gain):
    scaled = grad * gain
    back = inverse * (
        scaled
        - jnp.mean(scaled, -1, keepdims=True)
        - unit * jnp.mean(scaled * unit, -1, keepdims=True)
    )
    return (back, jnp.sum(grad * unit, 0, keepdims=True))


def silu_slope(values):
    sigma = jax.nn.sigmoid(values)
    return sigma * (1.0 + values * (1.0 - sigma))


def shaped(shape, dtype):
    return jax.ShapeDtypeStruct(shape, dtype)


def place_of(shape, axis):
    return lax.broadcasted_iota(jnp.int32, shape, axis)


def whole_call(kernel, out_shapes, scalars, arrays, flops, scratch=()):
    parts = [part if isinstance(part, tuple) else (part, None, None) for part in arrays]
    specs = [
        pl.BlockSpec(memory_space=pltpu.VMEM)
        if block is None
        else pl.BlockSpec(block, functools.partial(lambda fixed, step: fixed, at))
        for _, block, at in parts
    ]
    moved = sum(part.size * part.dtype.itemsize for part, _, _ in parts) + sum(
        part.size * part.dtype.itemsize for part in out_shapes
    )
    return pl.pallas_call(
        kernel,
        grid=(1,),
        out_shape=out_shapes,
        in_specs=[pl.BlockSpec(memory_space=pltpu.SMEM)] * len(scalars) + specs,
        out_specs=[pl.BlockSpec(memory_space=pltpu.VMEM)] * len(out_shapes),
        scratch_shapes=list(scratch),
        compiler_params=pltpu.CompilerParams(vmem_limit_bytes=48 * 1024 * 1024),
        cost_estimate=pl.CostEstimate(flops=flops, bytes_accessed=moved, transcendentals=0),
    )(*scalars, *[part for part, _, _ in parts])


def pack_small_kernel(owners, input_ref, router_ref, depth_ref, gains_ref, out_ref, turn_ref):
    bands, taps, gains = input_ref.shape[1], depth_ref.shape[0], gains_ref.shape[0]
    width = input_ref.shape[0]
    turn_ref[...] = jnp.zeros(turn_ref.shape, jnp.float32)
    turn_ref[2 * owners : 2 * owners + taps, :width] = depth_ref[...]
    turn_ref[2 * owners + taps : 2 * owners + taps + gains, :width] = gains_ref[...]
    turned = turn_ref[...].T[:width]
    out_ref[...] = jnp.zeros(out_ref.shape, jnp.float32)
    for owner in range(owners):
        out_ref[owner, :, LANES:] = turned
        out_ref[owner, :, :bands] = input_ref[...]
        out_ref[owner, :, LANES : LANES + owners] = router_ref[0]
        out_ref[owner, :, LANES + owners : LANES + 2 * owners] = router_ref[1]


def pack_small(input_turned, router, depthwise, norm_scales):
    owners, width = lax.axis_size("dp"), input_turned.shape[0]
    return whole_call(
        functools.partial(pack_small_kernel, owners),
        [shaped((owners, width, 2 * LANES), jnp.float32)],
        [],
        [input_turned, router, depthwise, norm_scales],
        1000,
        [pltpu.VMEM((LANES, LANES), jnp.float32)],
    )[0]


def pack_dense_kernel(attention_ref, branch_ref, pointwise_ref, *refs):
    out_ref = refs[-1]
    for part in range(3):
        out_ref[part] = to_low(attention_ref[:, part * D : (part + 1) * D])
    for part in range(2):
        out_ref[3 + part] = to_low(branch_ref[part])
        out_ref[5 + part] = to_low(pointwise_ref[:, part * D : (part + 1) * D])
    place = 7
    for ref in refs[:-1]:
        for part in range(ref.shape[1] // D):
            out_ref[place] = ref[:, part * D : (part + 1) * D]
            place += 1


def pack_dense(attention_in, branch_out, pointwise_in, senone_rows):
    rows = attention_in.shape[0]
    count = 7 + sum(part.shape[1] // D for part in senone_rows)
    return whole_call(
        pack_dense_kernel,
        [shaped((count, rows, D), jnp.bfloat16)],
        [],
        [attention_in, branch_out, pointwise_in, *senone_rows],
        1000,
    )[0]


def plan_kernel(experts, splits, share, wide, place_ref, routes_ref, out_ref):
    tokens = routes_ref.shape[1]
    before = (place_of((tokens, tokens), 0) < place_of((tokens, tokens), 1)).astype(jnp.float32)
    for mixture in range(2):
        route = routes_ref[mixture : mixture + 1]
        onehot = (place_of((experts, tokens), 0) == route).astype(jnp.float32)
        earlier = dot_low(to_low(onehot), to_low(before))
        slot = jnp.sum(earlier * onehot, 0, keepdims=True).astype(jnp.int32)
        quarter = sum((slot >= (part + 1) * share).astype(jnp.int32) for part in range(splits - 1))
        within = slot - quarter * share
        turned = (place_ref[0] - quarter + splits) % splits
        out_ref[2 * mixture : 2 * mixture + 1] = jnp.where(
            turned == 0, route * wide + within, -1
        )
        out_ref[2 * mixture + 1 : 2 * mixture + 2] = (turned * experts + route) * share + within


def plan_slots(place, routes, share, wide):
    return whole_call(
        functools.partial(
            plan_kernel, lax.axis_size("dp"), lax.axis_size("hid"), share, wide
        ),
        [shaped((4, routes.shape[1]), jnp.int32)],
        [place],
        [routes],
        1_000_000,
    )[0]


def narrowing(share_rows, wide_rows, share, wide):
    at = place_of((share_rows, wide_rows), 1)
    within = at % wide
    return to_low(
        ((place_of((share_rows, wide_rows), 0) == at // wide * share + within) & (within < share))
        .astype(jnp.float32)
    )


def routing(mixture, experts, normed, router, route):
    column = place_of((normed.shape[0], LANES), 1) - mixture * experts
    inside = (column >= 0) & (column < experts)
    logits = jnp.where(inside, exact_dot(normed, router), -1e30)
    raised = jnp.where(inside, jnp.exp(logits - jnp.max(logits, 1, keepdims=True)), 0.0)
    return raised / jnp.sum(raised, 1, keepdims=True), (column == route).astype(jnp.float32)


def dispatch(mixture, experts, values, gain, router, route, index, slots_ref, gate_ref, chances_ref):
    normed, _, _ = norm_forward(values, gain)
    chosen = (place_of((slots_ref.shape[0], values.shape[0]), 0) == index).astype(jnp.float32)
    slots_ref[...] = to_low(dot_low(to_low(chosen), to_low(normed)))
    chances, onehot = routing(mixture, experts, normed, router, route)
    gate_ref[...] = jnp.sum(chances * onehot, 1, keepdims=True)
    chances_ref[...] = chances


def dispatch_shapes(tokens, wide_rows):
    return [
        shaped((wide_rows, D), jnp.bfloat16),
        shaped((tokens, 1), jnp.float32),
        shaped((tokens, LANES), jnp.float32),
    ]


def start_kernel(
    experts, gain_row, small_ref, features_ref, plan_ref, route_ref, start_ref, turned_ref, *out
):
    bands = features_ref.shape[0]
    start = lax.dot_general(
        features_ref[...],
        to_low(small_ref[:, :bands]),
        (((0,), (1,)), ((), ())),
        preferred_element_type=jnp.float32,
    )
    start_ref[...] = start
    router = small_ref[:, LANES:]
    turned_ref[...] = router.T
    gain = turned_ref[gain_row : gain_row + 1]
    dispatch(0, experts, start, gain, router, route_ref[0], plan_ref[:1], *out)


def start_step(small, features_turned, plan, routes, gain_row, wide_rows):
    tokens = features_turned.shape[1]
    return whole_call(
        functools.partial(start_kernel, lax.axis_size("dp"), gain_row),
        [shaped((tokens, D), jnp.float32), shaped((LANES, D), jnp.float32)]
        + dispatch_shapes(tokens, wide_rows),
        [],
        [small, features_turned, plan, routes],
        700_000_000,
    )


def dispatch_kernel(
    mixture, experts, gain_row, values_ref, small_ref, turned_ref, plan_ref, route_ref, *out
):
    dispatch(
        mixture,
        experts,
        values_ref[...],
        turned_ref[gain_row : gain_row + 1],
        small_ref[:, LANES:],
        route_ref[mixture],
        plan_ref[2 * mixture : 2 * mixture + 1],
        *out,
    )


def dispatch_step(mixture, values, small, turned, plan, routes, gain_row, wide_rows):
    return whole_call(
        functools.partial(dispatch_kernel, mixture, lax.axis_size("dp"), gain_row),
        dispatch_shapes(values.shape[0], wide_rows),
        [],
        [values, small, turned, plan, routes],
        700_000_000,
    )


def expert_pieces(refs, place, step, splits):
    if len(refs) == 1:
        return tuple(refs[0][(place + splits - step) % splits, part] for part in range(2))
    own, before, behind, across_in, across_out = refs
    if step == 2:
        return across_in[...], across_out[...]
    chosen = (own, before, None, behind)[step]
    return chosen[0], chosen[1]


def expert_forward_kernel(splits, share, wide, place_ref, rows_ref, *refs):
    weights, sent_refs, returned_ref = refs[: -splits - 1], refs[-splits - 1 : -1], refs[-1]
    place, count = place_ref[0], sent_refs[0].shape[0] // 2
    narrow = narrowing(count, rows_ref.shape[0], share, wide)
    rows = to_low(dot_low(narrow, rows_ref[...]))
    total = jnp.zeros(rows.shape, jnp.float32)
    for step in range(splits):
        weight_in, weight_out = expert_pieces(weights, place, step, splits)
        active = dot_low(rows, weight_in)
        hidden = to_low(active * jax.nn.sigmoid(active))
        sent_ref = sent_refs[(splits - step) % splits]
        sent_ref[:count] = rows
        sent_ref[count:] = hidden
        total = total + dot_right(hidden, weight_out)
    returned_ref[...] = to_low(dot_left(narrow, to_low(total)))


def expert_backward_kernel(splits, share, wide, place_ref, kept_ref, grad_ref, *refs):
    weights, sent_refs, returned_ref = refs[: -splits - 1], refs[-splits - 1 : -1], refs[-1]
    place, count = place_ref[0], kept_ref.shape[0] // 2
    narrow = narrowing(count, grad_ref.shape[0], share, wide)
    rows, rows_grad = kept_ref[:count], to_low(dot_low(narrow, grad_ref[...]))
    total = jnp.zeros(rows.shape, jnp.float32)
    for step in range(splits):
        weight_in, weight_out = expert_pieces(weights, place, step, splits)
        active = dot_low(rows, weight_in)
        active_grad = to_low(dot_low(rows_grad, weight_out) * silu_slope(active))
        sent_ref = sent_refs[(splits - step) % splits]
        sent_ref[:count] = rows_grad
        sent_ref[count:] = active_grad
        total = total + dot_right(active_grad, weight_in)
    returned_ref[...] = to_low(dot_left(narrow, to_low(total)))


def expert_call(kernel, place, arrays, weights, slots, rows, flops):
    splits, experts = lax.axis_size("hid"), lax.axis_size("dp")
    share, wide = slots
    *sent, returned = whole_call(
        functools.partial(kernel, splits, share, wide),
        [shaped((2 * experts * share, D), jnp.bfloat16)] * splits
        + [shaped(rows.shape, jnp.bfloat16)],
        [place],
        [*arrays, *weights],
        flops,
    )
    return sent, returned


def expert_forward(place, rows, weights, slots):
    return expert_call(
        expert_forward_kernel, place, [rows], weights, slots, rows, 4 * rows.shape[0] * D * FF
    )


def expert_backward(place, kept, rows_grad, weights, slots):
    return expert_call(
        expert_backward_kernel,
        place,
        [kept, rows_grad],
        weights,
        slots,
        rows_grad,
        6 * rows_grad.shape[0] * D * FF,
    )


def narrow_kernel(share, wide, rows_ref, out_ref):
    narrow = narrowing(out_ref.shape[0], rows_ref.shape[0], share, wide)
    out_ref[...] = to_low(dot_low(narrow, rows_ref[...]))


def gather_slots(rows, slots):
    share, wide = slots
    narrow = whole_call(
        functools.partial(narrow_kernel, share, wide),
        [shaped((rows.shape[0] // wide * share, D), jnp.bfloat16)],
        [],
        [rows],
        50_000_000,
    )[0]
    return gather_near(narrow)


def combined(position, blocks):
    share, tokens = blocks[0].shape[0], position.shape[1]
    row = place_of((share, tokens), 0)
    return sum(
        dot_left(to_low((position - step * share == row).astype(jnp.float32)), block[...])
        for step, block in enumerate(blocks)
    )


def combine_kernel(mixture, plan_ref, gate_ref, base_ref, *refs):
    blocks, expert_out_ref, out_ref = refs[:-2], refs[-2], refs[-1]
    total = combined(plan_ref[2 * mixture + 1 : 2 * mixture + 2], blocks)
    expert_out_ref[...] = total
    out_ref[...] = base_ref[...] + 0.5 * gate_ref[...] * total


def combine_step(mixture, plan, gate, base, blocks):
    return whole_call(
        functools.partial(combine_kernel, mixture),
        [shaped(base.shape, jnp.float32)] * 2,
        [],
        [plan, gate, base, *blocks],
        500_000_000,
    )


def both_grads(forward, backward):
    share = forward[0].shape[0] // 2
    return (
        sum(dot_left(ahead[:share], behind[share:]) for ahead, behind in zip(forward, backward)),
        sum(dot_left(behind[:share], ahead[share:]) for ahead, behind in zip(forward, backward)),
    )


def expert_grad_kernel(splits, *refs):
    out_ref = refs[-1]
    out_ref[0], out_ref[1] = both_grads(refs[:splits], refs[splits : 2 * splits])


def last_grad_kernel(splits, place_ref, *refs):
    later_ref, out_ref = refs[2 * splits], refs[2 * splits + 1]
    square_ref, sent_refs, all_ref = refs[2 * splits + 2], refs[2 * splits + 3 : -1], refs[-1]
    all_ref[0], all_ref[1] = both_grads(refs[:splits], refs[splits : 2 * splits])
    out_ref[...] = all_ref[:2]
    all_ref[2:] = later_ref[...]
    square = jnp.zeros((1, D), jnp.float32)
    for part in range(4):
        square = square + jnp.sum(all_ref[part] * all_ref[part], 0, keepdims=True)
    square_ref[...] = square
    for step, sent_ref in enumerate(sent_refs):
        sent_ref[...] = to_low(all_ref[(place_ref[0] + step) % 4])


def expert_grads(forward, backward):
    rows, width = forward[0].shape
    return whole_call(
        functools.partial(expert_grad_kernel, len(forward)),
        [shaped((2, width, width), jnp.float32)],
        [],
        [*forward, *backward],
        4 * rows * width * width * len(forward) // 2,
    )[0]


def last_expert_grads(place, forward, backward, later):
    rows, width = forward[0].shape
    splits = len(forward)
    out, square, *sent = whole_call(
        functools.partial(last_grad_kernel, splits),
        [shaped(later.shape, jnp.float32), shaped((1, width), jnp.float32)]
        + [shaped((width, width), jnp.bfloat16)] * splits,
        [place],
        [*forward, *backward, later],
        4 * rows * width * width * splits // 2,
        [pltpu.VMEM((4, width, width), jnp.float32)],
    )
    return out, square, sent


def attention_forward_kernel(
    gain_row, length_ref, values_ref, turned_ref, weight_ref, branch_ref, out_ref, parts_ref, log_ref, context_ref
):
    values = values_ref[...]
    tokens = values.shape[0]
    normed, _, _ = norm_forward(values, turned_ref[gain_row : gain_row + 1])
    low_normed = to_low(normed)
    for part in range(3):
        parts_ref[part] = to_low(dot_low(low_normed, weight_ref[part]))
    seen = place_of((tokens, tokens), 1) < length_ref[0]
    lane = place_of((tokens, LANES), 1)
    logs = jnp.zeros((tokens, LANES), jnp.float32)
    pair = LANES // HEAD_DIM
    for first in range(0, HEADS, pair):
        columns = slice(first * HEAD_DIM, (first + pair) * HEAD_DIM)
        queries, keys, contents = (parts_ref[part, :, columns] for part in range(3))
        context = jnp.zeros((tokens, LANES), jnp.float32)
        for head in range(pair):
            mine = lane // HEAD_DIM == head
            scores = dot_right(jnp.where(mine, queries, jnp.zeros_like(queries)), keys)
            scores = jnp.where(seen, scores * HEAD_DIM ** (-0.5), -1e30)
            top = jnp.max(scores, 1, keepdims=True)
            raised = jnp.exp(scores - top)
            total = jnp.sum(raised, 1, keepdims=True)
            mixed = dot_low(to_low(raised * (1.0 / total)), contents)
            context = jnp.where(mine, mixed, context)
            logs = jnp.where(lane == first + head, top + jnp.log(total), logs)
        context_ref[:, columns] = to_low(context)
    log_ref[...] = logs
    out_ref[...] = values + dot_low(context_ref[...], branch_ref[0])


def attention_forward(length, values, turned, dense, gain_row):
    tokens = values.shape[0]
    return whole_call(
        functools.partial(attention_forward_kernel, gain_row),
        [
            shaped((tokens, D), jnp.float32),
            shaped((3, tokens, D), jnp.bfloat16),
            shaped((tokens, LANES), jnp.float32),
            shaped((tokens, D), jnp.bfloat16),
        ],
        [length],
        [values, turned, (dense, (3, D, D), (0, 0, 0)), (dense, (1, D, D), (3, 0, 0))],
        4_000_000_000,
    )


def attention_backward_kernel(
    gain_row,
    length_ref,
    place_ref,
    grad_ref,
    values_ref,
    turned_ref,
    weight_ref,
    branch_ref,
    parts_ref,
    log_ref,
    context_ref,
    out_ref,
    gain_grad_ref,
    weight_grad_ref,
    low_ref,
    project_ref,
):
    grad = grad_ref[...]
    tokens = grad.shape[0]
    low_grad = to_low(grad)
    low_ref[...] = low_grad
    context_grad = to_low(dot_right(low_grad, branch_ref[0]))
    seen = place_of((tokens, tokens), 1) < length_ref[0]
    lane = place_of((tokens, LANES), 1)
    pair = LANES // HEAD_DIM
    scale = HEAD_DIM ** (-0.5)
    for first in range(0, HEADS, pair):
        columns = slice(first * HEAD_DIM, (first + pair) * HEAD_DIM)
        queries, keys, contents = (parts_ref[part, :, columns] for part in range(3))
        mixed_grad = context_grad[:, columns]
        grads = [jnp.zeros((tokens, LANES), jnp.float32)] * 3
        for head in range(pair):
            mine = lane // HEAD_DIM == head
            none = jnp.zeros_like(queries)
            scores = dot_right(jnp.where(mine, queries, none), keys) * scale
            log_total = jnp.sum(
                jnp.where(lane == first + head, log_ref[...], 0.0), 1, keepdims=True
            )
            weights = jnp.where(seen, jnp.exp(jnp.where(seen, scores, -1e30) - log_total), 0.0)
            weight_grad = dot_right(jnp.where(mine, mixed_grad, none), contents)
            score_grad = to_low(
                weights * (weight_grad - jnp.sum(weight_grad * weights, 1, keepdims=True))
            )
            found = (
                dot_low(score_grad, keys) * scale,
                dot_left(score_grad, queries) * scale,
                dot_left(to_low(weights), mixed_grad),
            )
            grads = [jnp.where(mine, new, old) for new, old in zip(found, grads)]
        for part in range(3):
            project_ref[part, :, columns] = to_low(grads[part])
    gain = turned_ref[gain_row : gain_row + 1]
    normed, unit, inverse = norm_forward(values_ref[...], gain)
    low_normed = to_low(normed)
    normed_grad = sum(dot_right(project_ref[part], weight_ref[part]) for part in range(3))
    back, gain_grad_ref[...] = norm_backward(normed_grad, unit, inverse, gain)
    out_ref[...] = grad + back
    width = weight_grad_ref.shape[1] // 4
    own = pl.ds(pl.multiple_of(place_ref[0] * width, width), width)
    for part in range(3):
        weight_grad_ref[:, part * width : (part + 1) * width] = to_low(
            dot_left(low_normed, project_ref[part, :, own])
        )
    weight_grad_ref[:, 3 * width :] = to_low(dot_left(context_ref[...], low_ref[:, own]))


def attention_backward(length, place, grad, values, turned, dense, kept, gain_row):
    tokens = values.shape[0]
    splits = lax.axis_size("hid")
    return whole_call(
        functools.partial(attention_backward_kernel, gain_row),
        [
            shaped((tokens, D), jnp.float32),
            shaped((1, D), jnp.float32),
            shaped((D, 4 * D // splits), jnp.bfloat16),
        ],
        [length, place],
        [
            grad,
            values,
            turned,
            (dense, (3, D, D), (0, 0, 0)),
            (dense, (1, D, D), (3, 0, 0)),
            *kept,
        ],
        9_000_000_000,
        [pltpu.VMEM((tokens, D), jnp.bfloat16), pltpu.VMEM((3, tokens, D), jnp.bfloat16)],
    )


def senone_kernel(
    gain_row, splits, length_ref, place_ref, values_ref, turned_ref, targets_ref, *refs
):
    low_ref, loss_ref, sent_ref = refs[-3 - splits], refs[-2 - splits], refs[-1 - splits]
    logit_refs = refs[-splits:]
    tables = refs[: -3 - splits]
    rows = values_ref.shape[0] // splits
    place = place_ref[0]
    gain = turned_ref[gain_row : gain_row + 1]
    normed, _, _ = norm_forward(values_ref[...], gain)
    low_ref[...] = to_low(normed)
    own = pl.ds(pl.multiple_of(place * rows, rows), rows)
    normed, unit, inverse = norm_forward(values_ref[own], gain)
    own_rows, targets = to_low(normed), targets_ref[own]
    halves = len(tables) // splits
    width = tables[0].shape[2]
    logits, picked = [], []
    for number, table in enumerate(tables):
        begin = ((place + splits - number // halves) % splits * halves + number % halves) * width
        logits.append(dot_low(own_rows, table[0]))
        picked.append(place_of((rows, width), 1) + begin == targets)
    top = functools.reduce(
        jnp.maximum, [jnp.max(part, 1, keepdims=True) for part in logits]
    )
    total = sum(jnp.sum(jnp.exp(part - top), 1, keepdims=True) for part in logits)
    target = sum(
        jnp.sum(jnp.where(chosen, part, 0.0), 1, keepdims=True)
        for chosen, part in zip(picked, logits)
    )
    log_total = top + jnp.log(total)
    valid = (place_of((rows, 1), 0) + place * rows < length_ref[0]).astype(jnp.float32)
    loss_ref[...] = jnp.sum(valid * (log_total - target), 0, keepdims=True)
    normed_grad = jnp.zeros((rows, D), jnp.float32)
    for number, (chosen, part, table) in enumerate(zip(picked, logits, tables)):
        logit_grad = to_low(
            valid * (jnp.exp(part - log_total) - chosen.astype(jnp.float32))
        )
        half = number % halves
        logit_refs[(splits - number // halves) % splits][
            :, half * width : (half + 1) * width
        ] = logit_grad
        normed_grad = normed_grad + dot_right(logit_grad, table[0])
    own_grad, gain_grad = norm_backward(normed_grad, unit, inverse, gain)
    high, low = two_parts(gain_grad)
    extra = place_of((sent_ref.shape[0] - rows, D), 0)
    sent_ref[:rows] = to_low(own_grad)
    sent_ref[rows:] = to_low(
        jnp.where(
            extra == 0,
            high.astype(jnp.float32),
            jnp.where(extra == 1, low.astype(jnp.float32), 0.0),
        )
    )


def senone_step(length, place, values, turned, targets, dense, gain_row):
    splits, tokens = lax.axis_size("hid"), values.shape[0]
    rows, first = tokens // splits, 7
    count = dense.shape[0] - first
    return whole_call(
        functools.partial(senone_kernel, gain_row, splits),
        [
            shaped((tokens, D), jnp.bfloat16),
            shaped((1, 1), jnp.float32),
            shaped((rows + 16, D), jnp.bfloat16),
        ]
        + [shaped((rows, count * D // splits), jnp.bfloat16)] * splits,
        [length, place],
        [values, turned, targets]
        + [(dense, (1, D, D), (first + number, 0, 0)) for number in range(count)],
        1_100_000_000,
    )


def pack_early_kernel(splits, place_ref, low_ref, *refs):
    blocks, others, out_ref = refs[:splits], refs[splits:-1], refs[-1]
    rows, width = blocks[0].shape
    total = None
    for step, block in enumerate(blocks):
        begin = pl.multiple_of((place_ref[0] + splits - step) % splits * rows, rows)
        part = dot_left(low_ref[pl.ds(begin, rows)], block[...])
        total = part if total is None else total + part
    out_ref[:, :width] = to_low(total)
    for other in others:
        out_ref[:, width : width + other.shape[1]] = to_low(other[...])
        width += other.shape[1]


def pack_early(place, low_normed, blocks, others):
    width = blocks[0].shape[1] + sum(part.shape[1] for part in others)
    return whole_call(
        functools.partial(pack_early_kernel, len(blocks)),
        [shaped((D, width), jnp.bfloat16)],
        [place],
        [low_normed, *blocks, *others],
        600_000_000,
    )[0]


def send_back(mixture, grad, plan_ref, gate_ref, rows_ref):
    index = plan_ref[2 * mixture : 2 * mixture + 1]
    chosen = (place_of((rows_ref.shape[0], grad.shape[0]), 0) == index).astype(jnp.float32)
    rows_ref[...] = to_low(dot_low(to_low(chosen), to_low(gate_ref[...] * (0.5 * grad))))


def assemble_kernel(mixture, place_ref, plan_ref, gate_ref, *refs):
    blocks, grad_ref, gain_grad_ref, rows_ref = refs[:-3], refs[-3], refs[-2], refs[-1]
    splits = len(blocks)
    rows = grad_ref.shape[0] // splits
    for step, block in enumerate(blocks):
        begin = pl.multiple_of((place_ref[0] + splits - step) % splits * rows, rows)
        grad_ref[pl.ds(begin, rows)] = block[:rows].astype(jnp.float32)
    gain_grad_ref[...] = sum(
        jnp.sum(block[rows:].astype(jnp.float32), 0, keepdims=True) for block in blocks
    )
    send_back(mixture, grad_ref[...], plan_ref, gate_ref, rows_ref)


def assemble_step(mixture, place, plan, gate, blocks, wide_rows):
    tokens = gate.shape[0]
    return whole_call(
        functools.partial(assemble_kernel, mixture),
        [
            shaped((tokens, D), jnp.float32),
            shaped((1, D), jnp.float32),
            shaped((wide_rows, D), jnp.bfloat16),
        ],
        [place],
        [plan, gate, *blocks],
        200_000_000,
    )


def send_back_kernel(mixture, plan_ref, gate_ref, grad_ref, rows_ref):
    send_back(mixture, grad_ref[...], plan_ref, gate_ref, rows_ref)


def send_back_step(mixture, plan, gate, grad, wide_rows):
    return whole_call(
        functools.partial(send_back_kernel, mixture),
        [shaped((wide_rows, D), jnp.bfloat16)],
        [],
        [plan, gate, grad],
        200_000_000,
    )[0]


def gate_backward_kernel(
    mixture,
    experts,
    gain_row,
    grad_ref,
    expert_out_ref,
    gate_ref,
    chances_ref,
    route_ref,
    values_ref,
    small_ref,
    turned_ref,
    side_ref,
    router_grad_ref,
):
    column = place_of((values_ref.shape[0], LANES), 1) - mixture * experts
    onehot = (column == route_ref[mixture]).astype(jnp.float32)
    gate_grad = jnp.sum(0.5 * grad_ref[...] * expert_out_ref[...], 1, keepdims=True)
    logit_grad = (gate_ref[...] * gate_grad) * (onehot - chances_ref[...])
    normed, _, _ = norm_forward(values_ref[...], turned_ref[gain_row : gain_row + 1])
    router_grad_ref[...] = exact_dot(normed, logit_grad, ((0,), (0,)))
    side_ref[...] = exact_dot(logit_grad, small_ref[:, LANES:], ((1,), (1,)))


def gate_backward(mixture, gain_row, grad, expert_out, gate, chances, routes, values, small, turned):
    return whole_call(
        functools.partial(gate_backward_kernel, mixture, lax.axis_size("dp"), gain_row),
        [shaped(grad.shape, jnp.float32), shaped((D, LANES), jnp.float32)],
        [],
        [grad, expert_out, gate, chances, routes, values, small, turned],
        800_000_000,
    )


def combine_backward_kernel(
    mixture, gain_row, plan_ref, grad_ref, side_ref, values_ref, turned_ref, *refs
):
    blocks, out_ref, gain_grad_ref = refs[:-2], refs[-2], refs[-1]
    gain = turned_ref[gain_row : gain_row + 1]
    normed_grad = side_ref[...] + combined(
        plan_ref[2 * mixture + 1 : 2 * mixture + 2], blocks
    )
    _, unit, inverse = norm_forward(values_ref[...], gain)
    back, gain_grad_ref[...] = norm_backward(normed_grad, unit, inverse, gain)
    out_ref[...] = grad_ref[...] + back


def combine_backward(mixture, gain_row, plan, grad, side, values, turned, blocks):
    return whole_call(
        functools.partial(combine_backward_kernel, mixture, gain_row),
        [shaped(grad.shape, jnp.float32), shaped((1, D), jnp.float32)],
        [],
        [plan, grad, side, values, turned, *blocks],
        500_000_000,
    )


def pack_grads_kernel(
    owners, grad_ref, features_ref, router_one_ref, router_two_ref, taps_ref, attend_ref, *refs
):
    gain_refs, out_ref, turn_ref = refs[:-2], refs[-2], refs[-1]
    bands, taps = features_ref.shape[0], taps_ref.shape[0]
    turn_ref[...] = jnp.zeros(turn_ref.shape, jnp.float32)
    turn_ref[2 * owners : 2 * owners + taps] = taps_ref[...]
    for number, gain_ref in enumerate(gain_refs):
        at = 2 * owners + taps + number
        turn_ref[at : at + 1] = gain_ref[...]
    out_ref[:, :LANES] = jnp.zeros((D, LANES), jnp.bfloat16)
    out_ref[:, :bands] = to_low(
        lax.dot_general(
            to_low(grad_ref[...]),
            features_ref[...],
            (((0,), (1,)), ((), ())),
            preferred_element_type=jnp.float32,
        )
    )
    out_ref[:, LANES : 2 * LANES] = to_low(
        turn_ref[...].T + router_one_ref[...] + router_two_ref[...]
    )
    out_ref[:, 2 * LANES :] = attend_ref[...]


def pack_grads(grad, features_turned, router_one, router_two, taps_grad, attend_grad, gain_grads):
    return whole_call(
        functools.partial(pack_grads_kernel, lax.axis_size("dp")),
        [shaped((D, 2 * LANES + attend_grad.shape[1]), jnp.bfloat16)],
        [],
        [grad, features_turned, router_one, router_two, taps_grad, attend_grad, *gain_grads],
        60_000_000,
        [pltpu.VMEM((LANES, D), jnp.float32)],
    )[0]


def shares_kernel(
    place_ref, length_ref, moved_ref, early_ref, square_ref, loss_ref, share_ref, out_ref
):
    share = jnp.zeros(share_ref.shape, jnp.float32)
    for owner in range(moved_ref.shape[0]):
        share = share + moved_ref[owner].astype(jnp.float32)
    share_ref[...] = share
    leading = place_ref[0] == 0
    small = share[:, : 2 * LANES]
    rest = share[:, 2 * LANES :]
    square = (
        jnp.where(leading, jnp.sum(small * small), 0.0)
        + jnp.sum(rest * rest)
        + jnp.sum(early_ref[...] * early_ref[...])
        + jnp.sum(square_ref[...])
    )
    count = jnp.where(leading, length_ref[0], 0).astype(jnp.float32)
    lane = place_of((1, LANES), 1)
    row = jnp.where(
        lane == 0, square, jnp.where(lane == 1, count, jnp.where(lane == 2, loss_ref[...], 0.0))
    )
    for device in range(out_ref.shape[0]):
        out_ref[device] = row


def shares_step(place, length, moved, early_share, squares, loss):
    devices = lax.axis_size("dp") * lax.axis_size("hid")
    return whole_call(
        shares_kernel,
        [shaped(moved.shape[1:], jnp.float32), shaped((devices, 1, LANES), jnp.float32)],
        [place, length],
        [moved, early_share, squares, loss],
        1_000_000,
    )


def totals_of(ref):
    rows = jnp.sum(ref[...], 0)
    lane = place_of(rows.shape, 1)
    square, count, loss = (jnp.sum(jnp.where(lane == part, rows, 0.0)) for part in range(3))
    norm = jnp.sqrt(square) / count
    return count, loss, norm, jnp.minimum(1.0, clip_limit / (norm + 1e-06)) / count


def orthogonal_kernel(pieces, experts, place_ref, totals_ref, *refs):
    momentum_refs, grad_refs = refs[:pieces], refs[pieces : 2 * pieces]
    out_refs, matrix_ref = refs[2 * pieces : 3 * pieces], refs[3 * pieces]
    _, _, _, factor = totals_of(totals_ref)
    gram = jnp.zeros((D, D), jnp.float32)
    for piece in range(pieces):
        current = muon_beta * momentum_refs[piece][...] + factor * grad_refs[piece][...].astype(
            jnp.float32
        )
        matrix_ref[piece] = current
        high, low = two_parts(current)
        cross = dot_right(high, low)
        gram = gram + (dot_right(high, high) + (cross + cross.T))
    row, column = place_of((D, D), 0), place_of((D, D), 1)
    square = jnp.sum(jnp.where(row == column, gram, 0.0))
    inverse = 1.0 / (jnp.sqrt(square) + 1e-07)
    gram = gram * (inverse * inverse)
    identity = jnp.where(row == column, newton_first, 0.0)
    total = None
    for turn in range(5):
        parts = two_parts(gram)
        poly = identity + newton_second * gram + newton_third * close_dot(parts, parts)
        poly_parts = two_parts(poly)
        total = poly if total is None else close_dot(poly_parts, two_parts(total))
        if turn < 4:
            gram = close_dot(poly_parts, two_parts(close_dot(poly_parts, parts)))
    kind_scale = jnp.where(
        place_ref[0] % 2 == 0,
        D ** (-0.5) * muon_rate * FF**0.5,
        3 * experts * FF ** (-0.5) * muon_rate * FF**0.5,
    )
    total_parts = two_parts(total * (inverse * kind_scale))
    for piece in range(pieces):
        out_refs[piece][...] = to_low(close_dot(total_parts, two_parts(matrix_ref[piece])))


def orthogonal(place, totals, momentum, grads):
    pieces = len(momentum)
    return whole_call(
        functools.partial(orthogonal_kernel, pieces, lax.axis_size("dp")),
        [shaped((D, D), jnp.bfloat16)] * pieces,
        [place],
        [totals, *momentum, *grads],
        19_000_000_000,
        [pltpu.VMEM((pieces, D, D), jnp.float32)],
    )


def momentum_kernel(totals_ref, momentum_ref, one_ref, two_ref, out_ref):
    _, _, _, factor = totals_of(totals_ref)
    first = pl.program_id(0) < 2
    grad = jnp.where(first, one_ref[0], two_ref[0])
    out_ref[0] = muon_beta * momentum_ref[0] + factor * grad


def momentum_update(totals, momentum, grads_one, grads_two):
    block = (1,) + momentum.shape[1:]
    return pl.pallas_call(
        momentum_kernel,
        grid=(4,),
        out_shape=shaped(momentum.shape, jnp.float32),
        in_specs=[
            pl.BlockSpec(totals.shape, lambda step: (0, 0, 0)),
            pl.BlockSpec(block, lambda step: (step, 0, 0)),
            pl.BlockSpec(block, lambda step: (jnp.minimum(step, 1), 0, 0)),
            pl.BlockSpec(block, lambda step: (jnp.maximum(step - 2, 0), 0, 0)),
        ],
        out_specs=pl.BlockSpec(block, lambda step: (step, 0, 0)),
        compiler_params=pltpu.CompilerParams(vmem_limit_bytes=32 * 1024 * 1024),
        cost_estimate=pl.CostEstimate(
            flops=3_000_000, bytes_accessed=12_000_000, transcendentals=0
        ),
    )(totals, momentum, grads_one, grads_two)


def update_kernel(place_ref, weight_ref, *refs):
    out_ref, turn = refs[-1], pl.program_id(0)
    for step, update_ref in enumerate(refs[:-1]):

        @pl.when(turn == step)
        def _():
            out_ref[0] = (1.0 - muon_decay) * weight_ref[0] - update_ref[...].astype(jnp.float32)


def expert_update(place, weights, updates):
    count = weights.shape[0]

    def turned(step, place_ref):
        return ((place_ref[0] + step) % count, 0, 0)

    block = (1,) + weights.shape[1:]
    return pl.pallas_call(
        update_kernel,
        out_shape=jax.ShapeDtypeStruct(weights.shape, jnp.float32),
        grid_spec=pltpu.PrefetchScalarGridSpec(
            num_scalar_prefetch=1,
            grid=(count,),
            in_specs=[pl.BlockSpec(block, turned)]
            + [pl.BlockSpec(update.shape, lambda step, place_ref: (0, 0)) for update in updates],
            out_specs=pl.BlockSpec(block, turned),
        ),
        compiler_params=pltpu.CompilerParams(vmem_limit_bytes=32 * 1024 * 1024),
        cost_estimate=pl.CostEstimate(
            flops=3_000_000, bytes_accessed=10_000_000, transcendentals=0
        ),
    )(place, weights, *updates)


def adam_update(weight, grad, first, second, rate, decay):
    first_new = beta_one * first + (1.0 - beta_one) * grad
    second_new = beta_two * second + (1.0 - beta_two) * grad * grad
    corrected = (
        first_new
        / (1.0 - beta_one**STEP)
        / (jnp.sqrt(second_new / (1.0 - beta_two**STEP)) + adam_epsilon)
    )
    return (first_new, second_new, weight - rate * (corrected + decay * weight))


def adam_kernel(owners, splits, place_ref, totals_ref, share_ref, senone_ref, *refs):
    blocks, states = refs[:splits], refs[splits : splits + 24]
    outs, scalars_ref = refs[splits + 24 : splits + 48], refs[splits + 48]
    turn_ref, gather_ref = refs[splits + 49 :]
    count, loss, norm, factor = totals_of(totals_ref)
    lane = place_of((1, LANES), 1)
    scalars_ref[...] = jnp.where(
        lane == 0, loss, jnp.where(lane == 1, count, jnp.where(lane == 2, norm, 0.0))
    )
    width = blocks[0].shape[1] // 7
    for step, block in enumerate(blocks):
        begin = pl.multiple_of((place_ref[0] + splits - step) % splits * width, width)
        for part in range(7):
            gather_ref[part, :, pl.ds(begin, width)] = block[:, part * width : (part + 1) * width]
    own = share_ref.shape[0]
    bands = states[0].shape[1]
    taps, gains = states[4].shape[0], states[7].shape[0]
    turn_ref[...] = jnp.zeros(turn_ref.shape, jnp.float32)
    turn_ref[:own] = share_ref[:, LANES : 2 * LANES]
    turned = turn_ref[...].T
    begin = 2 * owners

    def apply(number, at, grad, rate=adam_rate, decay=weight_decay):
        first, second, weight = (states[number + 8 * part] for part in (1, 2, 0))
        found = adam_update(weight[at], grad * factor, first[at], second[at], rate, decay)
        for ref, value in zip(outs[3 * number : 3 * number + 3], found):
            ref[at] = value

    everything = (slice(None), slice(None))
    apply(0, everything, share_ref[:, :bands])
    for part in range(3):
        apply(1, (slice(None), slice(part * D, (part + 1) * D)), gather_ref[part])
    for part in range(2):
        apply(2, (part,), gather_ref[3 + part])
        apply(3, (slice(None), slice(part * D, (part + 1) * D)), gather_ref[5 + part])
        apply(
            5,
            (part,),
            share_ref[:, LANES + part * owners : LANES + (part + 1) * owners],
        )
    apply(4, everything, turned[begin : begin + taps, :own])
    apply(6, everything, senone_ref[...])
    apply(7, everything, turned[begin + taps : begin + taps + gains, :own], gain_rate, 0.0)


def adam_step(place, totals, share, senone_share, blocks, weights, firsts, seconds):
    rows, splits = share.shape[0], len(blocks)
    outs = [shaped(part.shape, jnp.float32) for part in weights for _ in range(3)]
    return whole_call(
        functools.partial(adam_kernel, lax.axis_size("dp"), splits),
        outs + [shaped((1, LANES), jnp.float32)],
        [place],
        [totals, share, senone_share, *blocks, *weights, *firsts, *seconds],
        4_000_000,
        [
            pltpu.VMEM((LANES, LANES), jnp.float32),
            pltpu.VMEM((7, rows, D), jnp.float32),
        ],
    )


def convolution_forward(values, gains, weight_in, depth, weight_out, valid):
    tokens = values.shape[0]
    normed, unit, inverse = norm_forward(values, gains[2])
    low_normed = to_low(normed)
    linear = dot_low(low_normed, weight_in[0])
    gating = jax.nn.sigmoid(dot_low(low_normed, weight_in[1]))
    mixed = linear * gating * valid[:, None]
    reach = (depth.shape[0] - 1) // 2
    padded = jnp.pad(mixed, ((reach, reach), (0, 0)))
    deep = jnp.zeros_like(mixed)
    for offset in range(depth.shape[0]):
        deep = deep + depth[offset] * padded[offset : offset + tokens]
    count = jnp.sum(valid)
    mask = valid[:, None]
    mean = jnp.sum(mask * deep, 0) / count
    spread = jnp.sum(mask * deep * deep, 0) / count - mean * mean
    scale = lax.rsqrt(spread + 1e-05)
    unit_batch = (deep - mean) * scale
    shifted = unit_batch * gains[5] + gains[6]
    activated = to_low(jax.nn.silu(shifted))
    kept = (
        unit,
        inverse,
        low_normed,
        linear,
        gating,
        padded,
        scale,
        unit_batch,
        shifted,
        activated,
    )
    return (values + dot_low(activated, weight_out), kept)


def convolution_backward(grad, gains, weight_in, depth, weight_out, valid, kept):
    unit, inverse, low_normed, linear, gating, padded, scale, unit_batch, shifted, activated = kept
    tokens = grad.shape[0]
    low_grad = to_low(grad)
    out_grad = dot_left(activated, own_part(low_grad, 1))
    shifted_grad = dot_right(low_grad, weight_out) * silu_slope(shifted)
    gamma_grad = jnp.sum(shifted_grad * unit_batch, 0)
    beta_grad = jnp.sum(shifted_grad, 0)
    unit_grad = shifted_grad * gains[5]
    count = jnp.sum(valid)
    mask = valid[:, None]
    first_sum = jnp.sum(mask * unit_grad, 0) / count
    second_sum = jnp.sum(mask * unit_grad * unit_batch, 0) / count
    deep_grad = scale * (unit_grad - mask * (first_sum + unit_batch * second_sum))
    reach = (depth.shape[0] - 1) // 2
    padded_grad = jnp.pad(deep_grad, ((reach, reach), (0, 0)))
    mixed_grad = jnp.zeros_like(deep_grad)
    depth_rows = []
    for offset in range(depth.shape[0]):
        begin = 2 * reach - offset
        mixed_grad = mixed_grad + depth[offset] * padded_grad[begin : begin + tokens]
        depth_rows.append(jnp.sum(deep_grad * padded[offset : offset + tokens], 0))
    mixed_grad = mixed_grad * mask
    project_grad = [
        to_low(mixed_grad * gating),
        to_low(mixed_grad * linear * gating * (1.0 - gating)),
    ]
    in_grad = [dot_left(low_normed, own_part(part, 1)) for part in project_grad]
    normed_grad = sum(dot_right(part, weight_in[place]) for place, part in enumerate(project_grad))
    values_grad, gain_grad = norm_backward(normed_grad, unit, inverse, gains[2])
    return (
        grad + values_grad,
        gain_grad,
        gamma_grad[None],
        beta_grad[None],
        in_grad,
        jnp.stack(depth_rows),
        out_grad,
    )


def on_device(
    features,
    lengths,
    routes,
    alignments,
    input_weight,
    attention_in,
    branch_out,
    pointwise_in,
    depthwise,
    router,
    senone_table,
    norm_scales,
    expert_weights,
    input_first,
    input_second,
    attention_first,
    attention_second,
    branch_first,
    branch_second,
    pointwise_first,
    pointwise_second,
    depthwise_first,
    depthwise_second,
    router_first,
    router_second,
    senone_first,
    senone_second,
    scales_first,
    scales_second,
    expert_momentum,
):
    owners, splits = lax.axis_size("dp"), lax.axis_size("hid")
    tokens = features.shape[0]
    taps, gains = depthwise.shape[0], norm_scales.shape[0]
    place = lax.axis_index("hid")
    place_array = place[None].astype(jnp.int32)
    gain_begin = 2 * owners + taps
    share = 3 * tokens // (2 * owners) // splits
    wide = -(-share // 8) * 8
    slots, wide_rows = (share, wide), owners * wide

    small = pack_small(input_weight.T, router, depthwise, norm_scales)
    near = to_low(expert_weights[0, :, 0])
    before, behind = shift(near, 1), shift(near, -1)
    small = after(
        exchange_rows(small.reshape(owners * small.shape[1], -1)), before, behind
    )
    weights_one = [near, before, behind, shift(before[0], 1), shift(behind[1], -1)]
    dense = pack_dense(
        attention_in, branch_out, pointwise_in, gather_near(to_low(senone_table))
    )
    dense = lax.all_gather(dense, "dp", axis=1, tiled=True)
    low_two = to_low(expert_weights[1, :, 0])
    momentum_pieces = expert_momentum.reshape((2 * 2,) + expert_momentum.shape[3:])
    valid = (jnp.arange(tokens, dtype=jnp.int32) < lengths[0]).astype(jnp.float32)
    plan = plan_slots(place_array, routes[:, :, 0], share, wide)
    targets = alignments[:, None]
    features_turned = features.T

    start, turned, rows, gate_one, chances_one = start_step(
        small, features_turned, plan, routes, gain_begin, wide_rows
    )
    depth_full = turned[2 * owners : gain_begin]
    scales_full = turned[gain_begin : gain_begin + gains]
    weights_two = [lax.all_gather(after(low_two, rows), "hid", axis=0, tiled=False)]
    forward_one, returned = expert_forward(place_array, exchange_rows(rows), weights_one, slots)
    blocks = gather_slots(exchange_rows(returned), slots)
    expert_out_one, first = combine_step(0, plan, gate_one, start, blocks)

    second, *kept_attend = attention_forward(lengths, first, turned, dense, gain_begin + 1)
    third, kept_convolve = convolution_forward(
        second, scales_full, dense[5:7], depth_full, dense[4], valid
    )

    rows, gate_two, chances_two = dispatch_step(
        1, third, small, turned, plan, routes, gain_begin + 3, wide_rows
    )
    kept_rows_one = forward_one[0]
    forward_one = spread(forward_one, rows)
    forward_two, returned = expert_forward(place_array, exchange_rows(rows), weights_two, slots)
    blocks = gather_slots(after(exchange_rows(returned), *forward_one), slots)
    expert_out_two, fourth = combine_step(1, plan, gate_two, third, blocks)
    kept_rows_two = forward_two[0]

    low_normed, loss_local, sent, *logit_grad = senone_step(
        lengths, place_array, fourth, turned, targets, dense, gain_begin + 4
    )
    blocks = gather_near(sent)
    grad, gain_five, rows = assemble_step(1, place_array, plan, gate_two, blocks, wide_rows)
    logit_grad = spread(logit_grad, grad)
    forward_two = spread(forward_two, grad)

    rows_grad = after(exchange_rows(rows), *logit_grad)
    backward_two, returned = expert_backward(
        place_array, kept_rows_two, rows_grad, weights_two, slots
    )
    side, router_two = gate_backward(
        1,
        gain_begin + 3,
        grad,
        expert_out_two,
        gate_two,
        chances_two,
        routes,
        third,
        small,
        turned,
    )
    blocks = gather_slots(after(exchange_rows(returned), *forward_two), slots)
    grad, gain_four = combine_backward(
        1, gain_begin + 3, plan, grad, side, third, turned, blocks
    )
    backward_two = spread(backward_two, grad)
    ready = after(momentum_pieces, grad)
    owned_momentum = [ready[place]] + [
        shift(ready[(place + step) % splits], step) for step in range(1, splits)
    ]

    grad, gain_three, gamma_grad, beta_grad, pointwise_grad, depth_grad, conv_out_grad = (
        convolution_backward(
            grad, scales_full, dense[5:7], depth_full, dense[4], valid, kept_convolve
        )
    )
    early = pack_early(place_array, low_normed, logit_grad, [conv_out_grad] + pointwise_grad)
    grad = after(grad, *backward_two)
    experts_two = expert_grads(forward_two, backward_two)
    grad, gain_two, attend_grad = attention_backward(
        lengths, place_array, grad, first, turned, dense, kept_attend, gain_begin + 1
    )

    grad = after(grad, owned_momentum[1])
    rows_grad = exchange_rows(send_back_step(0, plan, gate_one, grad, wide_rows))
    rows_grad = after(rows_grad, owned_momentum[3])
    backward_one, returned = expert_backward(
        place_array, kept_rows_one, rows_grad, weights_one, slots
    )
    side, router_one = gate_backward(
        0, gain_begin, grad, expert_out_one, gate_one, chances_one, routes, start, small, turned
    )
    returned = after(exchange_rows(returned), owned_momentum[2])
    early_moved = exchange_rows(after(early, returned))
    blocks = gather_slots(returned, slots)
    grad, gain_one = combine_backward(0, gain_begin, plan, grad, side, start, turned, blocks)
    last = pack_grads(
        grad,
        features_turned,
        router_one,
        router_two,
        depth_grad,
        attend_grad,
        [gain_one, gain_two, gain_three, gain_four, gain_five, gamma_grad, beta_grad],
    )
    received = spread(backward_one, *blocks)
    experts_one, squares, sent = last_expert_grads(
        place_array, forward_one, after(tuple(received), last), experts_two
    )
    owned_grad = spread(sent)
    moved = exchange_rows(last)
    early_share = jnp.sum(
        early_moved.reshape(owners, D // owners, -1).astype(jnp.float32), 0
    )
    width = senone_table.shape[1]
    senone_share, conv_share = early_share[:, :width], early_share[:, width:]
    last_share, totals = shares_step(
        place_array,
        lengths,
        moved.reshape(owners, D // owners, -1),
        early_share,
        squares,
        loss_local,
    )
    blocks = gather_near(jnp.concatenate([last_share[:, 2 * LANES :], conv_share], 1))
    totals = lax.all_to_all(totals, ("dp", "hid"), split_axis=0, concat_axis=0, tiled=True)
    totals = after(totals, *blocks)

    orth = orthogonal(place_array, totals, owned_momentum, owned_grad)
    returned = [orth[0]] + [shift(orth[step], -step) for step in range(1, splits)]
    momentum_new = momentum_update(totals, momentum_pieces, experts_one, experts_two)
    *updated, scalars = adam_step(
        place_array,
        totals,
        last_share,
        senone_share,
        blocks,
        [
            input_weight.T,
            attention_in,
            branch_out,
            pointwise_in,
            depthwise,
            router,
            senone_table,
            norm_scales,
        ],
        [
            input_first.T,
            attention_first,
            branch_first,
            pointwise_first,
            depthwise_first,
            router_first,
            senone_first,
            scales_first,
        ],
        [
            input_second.T,
            attention_second,
            branch_second,
            pointwise_second,
            depthwise_second,
            router_second,
            senone_second,
            scales_second,
        ],
    )
    experts_new = expert_update(
        place_array, expert_weights.reshape(momentum_pieces.shape), returned
    )
    return (
        scalars[0, 0],
        scalars[0, 1],
        scalars[0, 2],
        *[part.T for part in updated[:3]],
        *updated[3:],
        momentum_new.reshape(expert_momentum.shape),
        experts_new.reshape(expert_weights.shape),
    )


def solution(mesh):
    return jax.shard_map(
        on_device,
        mesh=mesh,
        in_specs=(
            P("dp", None),
            P("dp"),
            P(None, "dp", None),
            P("dp"),
            P(None, "dp"),
            P("dp", None),
            P(None, "dp", None),
            P("dp", None),
            P(None, "dp"),
            P(None, "dp", None),
            P("dp", "hid"),
            P(None, "dp"),
            P(None, None, "dp", None, "hid"),
            P(None, "dp"),
            P(None, "dp"),
            P("dp", None),
            P("dp", None),
            P(None, "dp", None),
            P(None, "dp", None),
            P("dp", None),
            P("dp", None),
            P(None, "dp"),
            P(None, "dp"),
            P(None, "dp", None),
            P(None, "dp", None),
            P("dp", "hid"),
            P("dp", "hid"),
            P(None, "dp"),
            P(None, "dp"),
            P(None, None, "dp", None, "hid"),
        ),
        out_specs=(
            P(),
            P(),
            P(),
            P(None, "dp"),
            P(None, "dp"),
            P(None, "dp"),
            P("dp", None),
            P("dp", None),
            P("dp", None),
            P(None, "dp", None),
            P(None, "dp", None),
            P(None, "dp", None),
            P("dp", None),
            P("dp", None),
            P("dp", None),
            P(None, "dp"),
            P(None, "dp"),
            P(None, "dp"),
            P(None, "dp", None),
            P(None, "dp", None),
            P(None, "dp", None),
            P("dp", "hid"),
            P("dp", "hid"),
            P("dp", "hid"),
            P(None, "dp"),
            P(None, "dp"),
            P(None, "dp"),
            P(None, None, "dp", None, "hid"),
            P(None, None, "dp", None, "hid"),
        ),
        check_vma=False,
    )
```

```python
import functools

import jax
import jax.numpy as jnp
from jax import lax
from jax.experimental import pallas as pl
from jax.experimental.pallas import tpu as pltpu
from jax.sharding import PartitionSpec as P

D = 512
HEADS = 8
HEAD_DIM = 64
FF = 2048
STEP = 10
LANES = 128


clip_limit = 0.02
beta_one = 0.9
beta_two = 0.999
adam_epsilon = 1e-08
adam_rate = 0.2
gain_rate = 0.6
weight_decay = 0.01
muon_beta = 0.95
muon_rate = 1.0
muon_decay = 0.01
newton_first = 3.4445
newton_second = -4.775
newton_third = 2.0315


def shift(values, step):
    size = lax.axis_size("hid")
    return lax.ppermute(values, "hid", [(i, (i + step) % size) for i in range(size)])


def gather_near(values):
    return [values] + [shift(values, step) for step in range(1, lax.axis_size("hid"))]


def together(*values):
    return lax.optimization_barrier(values)


def spread(pieces):
    return [pieces[0]] + [shift(pieces[step], step) for step in range(1, len(pieces))]


def own_part(values, axis):
    width = values.shape[axis] // lax.axis_size("hid")
    return lax.dynamic_slice_in_dim(values, lax.axis_index("hid") * width, width, axis)


def exchange_rows(values):
    owners = lax.axis_size("dp")
    shape = values.shape
    shaped_rows = values.reshape((owners, shape[0] // owners) + shape[1:])
    moved = lax.all_to_all(shaped_rows, "dp", split_axis=0, concat_axis=0, tiled=True)
    return moved.reshape(shape)


def to_low(values):
    return values.astype(jnp.bfloat16)


def dot_low(left, right):
    return jnp.dot(left, right, preferred_element_type=jnp.float32)


def dot_left(left, right):
    return lax.dot_general(
        left, right, (((0,), (0,)), ((), ())), preferred_element_type=jnp.float32
    )


def dot_right(left, right):
    return lax.dot_general(
        left, right, (((1,), (1,)), ((), ())), preferred_element_type=jnp.float32
    )


def exact_dot(left, right, dims=((1,), (0,))):
    return lax.dot_general(
        left,
        right,
        (dims, ((), ())),
        precision=lax.Precision.HIGHEST,
        preferred_element_type=jnp.float32,
    )


def two_parts(values):
    high = to_low(values)
    return high, to_low(values - high.astype(jnp.float32))


def close_dot(left, right):
    return dot_low(left[0], right[0]) + (dot_low(left[0], right[1]) + dot_low(left[1], right[0]))


def norm_forward(values, gain):
    centered = values - jnp.mean(values, -1, keepdims=True)
    inverse = lax.rsqrt(jnp.mean(centered * centered, -1, keepdims=True) + 1e-05)
    unit = centered * inverse
    return (unit * gain, unit, inverse)


def norm_backward(grad, unit, inverse, gain):
    scaled = grad * gain
    back = inverse * (
        scaled
        - jnp.mean(scaled, -1, keepdims=True)
        - unit * jnp.mean(scaled * unit, -1, keepdims=True)
    )
    return (back, jnp.sum(grad * unit, 0, keepdims=True))


def silu_slope(values):
    sigma = jax.nn.sigmoid(values)
    return sigma * (1.0 + values * (1.0 - sigma))


def shaped(shape, dtype):
    return jax.ShapeDtypeStruct(shape, dtype)


def place_of(shape, axis):
    return lax.broadcasted_iota(jnp.int32, shape, axis)


def whole_call(kernel, out_shapes, scalars, arrays, flops, scratch=(), room=48):
    parts = [
        part if isinstance(part, tuple) else (part, part.shape, (0,) * part.ndim)
        for part in arrays
    ]
    specs = [
        pl.BlockSpec(block, functools.partial(lambda fixed, step: fixed, at))
        for _, block, at in parts
    ]
    moved = sum(part.size * part.dtype.itemsize for part, _, _ in parts) + sum(
        part.size * part.dtype.itemsize for part in out_shapes
    )
    return pl.pallas_call(
        kernel,
        grid=(1,),
        out_shape=out_shapes,
        in_specs=[pl.BlockSpec(memory_space=pltpu.SMEM)] * len(scalars) + specs,
        out_specs=[
            pl.BlockSpec(part.shape, functools.partial(lambda rank, step: (0,) * rank, len(part.shape)))
            for part in out_shapes
        ],
        scratch_shapes=list(scratch),
        compiler_params=pltpu.CompilerParams(vmem_limit_bytes=room * 1024 * 1024),
        cost_estimate=pl.CostEstimate(flops=flops, bytes_accessed=moved, transcendentals=0),
    )(*scalars, *[part for part, _, _ in parts])


def pack_small_kernel(owners, input_ref, router_ref, depth_ref, gains_ref, out_ref, turn_ref):
    bands, taps, gains = input_ref.shape[1], depth_ref.shape[0], gains_ref.shape[0]
    width = input_ref.shape[0]
    turn_ref[...] = jnp.zeros(turn_ref.shape, jnp.float32)
    turn_ref[2 * owners : 2 * owners + taps, :width] = depth_ref[...]
    turn_ref[2 * owners + taps : 2 * owners + taps + gains, :width] = gains_ref[...]
    turned = turn_ref[...].T[:width]
    out_ref[...] = jnp.zeros(out_ref.shape, jnp.float32)
    for owner in range(owners):
        out_ref[owner, :, LANES:] = turned
        out_ref[owner, :, :bands] = input_ref[...]
        out_ref[owner, :, LANES : LANES + owners] = router_ref[0]
        out_ref[owner, :, LANES + owners : LANES + 2 * owners] = router_ref[1]


def pack_small(input_turned, router, depthwise, norm_scales):
    owners, width = lax.axis_size("dp"), input_turned.shape[0]
    return whole_call(
        functools.partial(pack_small_kernel, owners),
        [shaped((owners, width, 2 * LANES), jnp.float32)],
        [],
        [input_turned, router, depthwise, norm_scales],
        1000,
        [pltpu.VMEM((LANES, LANES), jnp.float32)],
    )[0]


def pack_dense_kernel(attention_ref, branch_ref, pointwise_ref, out_ref):
    for part in range(3):
        out_ref[part] = to_low(attention_ref[:, part * D : (part + 1) * D])
    for part in range(2):
        out_ref[3 + part] = to_low(branch_ref[part])
        out_ref[5 + part] = to_low(pointwise_ref[:, part * D : (part + 1) * D])


def pack_dense(attention_in, branch_out, pointwise_in):
    return whole_call(
        pack_dense_kernel,
        [shaped((7, attention_in.shape[0], D), jnp.bfloat16)],
        [],
        [attention_in, branch_out, pointwise_in],
        1000,
    )[0]


def plan_kernel(experts, splits, share, wide, place_ref, routes_ref, out_ref):
    tokens = routes_ref.shape[1]
    before = (place_of((tokens, tokens), 0) < place_of((tokens, tokens), 1)).astype(jnp.float32)
    for mixture in range(2):
        route = routes_ref[mixture : mixture + 1]
        onehot = (place_of((experts, tokens), 0) == route).astype(jnp.float32)
        earlier = dot_low(to_low(onehot), to_low(before))
        slot = jnp.sum(earlier * onehot, 0, keepdims=True).astype(jnp.int32)
        quarter = sum((slot >= (part + 1) * share).astype(jnp.int32) for part in range(splits - 1))
        within = slot - quarter * share
        out_ref[2 * mixture : 2 * mixture + 1] = jnp.where(
            quarter == place_ref[0], route * wide + within, -1
        )
        out_ref[2 * mixture + 1 : 2 * mixture + 2] = (
            route * splits + quarter
        ) * wide + within
        if mixture == 0:
            out_ref[0:1] = route * (share * splits) + slot
            out_ref[1:2] = (
                (place_ref[0] - quarter + splits) % splits * experts + route
            ) * share + within


def plan_slots(place, routes, share, wide):
    return whole_call(
        functools.partial(
            plan_kernel, lax.axis_size("dp"), lax.axis_size("hid"), share, wide
        ),
        [shaped((4, routes.shape[1]), jnp.int32)],
        [place],
        [routes],
        1_000_000,
    )[0]


def narrowing(share_rows, wide_rows, share, wide):
    at = place_of((share_rows, wide_rows), 1)
    within = at % wide
    return to_low(
        ((place_of((share_rows, wide_rows), 0) == at // wide * share + within) & (within < share))
        .astype(jnp.float32)
    )


def routing(mixture, experts, normed, router, route):
    column = place_of((normed.shape[0], LANES), 1) - mixture * experts
    inside = (column >= 0) & (column < experts)
    logits = jnp.where(inside, exact_dot(normed, router), -1e30)
    raised = jnp.where(inside, jnp.exp(logits - jnp.max(logits, 1, keepdims=True)), 0.0)
    return raised / jnp.sum(raised, 1, keepdims=True), (column == route).astype(jnp.float32)


def dispatch(mixture, experts, values, gain, router, route, index, slots_ref, gate_ref, chances_ref):
    normed, _, _ = norm_forward(values, gain)
    chosen = (place_of((slots_ref.shape[0], values.shape[0]), 0) == index).astype(jnp.float32)
    slots_ref[...] = to_low(dot_low(to_low(chosen), to_low(normed)))
    chances, onehot = routing(mixture, experts, normed, router, route)
    gate_ref[...] = jnp.sum(chances * onehot, 1, keepdims=True)
    chances_ref[...] = chances


def dispatch_shapes(tokens, wide_rows):
    return [
        shaped((wide_rows, D), jnp.bfloat16),
        shaped((tokens, 1), jnp.float32),
        shaped((tokens, LANES), jnp.float32),
    ]


def start_kernel(
    experts, gain_row, small_ref, features_ref, plan_ref, route_ref, start_ref, turned_ref, *out
):
    bands = features_ref.shape[0]
    start = lax.dot_general(
        features_ref[...],
        to_low(small_ref[:, :bands]),
        (((0,), (1,)), ((), ())),
        preferred_element_type=jnp.float32,
    )
    start_ref[...] = start
    router = small_ref[:, LANES:]
    turned_ref[...] = router.T
    gain = turned_ref[gain_row : gain_row + 1]
    dispatch(0, experts, start, gain, router, route_ref[0], plan_ref[:1], *out)


def start_step(small, features_turned, plan, routes, gain_row, wide_rows):
    tokens = features_turned.shape[1]
    return whole_call(
        functools.partial(start_kernel, lax.axis_size("dp"), gain_row),
        [shaped((tokens, D), jnp.float32), shaped((LANES, D), jnp.float32)]
        + dispatch_shapes(tokens, wide_rows),
        [],
        [small, features_turned, plan, routes],
        700_000_000,
    )


def dispatch_kernel(
    mixture, experts, gain_row, values_ref, small_ref, turned_ref, plan_ref, route_ref, *out
):
    dispatch(
        mixture,
        experts,
        values_ref[...],
        turned_ref[gain_row : gain_row + 1],
        small_ref[:, LANES:],
        route_ref[mixture],
        plan_ref[2 * mixture : 2 * mixture + 1],
        *out,
    )


def dispatch_step(mixture, values, small, turned, plan, routes, gain_row, wide_rows):
    return whole_call(
        functools.partial(dispatch_kernel, mixture, lax.axis_size("dp"), gain_row),
        dispatch_shapes(values.shape[0], wide_rows),
        [],
        [values, small, turned, plan, routes],
        700_000_000,
    )


def expert_pieces(refs, step):
    return refs[step][0], refs[step][1]


def for_all(narrow, total, splits, wide, out_ref):
    rows = dot_left(narrow, to_low(total)).reshape(-1, 1, wide, D)
    copies = jnp.broadcast_to(rows, (rows.shape[0], splits, wide, D))
    out_ref[...] = to_low(copies.reshape(out_ref.shape))


def expert_forward_kernel(splits, share, wide, place_ref, rows_ref, *refs):
    weights, sent_refs, returned_ref = refs[: -splits - 1], refs[-splits - 1 : -1], refs[-1]
    place, count = place_ref[0], sent_refs[0].shape[0] // 2
    narrow = narrowing(count, rows_ref.shape[0], share, wide)
    rows = to_low(dot_low(narrow, rows_ref[...]))
    total = jnp.zeros(rows.shape, jnp.float32)
    for step in range(splits):
        weight_in, weight_out = expert_pieces(weights, step)
        active = dot_low(rows, weight_in)
        hidden = to_low(active * jax.nn.sigmoid(active))
        sent_ref = sent_refs[(splits - step) % splits]
        sent_ref[:count] = rows
        sent_ref[count:] = hidden
        total = total + dot_right(hidden, weight_out)
    for_all(narrow, total, splits, wide, returned_ref)


def expert_backward_kernel(splits, share, wide, place_ref, kept_ref, grad_ref, *refs):
    weights, sent_refs, returned_ref = refs[: -splits - 1], refs[-splits - 1 : -1], refs[-1]
    place, count = place_ref[0], kept_ref.shape[0] // 2
    narrow = narrowing(count, grad_ref.shape[0], share, wide)
    rows, rows_grad = kept_ref[:count], to_low(dot_low(narrow, grad_ref[...]))
    total = jnp.zeros(rows.shape, jnp.float32)
    for step in range(splits):
        weight_in, weight_out = expert_pieces(weights, step)
        active = dot_low(rows, weight_in)
        active_grad = to_low(dot_low(rows_grad, weight_out) * silu_slope(active))
        sent_ref = sent_refs[(splits - step) % splits]
        sent_ref[:count] = rows_grad
        sent_ref[count:] = active_grad
        total = total + dot_right(active_grad, weight_in)
    for_all(narrow, total, splits, wide, returned_ref)


def expert_call(kernel, place, arrays, weights, slots, rows, flops):
    splits, experts = lax.axis_size("hid"), lax.axis_size("dp")
    share, wide = slots
    *sent, returned = whole_call(
        functools.partial(kernel, splits, share, wide),
        [shaped((2 * experts * share, D), jnp.bfloat16)] * splits
        + [shaped((rows.shape[0] * splits, D), jnp.bfloat16)],
        [place],
        [*arrays, *weights],
        flops,
    )
    return sent, returned


def expert_forward(place, rows, weights, slots):
    return expert_call(
        expert_forward_kernel, place, [rows], weights, slots, rows, 4 * rows.shape[0] * D * FF
    )


def expert_backward(place, kept, rows_grad, weights, slots):
    return expert_call(
        expert_backward_kernel,
        place,
        [kept, rows_grad],
        weights,
        slots,
        rows_grad,
        6 * rows_grad.shape[0] * D * FF,
    )


def widen(values, share, wide, out_ref):
    narrow = narrowing(32 * share, 32 * wide, share, wide)
    for block in range(values.shape[0] // narrow.shape[0]):
        part = values[block * narrow.shape[0] : (block + 1) * narrow.shape[0]]
        out_ref[block * narrow.shape[1] : (block + 1) * narrow.shape[1]] = to_low(
            dot_left(narrow, part)
        )


def split_forward_kernel(share, wide, rows_ref, weight_ref, returned_ref):
    active = dot_low(rows_ref[...], weight_ref[0])
    hidden = to_low(active * jax.nn.sigmoid(active))
    widen(to_low(dot_right(hidden, weight_ref[1])), share, wide, returned_ref)


def split_backward_kernel(
    share, wide, rows_ref, grad_ref, weight_ref, hidden_ref, active_grad_ref, returned_ref
):
    active = dot_low(rows_ref[...], weight_ref[0])
    active_grad = to_low(dot_low(grad_ref[...], weight_ref[1]) * silu_slope(active))
    widen(to_low(dot_right(active_grad, weight_ref[0])), share, wide, returned_ref)
    hidden_ref[...] = to_low(active * jax.nn.sigmoid(active))
    active_grad_ref[...] = active_grad


def split_forward(rows, weights, slots):
    share, wide = slots
    return whole_call(
        functools.partial(split_forward_kernel, share, wide),
        [shaped((rows.shape[0] // share * wide, D), jnp.bfloat16)],
        [],
        [rows, weights],
        4 * rows.shape[0] * D * D,
    )[0]


def split_backward(rows, rows_grad, weights, slots):
    share, wide = slots
    return whole_call(
        functools.partial(split_backward_kernel, share, wide),
        [shaped(rows.shape, jnp.bfloat16)] * 2
        + [shaped((rows.shape[0] // share * wide, D), jnp.bfloat16)],
        [],
        [rows, rows_grad, weights],
        6 * rows.shape[0] * D * D,
    )


def sum_kernel(share, wide, splits, moved_ref, out_ref):
    values = moved_ref[...].astype(jnp.float32).reshape(-1, splits, wide, D)
    total = to_low(jnp.sum(values, 1).reshape(-1, D))
    narrow = narrowing(out_ref.shape[0], total.shape[0], share, wide)
    out_ref[...] = to_low(dot_low(narrow, total))


def sum_kernel(share, wide, splits, moved_ref, out_ref):
    values = moved_ref[...].astype(jnp.float32).reshape(-1, splits, wide, D)
    total = to_low(jnp.sum(values, 1).reshape(-1, D))
    narrow = narrowing(out_ref.shape[0], total.shape[0], share, wide)
    out_ref[...] = to_low(dot_low(narrow, total))


def gather_sums(moved, slots):
    share, wide = slots
    splits = lax.axis_size("hid")
    rows = moved.shape[0] // splits // wide * share
    return gather_near(
        whole_call(
            functools.partial(sum_kernel, share, wide, splits),
            [shaped((rows, D), jnp.bfloat16)],
            [],
            [moved],
            50_000_000,
        )[0]
    )


def exchange_all(rows, wide):
    moved = lax.all_to_all(
        rows.reshape(-1, wide, D), ("dp", "hid"), split_axis=0, concat_axis=0, tiled=True
    )
    return moved.reshape(rows.shape)


def combined(position, slots_refs):
    tokens = position.shape[1]
    total, begin = None, 0
    for slots_ref in slots_refs:
        count = slots_ref.shape[0]
        part = min(count, 2 * LANES)
        row = place_of((part, tokens), 0)
        for at in range(0, count, part):
            chosen = to_low((position - (begin + at) == row).astype(jnp.float32))
            found = dot_left(chosen, slots_ref[at : at + part])
            total = found if total is None else total + found
        begin += count
    return total


def combine_kernel(mixture, plan_ref, gate_ref, base_ref, *refs):
    *slots_refs, expert_out_ref, out_ref = refs
    total = combined(plan_ref[2 * mixture + 1 : 2 * mixture + 2], slots_refs)
    expert_out_ref[...] = total
    out_ref[...] = base_ref[...] + 0.5 * gate_ref[...] * total


def combine_step(mixture, plan, gate, base, filled):
    return whole_call(
        functools.partial(combine_kernel, mixture),
        [shaped(base.shape, jnp.float32)] * 2,
        [],
        [plan, gate, base, *filled],
        500_000_000,
    )


def expert_grad_kernel(splits, place_ref, *refs):
    forward, backward, out_ref = refs[:splits], refs[splits : 2 * splits], refs[-1]
    share = forward[0].shape[0] // 2
    for step in range(splits):
        owner = (place_ref[0] + step) % splits
        out_ref[owner, 0] = dot_left(forward[step][:share], backward[step][share:])
        out_ref[owner, 1] = dot_left(backward[step][:share], forward[step][share:])


def last_grad_kernel(
    splits,
    place_ref,
    rows_ref,
    rows_grad_ref,
    hidden_ref,
    active_grad_ref,
    later_ref,
    out_ref,
    square_ref,
    *refs,
):
    sent_refs, all_ref = refs[:-1], refs[-1]
    all_ref[0] = dot_left(rows_ref[...], active_grad_ref[...])
    all_ref[1] = dot_left(rows_grad_ref[...], hidden_ref[...])
    out_ref[...] = all_ref[:2]
    all_ref[2:] = later_ref[...]
    square = jnp.zeros((1, D), jnp.float32)
    for part in range(4):
        square = square + jnp.sum(all_ref[part] * all_ref[part], 0, keepdims=True)
    square_ref[...] = square
    for step, sent_ref in enumerate(sent_refs):
        sent_ref[...] = to_low(all_ref[(place_ref[0] + step) % 4])


def expert_grads(place, forward, backward):
    rows, width = forward[0].shape
    splits = len(forward)
    return whole_call(
        functools.partial(expert_grad_kernel, splits),
        [shaped((splits, 2, width, width), jnp.float32)],
        [place],
        [*forward, *backward],
        2 * rows * width * width * splits,
    )[0]


def last_expert_grads(place, rows, rows_grad, hidden, active_grad, later):
    splits, width = lax.axis_size("hid"), later.shape[-1]
    out, square, *sent = whole_call(
        functools.partial(last_grad_kernel, splits),
        [shaped(later.shape, jnp.float32), shaped((1, width), jnp.float32)]
        + [shaped((width, width), jnp.bfloat16)] * splits,
        [place],
        [rows, rows_grad, hidden, active_grad, later],
        4 * rows.shape[0] * width * width,
        [pltpu.VMEM((4, width, width), jnp.float32)],
    )
    return out, square, sent


def attention_forward_kernel(
    gain_row, length_ref, values_ref, turned_ref, weight_ref, branch_ref, out_ref, parts_ref, log_ref, context_ref
):
    values = values_ref[...]
    tokens = values.shape[0]
    normed, _, _ = norm_forward(values, turned_ref[gain_row : gain_row + 1])
    low_normed = to_low(normed)
    for part in range(3):
        parts_ref[part] = to_low(dot_low(low_normed, weight_ref[part]))
    seen = place_of((tokens, tokens), 1) < length_ref[0]
    lane = place_of((tokens, LANES), 1)
    logs = jnp.zeros((tokens, LANES), jnp.float32)
    pair = LANES // HEAD_DIM
    for first in range(0, HEADS, pair):
        columns = slice(first * HEAD_DIM, (first + pair) * HEAD_DIM)
        queries, keys, contents = (parts_ref[part, :, columns] for part in range(3))
        context = jnp.zeros((tokens, LANES), jnp.float32)
        for head in range(pair):
            mine = lane // HEAD_DIM == head
            scores = dot_right(jnp.where(mine, queries, jnp.zeros_like(queries)), keys)
            scores = jnp.where(seen, scores * HEAD_DIM ** (-0.5), -1e30)
            top = jnp.max(scores, 1, keepdims=True)
            raised = jnp.exp(scores - top)
            total = jnp.sum(raised, 1, keepdims=True)
            mixed = dot_low(to_low(raised * (1.0 / total)), contents)
            context = jnp.where(mine, mixed, context)
            logs = jnp.where(lane == first + head, top + jnp.log(total), logs)
        context_ref[:, columns] = to_low(context)
    log_ref[...] = logs
    out_ref[...] = values + dot_low(context_ref[...], branch_ref[0])


def attention_forward(length, values, turned, dense, gain_row):
    tokens = values.shape[0]
    return whole_call(
        functools.partial(attention_forward_kernel, gain_row),
        [
            shaped((tokens, D), jnp.float32),
            shaped((3, tokens, D), jnp.bfloat16),
            shaped((tokens, LANES), jnp.float32),
            shaped((tokens, D), jnp.bfloat16),
        ],
        [length],
        [values, turned, (dense, (3, D, D), (0, 0, 0)), (dense, (1, D, D), (3, 0, 0))],
        4_000_000_000,
    )


def attention_backward_kernel(
    gain_row,
    length_ref,
    place_ref,
    grad_ref,
    values_ref,
    turned_ref,
    weight_ref,
    branch_ref,
    parts_ref,
    log_ref,
    context_ref,
    conv_out_ref,
    linear_ref,
    gating_ref,
    out_ref,
    gain_grad_ref,
    weight_grad_ref,
    low_ref,
    project_ref,
):
    grad = grad_ref[...]
    tokens = grad.shape[0]
    low_grad = to_low(grad)
    low_ref[...] = low_grad
    context_grad = to_low(dot_right(low_grad, branch_ref[0]))
    seen = place_of((tokens, tokens), 1) < length_ref[0]
    lane = place_of((tokens, LANES), 1)
    pair = LANES // HEAD_DIM
    scale = HEAD_DIM ** (-0.5)
    for first in range(0, HEADS, pair):
        columns = slice(first * HEAD_DIM, (first + pair) * HEAD_DIM)
        queries, keys, contents = (parts_ref[part, :, columns] for part in range(3))
        mixed_grad = context_grad[:, columns]
        grads = [jnp.zeros((tokens, LANES), jnp.float32)] * 3
        for head in range(pair):
            mine = lane // HEAD_DIM == head
            none = jnp.zeros_like(queries)
            scores = dot_right(jnp.where(mine, queries, none), keys) * scale
            log_total = jnp.sum(
                jnp.where(lane == first + head, log_ref[...], 0.0), 1, keepdims=True
            )
            weights = jnp.where(seen, jnp.exp(jnp.where(seen, scores, -1e30) - log_total), 0.0)
            weight_grad = dot_right(jnp.where(mine, mixed_grad, none), contents)
            score_grad = to_low(
                weights * (weight_grad - jnp.sum(weight_grad * weights, 1, keepdims=True))
            )
            found = (
                dot_low(score_grad, keys) * scale,
                dot_left(score_grad, queries) * scale,
                dot_left(to_low(weights), mixed_grad),
            )
            grads = [jnp.where(mine, new, old) for new, old in zip(found, grads)]
        for part in range(3):
            project_ref[part, :, columns] = to_low(grads[part])
    gain = turned_ref[gain_row : gain_row + 1]
    normed, unit, inverse = norm_forward(values_ref[...], gain)
    low_normed = to_low(normed)
    normed_grad = sum(dot_right(project_ref[part], weight_ref[part]) for part in range(3))
    back, gain_grad_ref[...] = norm_backward(normed_grad, unit, inverse, gain)
    out_ref[...] = grad + back
    width = weight_grad_ref.shape[1] // 7
    own = pl.ds(pl.multiple_of(place_ref[0] * width, width), width)
    for part in range(3):
        weight_grad_ref[:, part * width : (part + 1) * width] = to_low(
            dot_left(low_normed, project_ref[part, :, own])
        )
    weight_grad_ref[:, 3 * width : 4 * width] = to_low(dot_left(context_ref[...], low_ref[:, own]))
    for number, other_ref in enumerate((conv_out_ref, linear_ref, gating_ref)):
        weight_grad_ref[:, (4 + number) * width : (5 + number) * width] = to_low(other_ref[...])


def attention_backward(length, place, grad, values, turned, dense, kept, others, gain_row):
    tokens = values.shape[0]
    splits = lax.axis_size("hid")
    return whole_call(
        functools.partial(attention_backward_kernel, gain_row),
        [
            shaped((tokens, D), jnp.float32),
            shaped((1, D), jnp.float32),
            shaped((D, 7 * D // splits), jnp.bfloat16),
        ],
        [length, place],
        [
            grad,
            values,
            turned,
            (dense, (3, D, D), (0, 0, 0)),
            (dense, (1, D, D), (3, 0, 0)),
            *kept,
            *others,
        ],
        9_000_000_000,
        [pltpu.VMEM((tokens, D), jnp.bfloat16), pltpu.VMEM((3, tokens, D), jnp.bfloat16)],
        60,
    )


def senone_kernel(
    gain_row, splits, length_ref, place_ref, values_ref, turned_ref, targets_ref, *refs
):
    low_ref, loss_ref, sent_ref = refs[-3 - splits], refs[-2 - splits], refs[-1 - splits]
    logit_refs = refs[-splits:]
    table_ref = refs[0]
    count = table_ref.shape[0]
    rows = values_ref.shape[0] // splits
    place = place_ref[0]
    gain = turned_ref[gain_row : gain_row + 1]
    normed, _, _ = norm_forward(values_ref[...], gain)
    low_ref[...] = to_low(normed)
    own = pl.ds(pl.multiple_of(place * rows, rows), rows)
    normed, unit, inverse = norm_forward(values_ref[own], gain)
    own_rows, targets = to_low(normed), targets_ref[own]
    width = table_ref.shape[2]
    logits, picked = [], []
    for number in range(count):
        begin = (place + splits - number) % splits * width
        logits.append(dot_low(own_rows, table_ref[number]))
        picked.append(place_of((rows, width), 1) + begin == targets)
    top = functools.reduce(
        jnp.maximum, [jnp.max(part, 1, keepdims=True) for part in logits]
    )
    total = sum(jnp.sum(jnp.exp(part - top), 1, keepdims=True) for part in logits)
    target = sum(
        jnp.sum(jnp.where(chosen, part, 0.0), 1, keepdims=True)
        for chosen, part in zip(picked, logits)
    )
    log_total = top + jnp.log(total)
    valid = (place_of((rows, 1), 0) + place * rows < length_ref[0]).astype(jnp.float32)
    loss_ref[...] = jnp.sum(valid * (log_total - target), 0, keepdims=True)
    normed_grad = jnp.zeros((rows, D), jnp.float32)
    for number, (chosen, part) in enumerate(zip(picked, logits)):
        logit_grad = to_low(
            valid * (jnp.exp(part - log_total) - chosen.astype(jnp.float32))
        )
        logit_refs[(splits - number) % splits][...] = logit_grad
        normed_grad = normed_grad + dot_right(logit_grad, table_ref[number])
    own_grad, gain_grad = norm_backward(normed_grad, unit, inverse, gain)
    high, low = two_parts(gain_grad)
    extra = place_of((sent_ref.shape[0] - rows, D), 0)
    sent_ref[:rows] = to_low(own_grad)
    sent_ref[rows:] = to_low(
        jnp.where(
            extra == 0,
            high.astype(jnp.float32),
            jnp.where(extra == 1, low.astype(jnp.float32), 0.0),
        )
    )


def senone_step(length, place, values, turned, targets, tables, gain_row):
    splits, tokens = lax.axis_size("hid"), values.shape[0]
    rows = tokens // splits
    return whole_call(
        functools.partial(senone_kernel, gain_row, splits),
        [
            shaped((tokens, D), jnp.bfloat16),
            shaped((1, 1), jnp.float32),
            shaped((rows + 16, D), jnp.bfloat16),
        ]
        + [shaped((rows, tables.shape[2]), jnp.bfloat16)] * splits,
        [length, place],
        [values, turned, targets, tables],
        1_100_000_000,
        room=60,
    )


def table_grad_kernel(place_ref, low_ref, *refs):
    blocks, out_ref = refs[:-1], refs[-1]
    splits, rows = len(blocks), blocks[0].shape[0]
    total = None
    for step, block in enumerate(blocks):
        begin = pl.multiple_of((place_ref[0] + splits - step) % splits * rows, rows)
        part = dot_left(low_ref[pl.ds(begin, rows)], block[...])
        total = part if total is None else total + part
    out_ref[...] = to_low(total)


def table_grad(place, low_normed, blocks):
    return whole_call(
        table_grad_kernel,
        [shaped((D, blocks[0].shape[1]), jnp.bfloat16)],
        [place],
        [low_normed, *blocks],
        600_000_000,
    )[0]


def send_back(mixture, grad, plan_ref, gate_ref, rows_ref):
    index = plan_ref[2 * mixture : 2 * mixture + 1]
    chosen = (place_of((rows_ref.shape[0], grad.shape[0]), 0) == index).astype(jnp.float32)
    rows_ref[...] = to_low(dot_low(to_low(chosen), to_low(gate_ref[...] * (0.5 * grad))))


def assemble_kernel(mixture, place_ref, plan_ref, gate_ref, *refs):
    blocks, grad_ref, gain_grad_ref, rows_ref = refs[:-3], refs[-3], refs[-2], refs[-1]
    splits = len(blocks)
    rows = grad_ref.shape[0] // splits
    for step, block in enumerate(blocks):
        begin = pl.multiple_of((place_ref[0] + splits - step) % splits * rows, rows)
        grad_ref[pl.ds(begin, rows)] = block[:rows].astype(jnp.float32)
    gain_grad_ref[...] = sum(
        jnp.sum(block[rows:].astype(jnp.float32), 0, keepdims=True) for block in blocks
    )
    send_back(mixture, grad_ref[...], plan_ref, gate_ref, rows_ref)


def assemble_step(mixture, place, plan, gate, blocks, wide_rows):
    tokens = gate.shape[0]
    return whole_call(
        functools.partial(assemble_kernel, mixture),
        [
            shaped((tokens, D), jnp.float32),
            shaped((1, D), jnp.float32),
            shaped((wide_rows, D), jnp.bfloat16),
        ],
        [place],
        [plan, gate, *blocks],
        200_000_000,
    )


def send_back_kernel(mixture, plan_ref, gate_ref, grad_ref, rows_ref):
    send_back(mixture, grad_ref[...], plan_ref, gate_ref, rows_ref)


def send_back_step(mixture, plan, gate, grad, wide_rows):
    return whole_call(
        functools.partial(send_back_kernel, mixture),
        [shaped((wide_rows, D), jnp.bfloat16)],
        [],
        [plan, gate, grad],
        200_000_000,
    )[0]


def gate_backward_kernel(
    mixture,
    experts,
    gain_row,
    grad_ref,
    expert_out_ref,
    gate_ref,
    chances_ref,
    route_ref,
    values_ref,
    small_ref,
    turned_ref,
    side_ref,
    router_grad_ref,
):
    column = place_of((values_ref.shape[0], LANES), 1) - mixture * experts
    onehot = (column == route_ref[mixture]).astype(jnp.float32)
    gate_grad = jnp.sum(0.5 * grad_ref[...] * expert_out_ref[...], 1, keepdims=True)
    logit_grad = (gate_ref[...] * gate_grad) * (onehot - chances_ref[...])
    normed, _, _ = norm_forward(values_ref[...], turned_ref[gain_row : gain_row + 1])
    router_grad_ref[...] = exact_dot(normed, logit_grad, ((0,), (0,)))
    side_ref[...] = exact_dot(logit_grad, small_ref[:, LANES:], ((1,), (1,)))


def gate_backward(mixture, gain_row, grad, expert_out, gate, chances, routes, values, small, turned):
    return whole_call(
        functools.partial(gate_backward_kernel, mixture, lax.axis_size("dp"), gain_row),
        [shaped(grad.shape, jnp.float32), shaped((D, LANES), jnp.float32)],
        [],
        [grad, expert_out, gate, chances, routes, values, small, turned],
        800_000_000,
    )


def combine_backward_kernel(
    plan_row,
    gain_row,
    plan_ref,
    grad_ref,
    side_ref,
    values_ref,
    turned_ref,
    *refs,
):
    *slots_refs, out_ref, gain_grad_ref = refs
    gain = turned_ref[gain_row : gain_row + 1]
    normed_grad = side_ref[...] + combined(
        plan_ref[plan_row : plan_row + 1], slots_refs
    )
    _, unit, inverse = norm_forward(values_ref[...], gain)
    back, gain_grad_ref[...] = norm_backward(normed_grad, unit, inverse, gain)
    out_ref[...] = grad_ref[...] + back


def combine_backward(plan_row, gain_row, plan, grad, side, values, turned, filled):
    return whole_call(
        functools.partial(combine_backward_kernel, plan_row, gain_row),
        [shaped(grad.shape, jnp.float32), shaped((1, D), jnp.float32)],
        [],
        [plan, grad, side, values, turned, *filled],
        500_000_000,
    )


def pack_grads_kernel(
    owners, grad_ref, features_ref, router_one_ref, router_two_ref, taps_ref, *refs
):
    gain_refs, out_ref, turn_ref = refs[:-2], refs[-2], refs[-1]
    bands, taps = features_ref.shape[0], taps_ref.shape[0]
    turn_ref[...] = jnp.zeros(turn_ref.shape, jnp.float32)
    turn_ref[2 * owners : 2 * owners + taps] = taps_ref[...]
    for number, gain_ref in enumerate(gain_refs):
        at = 2 * owners + taps + number
        turn_ref[at : at + 1] = gain_ref[...]
    out_ref[:, :LANES] = jnp.zeros((D, LANES), jnp.bfloat16)
    out_ref[:, :bands] = to_low(
        lax.dot_general(
            to_low(grad_ref[...]),
            features_ref[...],
            (((0,), (1,)), ((), ())),
            preferred_element_type=jnp.float32,
        )
    )
    out_ref[:, LANES : 2 * LANES] = to_low(
        turn_ref[...].T + router_one_ref[...] + router_two_ref[...]
    )


def pack_grads(grad, features_turned, router_one, router_two, taps_grad, gain_grads):
    return whole_call(
        functools.partial(pack_grads_kernel, lax.axis_size("dp")),
        [shaped((D, 2 * LANES), jnp.bfloat16)],
        [],
        [grad, features_turned, router_one, router_two, taps_grad, *gain_grads],
        60_000_000,
        [pltpu.VMEM((LANES, D), jnp.float32)],
    )[0]


def shares_kernel(place_ref, length_ref, moved_ref, *refs):
    *part_refs, square_ref, loss_ref, share_ref, out_ref = refs
    share = jnp.zeros(share_ref.shape, jnp.float32)
    for owner in range(moved_ref.shape[0]):
        share = share + moved_ref[owner].astype(jnp.float32)
    share_ref[...] = share
    leading = place_ref[0] == 0
    square = jnp.where(leading, jnp.sum(share * share), 0.0) + jnp.sum(square_ref[...])
    for part_ref in part_refs:
        square = square + jnp.sum(part_ref[...] * part_ref[...])
    count = jnp.where(leading, length_ref[0], 0).astype(jnp.float32)
    lane = place_of((1, LANES), 1)
    row = jnp.where(
        lane == 0, square, jnp.where(lane == 1, count, jnp.where(lane == 2, loss_ref[...], 0.0))
    )
    for device in range(out_ref.shape[0]):
        out_ref[device] = row


def shares_step(place, length, moved, parts, squares, loss):
    devices = lax.axis_size("dp") * lax.axis_size("hid")
    return whole_call(
        shares_kernel,
        [shaped(moved.shape[1:], jnp.float32), shaped((devices, 1, LANES), jnp.float32)],
        [place, length],
        [moved, *parts, squares, loss],
        1_000_000,
    )


def summed(moved):
    owners = lax.axis_size("dp")
    return jnp.sum(moved.reshape(owners, D // owners, -1).astype(jnp.float32), 0)


def totals_of(ref):
    rows = jnp.sum(ref[...], 0)
    lane = place_of(rows.shape, 1)
    square, count, loss = (jnp.sum(jnp.where(lane == part, rows, 0.0)) for part in range(3))
    norm = jnp.sqrt(square) / count
    return count, loss, norm, jnp.minimum(1.0, clip_limit / (norm + 1e-06)) / count


def orthogonal_kernel(pieces, experts, place_ref, totals_ref, *refs):
    momentum_refs, grad_refs = refs[:pieces], refs[pieces : 2 * pieces]
    out_refs, matrix_ref = refs[2 * pieces : 3 * pieces], refs[3 * pieces]
    _, _, _, factor = totals_of(totals_ref)
    gram = jnp.zeros((D, D), jnp.float32)
    for piece in range(pieces):
        current = to_low(
            muon_beta * momentum_refs[piece][...].astype(jnp.float32)
            + factor * grad_refs[piece][...].astype(jnp.float32)
        )
        matrix_ref[piece] = current
        gram = gram + dot_right(current, current)
    row, column = place_of((D, D), 0), place_of((D, D), 1)
    square = jnp.sum(jnp.where(row == column, gram, 0.0))
    inverse = 1.0 / (jnp.sqrt(square) + 1e-07)
    gram = gram * (inverse * inverse)
    identity = jnp.where(row == column, newton_first, 0.0)
    total = None
    for turn in range(5):
        parts = two_parts(gram)
        poly = identity + newton_second * gram + newton_third * close_dot(parts, parts)
        poly_parts = two_parts(poly)
        total = poly if total is None else close_dot(poly_parts, two_parts(total))
        if turn < 4:
            gram = close_dot(poly_parts, two_parts(close_dot(poly_parts, parts)))
    kind_scale = jnp.where(
        place_ref[0] % 2 == 0,
        D ** (-0.5) * muon_rate * FF**0.5,
        3 * experts * FF ** (-0.5) * muon_rate * FF**0.5,
    )
    total_parts = two_parts(total * (inverse * kind_scale))
    for piece in range(pieces):
        out_refs[piece][...] = to_low(
            sum(dot_low(part, matrix_ref[piece]) for part in total_parts)
        )


def orthogonal(place, totals, momentum, grads):
    pieces = len(momentum)
    return whole_call(
        functools.partial(orthogonal_kernel, pieces, lax.axis_size("dp")),
        [shaped((D, D), jnp.bfloat16)] * pieces,
        [place],
        [totals, *momentum, *grads],
        17_000_000_000,
        [pltpu.VMEM((pieces, D, D), jnp.bfloat16)],
        60,
    )


def momentum_kernel(totals_ref, momentum_ref, one_ref, two_ref, out_ref):
    _, _, _, factor = totals_of(totals_ref)
    first = pl.program_id(0) < 2
    grad = jnp.where(first, one_ref[0], two_ref[0])
    out_ref[0] = muon_beta * momentum_ref[0] + factor * grad


def momentum_update(totals, momentum, grads_one, grads_two):
    block = (1,) + momentum.shape[1:]
    return pl.pallas_call(
        momentum_kernel,
        grid=(4,),
        out_shape=shaped(momentum.shape, jnp.float32),
        in_specs=[
            pl.BlockSpec(totals.shape, lambda step: (0, 0, 0)),
            pl.BlockSpec(block, lambda step: (step, 0, 0)),
            pl.BlockSpec(block, lambda step: (jnp.minimum(step, 1), 0, 0)),
            pl.BlockSpec(block, lambda step: (jnp.maximum(step - 2, 0), 0, 0)),
        ],
        out_specs=pl.BlockSpec(block, lambda step: (step, 0, 0)),
        compiler_params=pltpu.CompilerParams(vmem_limit_bytes=32 * 1024 * 1024),
        cost_estimate=pl.CostEstimate(
            flops=3_000_000, bytes_accessed=12_000_000, transcendentals=0
        ),
    )(totals, momentum, grads_one, grads_two)


def update_kernel(place_ref, weight_ref, *refs):
    out_ref, turn = refs[-1], pl.program_id(0)
    for step, update_ref in enumerate(refs[:-1]):

        @pl.when(turn == step)
        def _():
            out_ref[0] = (1.0 - muon_decay) * weight_ref[0] - update_ref[...].astype(jnp.float32)


def expert_update(place, weights, updates):
    count = weights.shape[0]

    def turned(step, place_ref):
        return ((place_ref[0] + step) % count, 0, 0)

    block = (1,) + weights.shape[1:]
    return pl.pallas_call(
        update_kernel,
        out_shape=jax.ShapeDtypeStruct(weights.shape, jnp.float32),
        grid_spec=pltpu.PrefetchScalarGridSpec(
            num_scalar_prefetch=1,
            grid=(count,),
            in_specs=[pl.BlockSpec(block, turned)]
            + [pl.BlockSpec(update.shape, lambda step, place_ref: (0, 0)) for update in updates],
            out_specs=pl.BlockSpec(block, turned),
        ),
        compiler_params=pltpu.CompilerParams(vmem_limit_bytes=32 * 1024 * 1024),
        cost_estimate=pl.CostEstimate(
            flops=3_000_000, bytes_accessed=10_000_000, transcendentals=0
        ),
    )(place, weights, *updates)


def adam_update(weight, grad, first, second, rate, decay):
    first_new = beta_one * first + (1.0 - beta_one) * grad
    second_new = beta_two * second + (1.0 - beta_two) * grad * grad
    corrected = (
        first_new
        / (1.0 - beta_one**STEP)
        / (jnp.sqrt(second_new / (1.0 - beta_two**STEP)) + adam_epsilon)
    )
    return (first_new, second_new, weight - rate * (corrected + decay * weight))


def adam_kernel(owners, splits, place_ref, totals_ref, share_ref, senone_ref, *refs):
    blocks, states = refs[:splits], refs[splits : splits + 24]
    outs, scalars_ref = refs[splits + 24 : splits + 48], refs[splits + 48]
    turn_ref, gather_ref = refs[splits + 49 :]
    count, loss, norm, factor = totals_of(totals_ref)
    lane = place_of((1, LANES), 1)
    scalars_ref[...] = jnp.where(
        lane == 0, loss, jnp.where(lane == 1, count, jnp.where(lane == 2, norm, 0.0))
    )
    width = blocks[0].shape[1] // 7
    for step, block in enumerate(blocks):
        begin = pl.multiple_of((place_ref[0] + splits - step) % splits * width, width)
        for part in range(7):
            gather_ref[part, :, pl.ds(begin, width)] = block[:, part * width : (part + 1) * width]
    own = share_ref.shape[0]
    bands = states[0].shape[1]
    taps, gains = states[4].shape[0], states[7].shape[0]
    turn_ref[...] = jnp.zeros(turn_ref.shape, jnp.float32)
    turn_ref[:own] = share_ref[:, LANES : 2 * LANES]
    turned = turn_ref[...].T
    begin = 2 * owners

    def apply(number, at, grad, rate=adam_rate, decay=weight_decay):
        first, second, weight = (states[number + 8 * part] for part in (1, 2, 0))
        found = adam_update(weight[at], grad * factor, first[at], second[at], rate, decay)
        for ref, value in zip(outs[3 * number : 3 * number + 3], found):
            ref[at] = value

    everything = (slice(None), slice(None))
    apply(0, everything, share_ref[:, :bands])
    for part in range(3):
        apply(1, (slice(None), slice(part * D, (part + 1) * D)), gather_ref[part])
    for part in range(2):
        apply(2, (part,), gather_ref[3 + part])
        apply(3, (slice(None), slice(part * D, (part + 1) * D)), gather_ref[5 + part])
        apply(
            5,
            (part,),
            share_ref[:, LANES + part * owners : LANES + (part + 1) * owners],
        )
    apply(4, everything, turned[begin : begin + taps, :own])
    apply(6, everything, senone_ref[...])
    apply(7, everything, turned[begin + taps : begin + taps + gains, :own], gain_rate, 0.0)


def adam_step(place, totals, share, senone_share, blocks, weights, firsts, seconds):
    rows, splits = share.shape[0], len(blocks)
    outs = [shaped(part.shape, jnp.float32) for part in weights for _ in range(3)]
    return whole_call(
        functools.partial(adam_kernel, lax.axis_size("dp"), splits),
        outs + [shaped((1, LANES), jnp.float32)],
        [place],
        [totals, share, senone_share, *blocks, *weights, *firsts, *seconds],
        4_000_000,
        [
            pltpu.VMEM((LANES, LANES), jnp.float32),
            pltpu.VMEM((7, rows, D), jnp.float32),
        ],
    )


def convolution_forward(values, gains, weight_in, depth, weight_out, valid):
    tokens = values.shape[0]
    normed, unit, inverse = norm_forward(values, gains[2])
    low_normed = to_low(normed)
    linear = dot_low(low_normed, weight_in[0])
    gating = jax.nn.sigmoid(dot_low(low_normed, weight_in[1]))
    mixed = linear * gating * valid[:, None]
    reach = (depth.shape[0] - 1) // 2
    padded = jnp.pad(mixed, ((reach, reach), (0, 0)))
    deep = jnp.zeros_like(mixed)
    for offset in range(depth.shape[0]):
        deep = deep + depth[offset] * padded[offset : offset + tokens]
    count = jnp.sum(valid)
    mask = valid[:, None]
    mean = jnp.sum(mask * deep, 0) / count
    spread = jnp.sum(mask * deep * deep, 0) / count - mean * mean
    scale = lax.rsqrt(spread + 1e-05)
    unit_batch = (deep - mean) * scale
    shifted = unit_batch * gains[5] + gains[6]
    activated = to_low(jax.nn.silu(shifted))
    kept = (
        unit,
        inverse,
        low_normed,
        linear,
        gating,
        padded,
        scale,
        unit_batch,
        shifted,
        activated,
    )
    return (values + dot_low(activated, weight_out), kept)


def convolution_backward(grad, gains, weight_in, depth, weight_out, valid, kept):
    unit, inverse, low_normed, linear, gating, padded, scale, unit_batch, shifted, activated = kept
    tokens = grad.shape[0]
    low_grad = to_low(grad)
    out_grad = dot_left(activated, own_part(low_grad, 1))
    shifted_grad = dot_right(low_grad, weight_out) * silu_slope(shifted)
    gamma_grad = jnp.sum(shifted_grad * unit_batch, 0)
    beta_grad = jnp.sum(shifted_grad, 0)
    unit_grad = shifted_grad * gains[5]
    count = jnp.sum(valid)
    mask = valid[:, None]
    first_sum = jnp.sum(mask * unit_grad, 0) / count
    second_sum = jnp.sum(mask * unit_grad * unit_batch, 0) / count
    deep_grad = scale * (unit_grad - mask * (first_sum + unit_batch * second_sum))
    reach = (depth.shape[0] - 1) // 2
    padded_grad = jnp.pad(deep_grad, ((reach, reach), (0, 0)))
    mixed_grad = jnp.zeros_like(deep_grad)
    depth_rows = []
    for offset in range(depth.shape[0]):
        begin = 2 * reach - offset
        mixed_grad = mixed_grad + depth[offset] * padded_grad[begin : begin + tokens]
        depth_rows.append(jnp.sum(deep_grad * padded[offset : offset + tokens], 0))
    mixed_grad = mixed_grad * mask
    project_grad = [
        to_low(mixed_grad * gating),
        to_low(mixed_grad * linear * gating * (1.0 - gating)),
    ]
    in_grad = [dot_left(low_normed, own_part(part, 1)) for part in project_grad]
    normed_grad = sum(dot_right(part, weight_in[place]) for place, part in enumerate(project_grad))
    values_grad, gain_grad = norm_backward(normed_grad, unit, inverse, gains[2])
    return (
        grad + values_grad,
        gain_grad,
        gamma_grad[None],
        beta_grad[None],
        in_grad,
        jnp.stack(depth_rows),
        out_grad,
    )


def on_device(
    features,
    lengths,
    routes,
    alignments,
    input_weight,
    attention_in,
    branch_out,
    pointwise_in,
    depthwise,
    router,
    senone_table,
    norm_scales,
    expert_weights,
    input_first,
    input_second,
    attention_first,
    attention_second,
    branch_first,
    branch_second,
    pointwise_first,
    pointwise_second,
    depthwise_first,
    depthwise_second,
    router_first,
    router_second,
    senone_first,
    senone_second,
    scales_first,
    scales_second,
    expert_momentum,
):
    owners, splits = lax.axis_size("dp"), lax.axis_size("hid")
    tokens = features.shape[0]
    taps, gains = depthwise.shape[0], norm_scales.shape[0]
    place = lax.axis_index("hid")
    place_array = place[None].astype(jnp.int32)
    gain_begin = 2 * owners + taps
    share = 3 * tokens // (2 * owners) // splits
    wide = -(-share // 8) * 8
    slots, wide_rows = (share, wide), owners * wide

    low_one, low_two = to_low(expert_weights[0, :, 0]), to_low(expert_weights[1, :, 0])
    momentum_pieces = expert_momentum.reshape((2 * 2,) + expert_momentum.shape[3:])
    owned_momentum = spread(
        [to_low(momentum_pieces[(place + step) % splits]) for step in range(splits)]
    )
    small = pack_small(input_weight.T, router, depthwise, norm_scales)
    small = exchange_rows(small.reshape(owners * small.shape[1], -1))
    small, owned_momentum[2] = together(small, owned_momentum[2])
    dense = lax.all_gather(
        pack_dense(attention_in, branch_out, pointwise_in), "dp", axis=1, tiled=True
    )
    valid = (jnp.arange(tokens, dtype=jnp.int32) < lengths[0]).astype(jnp.float32)
    plan = plan_slots(place_array, routes[:, :, 0], share, wide)
    targets = alignments[:, None]
    features_turned = features.T

    start, turned, rows, gate_one, chances_one = start_step(
        small, features_turned, plan, routes, gain_begin, owners * share * splits
    )
    depth_full = turned[2 * owners : gain_begin]
    scales_full = turned[gain_begin : gain_begin + gains]
    rows_one, owned_momentum[1], owned_momentum[3] = together(
        exchange_rows(rows), owned_momentum[1], owned_momentum[3]
    )
    returned, senone_low = together(
        split_forward(rows_one, low_one, slots), to_low(senone_table)
    )
    moved, *senone_rows = together(exchange_all(returned, wide), *gather_near(senone_low))
    tables = lax.all_gather(jnp.stack(senone_rows), "dp", axis=1, tiled=True)
    expert_out_one, first = combine_step(0, plan, gate_one, start, gather_sums(moved, slots))

    first, low_two = together(first, low_two)
    weights_two = gather_near(low_two)
    second, *kept_attend = attention_forward(lengths, first, turned, dense, gain_begin + 1)
    third, kept_convolve = convolution_forward(
        second, scales_full, dense[5:7], depth_full, dense[4], valid
    )

    rows, gate_two, chances_two = dispatch_step(
        1, third, small, turned, plan, routes, gain_begin + 3, wide_rows
    )
    forward_two, returned = expert_forward(place_array, exchange_rows(rows), weights_two, slots)
    filled = exchange_all(returned, wide)
    expert_out_two, fourth = combine_step(1, plan, gate_two, third, [filled])

    low_normed, loss_local, sent, *logit_grad = senone_step(
        lengths, place_array, fourth, turned, targets, tables, gain_begin + 4
    )
    grad, gain_five, rows = assemble_step(
        1, place_array, plan, gate_two, gather_near(sent), wide_rows
    )

    rows_grad = exchange_rows(rows)
    side, router_two = gate_backward(
        1,
        gain_begin + 3,
        grad,
        expert_out_two,
        gate_two,
        chances_two,
        routes,
        third,
        small,
        turned,
    )
    logit_grad = spread(logit_grad)
    rows_grad, side, *logit_grad[1:] = together(rows_grad, side, *logit_grad[1:])
    backward_two, returned = expert_backward(
        place_array, forward_two[0], rows_grad, weights_two, slots
    )
    filled = exchange_all(returned, wide)
    experts_two = lax.psum_scatter(
        expert_grads(place_array, forward_two, backward_two), "hid", scatter_dimension=0
    )
    grad, gain_four = combine_backward(
        3, gain_begin + 3, plan, grad, side, third, turned, [filled]
    )
    grad, gain_three, gamma_grad, beta_grad, pointwise_grad, depth_grad, conv_out_grad = (
        convolution_backward(
            grad, scales_full, dense[5:7], depth_full, dense[4], valid, kept_convolve
        )
    )
    grad, gain_two, attend_grad = attention_backward(
        lengths,
        place_array,
        grad,
        first,
        turned,
        dense,
        kept_attend,
        [conv_out_grad] + pointwise_grad,
        gain_begin + 1,
    )

    rows_grad = exchange_rows(
        send_back_step(0, plan, gate_one, grad, owners * share * splits)
    )
    hidden, active_grad, returned = split_backward(rows_one, rows_grad, low_one, slots)
    moved = exchange_all(returned, wide)
    side, router_one = gate_backward(
        0, gain_begin, grad, expert_out_one, gate_one, chances_one, routes, start, small, turned
    )
    experts_one, squares, sent = last_expert_grads(
        place_array, rows_one, rows_grad, hidden, active_grad, experts_two
    )
    senone_grad = table_grad(place_array, low_normed, logit_grad)
    early = jnp.concatenate([attend_grad, senone_grad], 1)
    moved, side, squares, sent, early = together(moved, side, squares, tuple(sent), early)
    early_moved = exchange_rows(early)
    filled = gather_sums(moved, slots)
    grad, gain_one = combine_backward(1, gain_begin, plan, grad, side, start, turned, filled)
    last = pack_grads(
        grad,
        features_turned,
        router_one,
        router_two,
        depth_grad,
        [gain_one, gain_two, gain_three, gain_four, gain_five, gamma_grad, beta_grad],
    )
    early_share = summed(early_moved)
    width = attend_grad.shape[1]
    early_share, senone_share = early_share[:, :width], early_share[:, width:]
    last, sent = together(last, sent)
    blocks = gather_near(early_share)
    owned_grad = spread(sent)
    moved = exchange_rows(last)
    last_share, totals = shares_step(
        place_array,
        lengths,
        moved.reshape(owners, D // owners, -1),
        [senone_share, early_share],
        squares,
        loss_local,
    )
    totals = lax.all_to_all(totals, ("dp", "hid"), split_axis=0, concat_axis=0, tiled=True)

    totals, blocks = together(totals, tuple(blocks))
    orth = orthogonal(place_array, totals, owned_momentum, owned_grad)
    returned = [orth[0]] + [shift(orth[step], -step) for step in range(1, splits)]
    momentum_new = momentum_update(totals, momentum_pieces, experts_one, experts_two)
    *updated, scalars = adam_step(
        place_array,
        totals,
        last_share,
        senone_share,
        blocks,
        [
            input_weight.T,
            attention_in,
            branch_out,
            pointwise_in,
            depthwise,
            router,
            senone_table,
            norm_scales,
        ],
        [
            input_first.T,
            attention_first,
            branch_first,
            pointwise_first,
            depthwise_first,
            router_first,
            senone_first,
            scales_first,
        ],
        [
            input_second.T,
            attention_second,
            branch_second,
            pointwise_second,
            depthwise_second,
            router_second,
            senone_second,
            scales_second,
        ],
    )
    experts_new = expert_update(
        place_array, expert_weights.reshape(momentum_pieces.shape), returned
    )
    return (
        scalars[0, 0],
        scalars[0, 1],
        scalars[0, 2],
        *[part.T for part in updated[:3]],
        *updated[3:],
        momentum_new.reshape(expert_momentum.shape),
        experts_new.reshape(expert_weights.shape),
    )


def solution(mesh):
    return jax.shard_map(
        on_device,
        mesh=mesh,
        in_specs=(
            P("dp", None),
            P("dp"),
            P(None, "dp", None),
            P("dp"),
            P(None, "dp"),
            P("dp", None),
            P(None, "dp", None),
            P("dp", None),
            P(None, "dp"),
            P(None, "dp", None),
            P("dp", "hid"),
            P(None, "dp"),
            P(None, None, "dp", None, "hid"),
            P(None, "dp"),
            P(None, "dp"),
            P("dp", None),
            P("dp", None),
            P(None, "dp", None),
            P(None, "dp", None),
            P("dp", None),
            P("dp", None),
            P(None, "dp"),
            P(None, "dp"),
            P(None, "dp", None),
            P(None, "dp", None),
            P("dp", "hid"),
            P("dp", "hid"),
            P(None, "dp"),
            P(None, "dp"),
            P(None, None, "dp", None, "hid"),
        ),
        out_specs=(
            P(),
            P(),
            P(),
            P(None, "dp"),
            P(None, "dp"),
            P(None, "dp"),
            P("dp", None),
            P("dp", None),
            P("dp", None),
            P(None, "dp", None),
            P(None, "dp", None),
            P(None, "dp", None),
            P("dp", None),
            P("dp", None),
            P("dp", None),
            P(None, "dp"),
            P(None, "dp"),
            P(None, "dp"),
            P(None, "dp", None),
            P(None, "dp", None),
            P(None, "dp", None),
            P("dp", "hid"),
            P("dp", "hid"),
            P("dp", "hid"),
            P(None, "dp"),
            P(None, "dp"),
            P(None, "dp"),
            P(None, None, "dp", None, "hid"),
            P(None, None, "dp", None, "hid"),
        ),
        check_vma=False,
    )
```

```python
import functools

import jax
import jax.numpy as jnp
from jax import lax
from jax.experimental import pallas as pl
from jax.experimental.pallas import tpu as pltpu
from jax.sharding import PartitionSpec as P

D = 512
HEADS = 8
HEAD_DIM = 64
FF = 2048
STEP = 10
LANES = 128


clip_limit = 0.02
beta_one = 0.9
beta_two = 0.999
adam_epsilon = 1e-08
adam_rate = 0.2
gain_rate = 0.6
weight_decay = 0.01
muon_beta = 0.95
muon_rate = 1.0
muon_decay = 0.01
newton_first = 3.4445
newton_second = -4.775
newton_third = 2.0315


def shift(values, step):
    size = lax.axis_size("hid")
    return lax.ppermute(values, "hid", [(i, (i + step) % size) for i in range(size)])


def gather_near(values):
    return [values] + [shift(values, step) for step in range(1, lax.axis_size("hid"))]


def together(*values):
    return lax.optimization_barrier(values)


def spread(pieces):
    return [pieces[0]] + [shift(pieces[step], step) for step in range(1, len(pieces))]


def own_part(values, axis):
    width = values.shape[axis] // lax.axis_size("hid")
    return lax.dynamic_slice_in_dim(values, lax.axis_index("hid") * width, width, axis)


def exchange_rows(values):
    owners = lax.axis_size("dp")
    shape = values.shape
    shaped_rows = values.reshape((owners, shape[0] // owners) + shape[1:])
    moved = lax.all_to_all(shaped_rows, "dp", split_axis=0, concat_axis=0, tiled=True)
    return moved.reshape(shape)


def to_low(values):
    return values.astype(jnp.bfloat16)


def dot_low(left, right):
    return jnp.dot(left, right, preferred_element_type=jnp.float32)


def dot_left(left, right):
    return lax.dot_general(
        left, right, (((0,), (0,)), ((), ())), preferred_element_type=jnp.float32
    )


def dot_right(left, right):
    return lax.dot_general(
        left, right, (((1,), (1,)), ((), ())), preferred_element_type=jnp.float32
    )


def exact_dot(left, right, dims=((1,), (0,))):
    return lax.dot_general(
        left,
        right,
        (dims, ((), ())),
        precision=lax.Precision.HIGHEST,
        preferred_element_type=jnp.float32,
    )


def two_parts(values):
    high = to_low(values)
    return high, to_low(values - high.astype(jnp.float32))


def close_dot(left, right):
    return dot_low(left[0], right[0]) + (dot_low(left[0], right[1]) + dot_low(left[1], right[0]))


def norm_forward(values, gain):
    centered = values - jnp.mean(values, -1, keepdims=True)
    inverse = lax.rsqrt(jnp.mean(centered * centered, -1, keepdims=True) + 1e-05)
    unit = centered * inverse
    return (unit * gain, unit, inverse)


def norm_backward(grad, unit, inverse, gain):
    scaled = grad * gain
    back = inverse * (
        scaled
        - jnp.mean(scaled, -1, keepdims=True)
        - unit * jnp.mean(scaled * unit, -1, keepdims=True)
    )
    return (back, jnp.sum(grad * unit, 0, keepdims=True))


def silu_slope(values):
    sigma = jax.nn.sigmoid(values)
    return sigma * (1.0 + values * (1.0 - sigma))


def shaped(shape, dtype):
    return jax.ShapeDtypeStruct(shape, dtype)


def place_of(shape, axis):
    return lax.broadcasted_iota(jnp.int32, shape, axis)


def whole_call(kernel, out_shapes, scalars, arrays, flops, scratch=(), room=48):
    parts = [
        part if isinstance(part, tuple) else (part, part.shape, (0,) * part.ndim)
        for part in arrays
    ]
    specs = [
        pl.BlockSpec(block, functools.partial(lambda fixed, step: fixed, at))
        for _, block, at in parts
    ]
    moved = sum(part.size * part.dtype.itemsize for part, _, _ in parts) + sum(
        part.size * part.dtype.itemsize for part in out_shapes
    )
    return pl.pallas_call(
        kernel,
        grid=(1,),
        out_shape=out_shapes,
        in_specs=[pl.BlockSpec(memory_space=pltpu.SMEM)] * len(scalars) + specs,
        out_specs=[
            pl.BlockSpec(part.shape, functools.partial(lambda rank, step: (0,) * rank, len(part.shape)))
            for part in out_shapes
        ],
        scratch_shapes=list(scratch),
        compiler_params=pltpu.CompilerParams(vmem_limit_bytes=room * 1024 * 1024),
        cost_estimate=pl.CostEstimate(flops=flops, bytes_accessed=moved, transcendentals=0),
    )(*scalars, *[part for part, _, _ in parts])


def pack_small_kernel(owners, input_ref, router_ref, depth_ref, gains_ref, out_ref, turn_ref):
    bands, taps, gains = input_ref.shape[1], depth_ref.shape[0], gains_ref.shape[0]
    width = input_ref.shape[0]
    turn_ref[...] = jnp.zeros(turn_ref.shape, jnp.float32)
    turn_ref[2 * owners : 2 * owners + taps, :width] = depth_ref[...]
    turn_ref[2 * owners + taps : 2 * owners + taps + gains, :width] = gains_ref[...]
    turned = turn_ref[...].T[:width]
    out_ref[...] = jnp.zeros(out_ref.shape, jnp.float32)
    for owner in range(owners):
        out_ref[owner, :, LANES:] = turned
        out_ref[owner, :, :bands] = input_ref[...]
        out_ref[owner, :, LANES : LANES + owners] = router_ref[0]
        out_ref[owner, :, LANES + owners : LANES + 2 * owners] = router_ref[1]


def pack_small(input_turned, router, depthwise, norm_scales):
    owners, width = lax.axis_size("dp"), input_turned.shape[0]
    return whole_call(
        functools.partial(pack_small_kernel, owners),
        [shaped((owners, width, 2 * LANES), jnp.float32)],
        [],
        [input_turned, router, depthwise, norm_scales],
        1000,
        [pltpu.VMEM((LANES, LANES), jnp.float32)],
    )[0]


def pack_dense_kernel(attention_ref, branch_ref, pointwise_ref, out_ref):
    for part in range(3):
        out_ref[part] = to_low(attention_ref[:, part * D : (part + 1) * D])
    for part in range(2):
        out_ref[3 + part] = to_low(branch_ref[part])
        out_ref[5 + part] = to_low(pointwise_ref[:, part * D : (part + 1) * D])


def pack_dense(attention_in, branch_out, pointwise_in):
    return whole_call(
        pack_dense_kernel,
        [shaped((7, attention_in.shape[0], D), jnp.bfloat16)],
        [],
        [attention_in, branch_out, pointwise_in],
        1000,
    )[0]


def plan_kernel(experts, splits, share, wide, place_ref, routes_ref, out_ref):
    tokens = routes_ref.shape[1]
    before = (place_of((tokens, tokens), 0) < place_of((tokens, tokens), 1)).astype(jnp.float32)
    for mixture in range(2):
        route = routes_ref[mixture : mixture + 1]
        onehot = (place_of((experts, tokens), 0) == route).astype(jnp.float32)
        earlier = dot_low(to_low(onehot), to_low(before))
        slot = jnp.sum(earlier * onehot, 0, keepdims=True).astype(jnp.int32)
        quarter = sum((slot >= (part + 1) * share).astype(jnp.int32) for part in range(splits - 1))
        within = slot - quarter * share
        out_ref[2 * mixture : 2 * mixture + 1] = jnp.where(
            quarter == place_ref[0], route * wide + within, -1
        )
        out_ref[2 * mixture + 1 : 2 * mixture + 2] = (
            route * splits + quarter
        ) * wide + within
        if mixture == 0:
            out_ref[0:1] = route * (share * splits) + slot
            out_ref[1:2] = (
                (place_ref[0] - quarter + splits) % splits * experts + route
            ) * share + within


def plan_slots(place, routes, share, wide):
    return whole_call(
        functools.partial(
            plan_kernel, lax.axis_size("dp"), lax.axis_size("hid"), share, wide
        ),
        [shaped((4, routes.shape[1]), jnp.int32)],
        [place],
        [routes],
        1_000_000,
    )[0]


def narrowing(share_rows, wide_rows, share, wide):
    at = place_of((share_rows, wide_rows), 1)
    within = at % wide
    return to_low(
        ((place_of((share_rows, wide_rows), 0) == at // wide * share + within) & (within < share))
        .astype(jnp.float32)
    )


def routing(mixture, experts, normed, router, route):
    column = place_of((normed.shape[0], LANES), 1) - mixture * experts
    inside = (column >= 0) & (column < experts)
    logits = jnp.where(inside, exact_dot(normed, router), -1e30)
    raised = jnp.where(inside, jnp.exp(logits - jnp.max(logits, 1, keepdims=True)), 0.0)
    return raised / jnp.sum(raised, 1, keepdims=True), (column == route).astype(jnp.float32)


def dispatch(mixture, experts, values, gain, router, route, index, slots_ref, gate_ref, chances_ref):
    normed, _, _ = norm_forward(values, gain)
    chosen = (place_of((slots_ref.shape[0], values.shape[0]), 0) == index).astype(jnp.float32)
    slots_ref[...] = to_low(dot_low(to_low(chosen), to_low(normed)))
    chances, onehot = routing(mixture, experts, normed, router, route)
    gate_ref[...] = jnp.sum(chances * onehot, 1, keepdims=True)
    chances_ref[...] = chances


def dispatch_shapes(tokens, wide_rows):
    return [
        shaped((wide_rows, D), jnp.bfloat16),
        shaped((tokens, 1), jnp.float32),
        shaped((tokens, LANES), jnp.float32),
    ]


def start_kernel(
    experts, gain_row, small_ref, features_ref, plan_ref, route_ref, start_ref, turned_ref, *out
):
    bands = features_ref.shape[0]
    start = lax.dot_general(
        features_ref[...],
        to_low(small_ref[:, :bands]),
        (((0,), (1,)), ((), ())),
        preferred_element_type=jnp.float32,
    )
    start_ref[...] = start
    router = small_ref[:, LANES:]
    turned_ref[...] = router.T
    gain = turned_ref[gain_row : gain_row + 1]
    dispatch(0, experts, start, gain, router, route_ref[0], plan_ref[:1], *out)


def start_step(small, features_turned, plan, routes, gain_row, wide_rows):
    tokens = features_turned.shape[1]
    return whole_call(
        functools.partial(start_kernel, lax.axis_size("dp"), gain_row),
        [shaped((tokens, D), jnp.float32), shaped((LANES, D), jnp.float32)]
        + dispatch_shapes(tokens, wide_rows),
        [],
        [small, features_turned, plan, routes],
        700_000_000,
    )


def dispatch_kernel(
    mixture, experts, gain_row, values_ref, small_ref, turned_ref, plan_ref, route_ref, *out
):
    dispatch(
        mixture,
        experts,
        values_ref[...],
        turned_ref[gain_row : gain_row + 1],
        small_ref[:, LANES:],
        route_ref[mixture],
        plan_ref[2 * mixture : 2 * mixture + 1],
        *out,
    )


def dispatch_step(mixture, values, small, turned, plan, routes, gain_row, wide_rows):
    return whole_call(
        functools.partial(dispatch_kernel, mixture, lax.axis_size("dp"), gain_row),
        dispatch_shapes(values.shape[0], wide_rows),
        [],
        [values, small, turned, plan, routes],
        700_000_000,
    )


def expert_pieces(refs, step):
    return refs[step][0], refs[step][1]


def for_all(narrow, total, splits, wide, out_ref):
    rows = dot_left(narrow, to_low(total)).reshape(-1, 1, wide, D)
    copies = jnp.broadcast_to(rows, (rows.shape[0], splits, wide, D))
    out_ref[...] = to_low(copies.reshape(out_ref.shape))


def expert_forward_kernel(splits, share, wide, place_ref, rows_ref, *refs):
    weights, sent_refs, returned_ref = refs[: -splits - 1], refs[-splits - 1 : -1], refs[-1]
    place, count = place_ref[0], sent_refs[0].shape[0] // 2
    narrow = narrowing(count, rows_ref.shape[0], share, wide)
    rows = to_low(dot_low(narrow, rows_ref[...]))
    total = jnp.zeros(rows.shape, jnp.float32)
    for step in range(splits):
        weight_in, weight_out = expert_pieces(weights, step)
        active = dot_low(rows, weight_in)
        hidden = to_low(active * jax.nn.sigmoid(active))
        sent_ref = sent_refs[(splits - step) % splits]
        sent_ref[:count] = rows
        sent_ref[count:] = hidden
        total = total + dot_right(hidden, weight_out)
    for_all(narrow, total, splits, wide, returned_ref)


def expert_backward_kernel(splits, share, wide, place_ref, kept_ref, grad_ref, *refs):
    weights, sent_refs, returned_ref = refs[: -splits - 1], refs[-splits - 1 : -1], refs[-1]
    place, count = place_ref[0], kept_ref.shape[0] // 2
    narrow = narrowing(count, grad_ref.shape[0], share, wide)
    rows, rows_grad = kept_ref[:count], to_low(dot_low(narrow, grad_ref[...]))
    total = jnp.zeros(rows.shape, jnp.float32)
    for step in range(splits):
        weight_in, weight_out = expert_pieces(weights, step)
        active = dot_low(rows, weight_in)
        active_grad = to_low(dot_low(rows_grad, weight_out) * silu_slope(active))
        sent_ref = sent_refs[(splits - step) % splits]
        sent_ref[:count] = rows_grad
        sent_ref[count:] = active_grad
        total = total + dot_right(active_grad, weight_in)
    for_all(narrow, total, splits, wide, returned_ref)


def expert_call(kernel, place, arrays, weights, slots, rows, flops):
    splits, experts = lax.axis_size("hid"), lax.axis_size("dp")
    share, wide = slots
    *sent, returned = whole_call(
        functools.partial(kernel, splits, share, wide),
        [shaped((2 * experts * share, D), jnp.bfloat16)] * splits
        + [shaped((rows.shape[0] * splits, D), jnp.bfloat16)],
        [place],
        [*arrays, *weights],
        flops,
    )
    return sent, returned


def expert_forward(place, rows, weights, slots):
    return expert_call(
        expert_forward_kernel, place, [rows], weights, slots, rows, 4 * rows.shape[0] * D * FF
    )


def expert_backward(place, kept, rows_grad, weights, slots):
    return expert_call(
        expert_backward_kernel,
        place,
        [kept, rows_grad],
        weights,
        slots,
        rows_grad,
        6 * rows_grad.shape[0] * D * FF,
    )


def widen(values, share, wide, out_ref):
    narrow = narrowing(32 * share, 32 * wide, share, wide)
    for block in range(values.shape[0] // narrow.shape[0]):
        part = values[block * narrow.shape[0] : (block + 1) * narrow.shape[0]]
        out_ref[block * narrow.shape[1] : (block + 1) * narrow.shape[1]] = to_low(
            dot_left(narrow, part)
        )


def split_forward_kernel(share, wide, rows_ref, weight_ref, returned_ref):
    active = dot_low(rows_ref[...], weight_ref[0])
    hidden = to_low(active * jax.nn.sigmoid(active))
    widen(to_low(dot_right(hidden, weight_ref[1])), share, wide, returned_ref)


def split_backward_kernel(
    share, wide, rows_ref, grad_ref, weight_ref, hidden_ref, active_grad_ref, returned_ref
):
    active = dot_low(rows_ref[...], weight_ref[0])
    active_grad = to_low(dot_low(grad_ref[...], weight_ref[1]) * silu_slope(active))
    widen(to_low(dot_right(active_grad, weight_ref[0])), share, wide, returned_ref)
    hidden_ref[...] = to_low(active * jax.nn.sigmoid(active))
    active_grad_ref[...] = active_grad


def split_forward(rows, weights, slots):
    share, wide = slots
    return whole_call(
        functools.partial(split_forward_kernel, share, wide),
        [shaped((rows.shape[0] // share * wide, D), jnp.bfloat16)],
        [],
        [rows, weights],
        4 * rows.shape[0] * D * D,
    )[0]


def split_backward(rows, rows_grad, weights, slots):
    share, wide = slots
    return whole_call(
        functools.partial(split_backward_kernel, share, wide),
        [shaped(rows.shape, jnp.bfloat16)] * 2
        + [shaped((rows.shape[0] // share * wide, D), jnp.bfloat16)],
        [],
        [rows, rows_grad, weights],
        6 * rows.shape[0] * D * D,
    )


def sum_kernel(share, wide, splits, moved_ref, out_ref):
    values = moved_ref[...].astype(jnp.float32).reshape(-1, splits, wide, D)
    total = to_low(jnp.sum(values, 1).reshape(-1, D))
    narrow = narrowing(out_ref.shape[0], total.shape[0], share, wide)
    out_ref[...] = to_low(dot_low(narrow, total))


def sum_kernel(share, wide, splits, moved_ref, out_ref):
    values = moved_ref[...].astype(jnp.float32).reshape(-1, splits, wide, D)
    total = to_low(jnp.sum(values, 1).reshape(-1, D))
    narrow = narrowing(out_ref.shape[0], total.shape[0], share, wide)
    out_ref[...] = to_low(dot_low(narrow, total))


def gather_sums(moved, slots):
    share, wide = slots
    splits = lax.axis_size("hid")
    rows = moved.shape[0] // splits // wide * share
    return gather_near(
        whole_call(
            functools.partial(sum_kernel, share, wide, splits),
            [shaped((rows, D), jnp.bfloat16)],
            [],
            [moved],
            50_000_000,
        )[0]
    )


def exchange_all(rows, wide):
    moved = lax.all_to_all(
        rows.reshape(-1, wide, D), ("dp", "hid"), split_axis=0, concat_axis=0, tiled=True
    )
    return moved.reshape(rows.shape)


def combined(position, slots_refs):
    tokens = position.shape[1]
    total, begin = None, 0
    for slots_ref in slots_refs:
        count = slots_ref.shape[0]
        part = min(count, 2 * LANES)
        row = place_of((part, tokens), 0)
        for at in range(0, count, part):
            chosen = to_low((position - (begin + at) == row).astype(jnp.float32))
            found = dot_left(chosen, slots_ref[at : at + part])
            total = found if total is None else total + found
        begin += count
    return total


def combine_kernel(mixture, plan_ref, gate_ref, base_ref, *refs):
    *slots_refs, expert_out_ref, out_ref = refs
    total = combined(plan_ref[2 * mixture + 1 : 2 * mixture + 2], slots_refs)
    expert_out_ref[...] = total
    out_ref[...] = base_ref[...] + 0.5 * gate_ref[...] * total


def combine_step(mixture, plan, gate, base, filled):
    return whole_call(
        functools.partial(combine_kernel, mixture),
        [shaped(base.shape, jnp.float32)] * 2,
        [],
        [plan, gate, base, *filled],
        500_000_000,
    )


def expert_grad_kernel(splits, place_ref, *refs):
    forward, backward, out_ref = refs[:splits], refs[splits : 2 * splits], refs[-1]
    share = forward[0].shape[0] // 2
    for step in range(splits):
        owner = (place_ref[0] + step) % splits
        out_ref[owner, 0] = to_low(dot_left(forward[step][:share], backward[step][share:]))
        out_ref[owner, 1] = to_low(dot_left(backward[step][:share], forward[step][share:]))


def last_grad_kernel(
    splits,
    place_ref,
    rows_ref,
    rows_grad_ref,
    hidden_ref,
    active_grad_ref,
    later_ref,
    out_ref,
    square_ref,
    *refs,
):
    sent_refs, all_ref = refs[:-1], refs[-1]
    all_ref[0] = dot_left(rows_ref[...], active_grad_ref[...])
    all_ref[1] = dot_left(rows_grad_ref[...], hidden_ref[...])
    out_ref[...] = all_ref[:2]
    all_ref[2:] = later_ref[...].astype(jnp.float32)
    square = jnp.zeros((1, D), jnp.float32)
    for part in range(4):
        square = square + jnp.sum(all_ref[part] * all_ref[part], 0, keepdims=True)
    square_ref[...] = square
    for step, sent_ref in enumerate(sent_refs):
        sent_ref[...] = to_low(all_ref[(place_ref[0] + step) % 4])


def expert_grads(place, forward, backward):
    rows, width = forward[0].shape
    splits = len(forward)
    return whole_call(
        functools.partial(expert_grad_kernel, splits),
        [shaped((splits, 2, width, width), jnp.bfloat16)],
        [place],
        [*forward, *backward],
        2 * rows * width * width * splits,
    )[0]


def last_expert_grads(place, rows, rows_grad, hidden, active_grad, later):
    splits, width = lax.axis_size("hid"), later.shape[-1]
    out, square, *sent = whole_call(
        functools.partial(last_grad_kernel, splits),
        [shaped(later.shape, jnp.float32), shaped((1, width), jnp.float32)]
        + [shaped((width, width), jnp.bfloat16)] * splits,
        [place],
        [rows, rows_grad, hidden, active_grad, later],
        4 * rows.shape[0] * width * width,
        [pltpu.VMEM((4, width, width), jnp.float32)],
    )
    return out, square, sent


def attention_forward_kernel(
    gain_row, length_ref, values_ref, turned_ref, weight_ref, branch_ref, out_ref, parts_ref, log_ref, context_ref
):
    values = values_ref[...]
    tokens = values.shape[0]
    normed, _, _ = norm_forward(values, turned_ref[gain_row : gain_row + 1])
    low_normed = to_low(normed)
    for part in range(3):
        parts_ref[part] = to_low(dot_low(low_normed, weight_ref[part]))
    seen = place_of((tokens, tokens), 1) < length_ref[0]
    lane = place_of((tokens, LANES), 1)
    logs = jnp.zeros((tokens, LANES), jnp.float32)
    pair = LANES // HEAD_DIM
    for first in range(0, HEADS, pair):
        columns = slice(first * HEAD_DIM, (first + pair) * HEAD_DIM)
        queries, keys, contents = (parts_ref[part, :, columns] for part in range(3))
        context = jnp.zeros((tokens, LANES), jnp.float32)
        for head in range(pair):
            mine = lane // HEAD_DIM == head
            scores = dot_right(jnp.where(mine, queries, jnp.zeros_like(queries)), keys)
            scores = jnp.where(seen, scores * HEAD_DIM ** (-0.5), -1e30)
            top = jnp.max(scores, 1, keepdims=True)
            raised = jnp.exp(scores - top)
            total = jnp.sum(raised, 1, keepdims=True)
            mixed = dot_low(to_low(raised * (1.0 / total)), contents)
            context = jnp.where(mine, mixed, context)
            logs = jnp.where(lane == first + head, top + jnp.log(total), logs)
        context_ref[:, columns] = to_low(context)
    log_ref[...] = logs
    out_ref[...] = values + dot_low(context_ref[...], branch_ref[0])


def attention_forward(length, values, turned, dense, gain_row):
    tokens = values.shape[0]
    return whole_call(
        functools.partial(attention_forward_kernel, gain_row),
        [
            shaped((tokens, D), jnp.float32),
            shaped((3, tokens, D), jnp.bfloat16),
            shaped((tokens, LANES), jnp.float32),
            shaped((tokens, D), jnp.bfloat16),
        ],
        [length],
        [values, turned, (dense, (3, D, D), (0, 0, 0)), (dense, (1, D, D), (3, 0, 0))],
        4_000_000_000,
    )


def attention_backward_kernel(
    gain_row,
    length_ref,
    place_ref,
    grad_ref,
    values_ref,
    turned_ref,
    weight_ref,
    branch_ref,
    parts_ref,
    log_ref,
    context_ref,
    conv_out_ref,
    linear_ref,
    gating_ref,
    out_ref,
    gain_grad_ref,
    weight_grad_ref,
    low_ref,
    project_ref,
):
    grad = grad_ref[...]
    tokens = grad.shape[0]
    low_grad = to_low(grad)
    low_ref[...] = low_grad
    context_grad = to_low(dot_right(low_grad, branch_ref[0]))
    seen = place_of((tokens, tokens), 1) < length_ref[0]
    lane = place_of((tokens, LANES), 1)
    pair = LANES // HEAD_DIM
    scale = HEAD_DIM ** (-0.5)
    for first in range(0, HEADS, pair):
        columns = slice(first * HEAD_DIM, (first + pair) * HEAD_DIM)
        queries, keys, contents = (parts_ref[part, :, columns] for part in range(3))
        mixed_grad = context_grad[:, columns]
        grads = [jnp.zeros((tokens, LANES), jnp.float32)] * 3
        for head in range(pair):
            mine = lane // HEAD_DIM == head
            none = jnp.zeros_like(queries)
            scores = dot_right(jnp.where(mine, queries, none), keys) * scale
            log_total = jnp.sum(
                jnp.where(lane == first + head, log_ref[...], 0.0), 1, keepdims=True
            )
            weights = jnp.where(seen, jnp.exp(jnp.where(seen, scores, -1e30) - log_total), 0.0)
            weight_grad = dot_right(jnp.where(mine, mixed_grad, none), contents)
            score_grad = to_low(
                weights * (weight_grad - jnp.sum(weight_grad * weights, 1, keepdims=True))
            )
            found = (
                dot_low(score_grad, keys) * scale,
                dot_left(score_grad, queries) * scale,
                dot_left(to_low(weights), mixed_grad),
            )
            grads = [jnp.where(mine, new, old) for new, old in zip(found, grads)]
        for part in range(3):
            project_ref[part, :, columns] = to_low(grads[part])
    gain = turned_ref[gain_row : gain_row + 1]
    normed, unit, inverse = norm_forward(values_ref[...], gain)
    low_normed = to_low(normed)
    normed_grad = sum(dot_right(project_ref[part], weight_ref[part]) for part in range(3))
    back, gain_grad_ref[...] = norm_backward(normed_grad, unit, inverse, gain)
    out_ref[...] = grad + back
    width = weight_grad_ref.shape[1] // 7
    own = pl.ds(pl.multiple_of(place_ref[0] * width, width), width)
    for part in range(3):
        weight_grad_ref[:, part * width : (part + 1) * width] = to_low(
            dot_left(low_normed, project_ref[part, :, own])
        )
    weight_grad_ref[:, 3 * width : 4 * width] = to_low(dot_left(context_ref[...], low_ref[:, own]))
    for number, other_ref in enumerate((conv_out_ref, linear_ref, gating_ref)):
        weight_grad_ref[:, (4 + number) * width : (5 + number) * width] = to_low(other_ref[...])


def attention_backward(length, place, grad, values, turned, dense, kept, others, gain_row):
    tokens = values.shape[0]
    splits = lax.axis_size("hid")
    return whole_call(
        functools.partial(attention_backward_kernel, gain_row),
        [
            shaped((tokens, D), jnp.float32),
            shaped((1, D), jnp.float32),
            shaped((D, 7 * D // splits), jnp.bfloat16),
        ],
        [length, place],
        [
            grad,
            values,
            turned,
            (dense, (3, D, D), (0, 0, 0)),
            (dense, (1, D, D), (3, 0, 0)),
            *kept,
            *others,
        ],
        9_000_000_000,
        [pltpu.VMEM((tokens, D), jnp.bfloat16), pltpu.VMEM((3, tokens, D), jnp.bfloat16)],
        60,
    )


def senone_kernel(
    gain_row, splits, length_ref, place_ref, values_ref, turned_ref, targets_ref, *refs
):
    low_ref, loss_ref, sent_ref = refs[-3 - splits], refs[-2 - splits], refs[-1 - splits]
    logit_refs = refs[-splits:]
    table_ref = refs[0]
    count = table_ref.shape[0]
    rows = values_ref.shape[0] // splits
    place = place_ref[0]
    gain = turned_ref[gain_row : gain_row + 1]
    normed, _, _ = norm_forward(values_ref[...], gain)
    low_ref[...] = to_low(normed)
    own = pl.ds(pl.multiple_of(place * rows, rows), rows)
    normed, unit, inverse = norm_forward(values_ref[own], gain)
    own_rows, targets = to_low(normed), targets_ref[own]
    width = table_ref.shape[2]
    logits, picked = [], []
    for number in range(count):
        begin = (place + splits - number) % splits * width
        logits.append(dot_low(own_rows, table_ref[number]))
        picked.append(place_of((rows, width), 1) + begin == targets)
    top = functools.reduce(
        jnp.maximum, [jnp.max(part, 1, keepdims=True) for part in logits]
    )
    total = sum(jnp.sum(jnp.exp(part - top), 1, keepdims=True) for part in logits)
    target = sum(
        jnp.sum(jnp.where(chosen, part, 0.0), 1, keepdims=True)
        for chosen, part in zip(picked, logits)
    )
    log_total = top + jnp.log(total)
    valid = (place_of((rows, 1), 0) + place * rows < length_ref[0]).astype(jnp.float32)
    loss_ref[...] = jnp.sum(valid * (log_total - target), 0, keepdims=True)
    normed_grad = jnp.zeros((rows, D), jnp.float32)
    for number, (chosen, part) in enumerate(zip(picked, logits)):
        logit_grad = to_low(
            valid * (jnp.exp(part - log_total) - chosen.astype(jnp.float32))
        )
        logit_refs[(splits - number) % splits][...] = logit_grad
        normed_grad = normed_grad + dot_right(logit_grad, table_ref[number])
    own_grad, gain_grad = norm_backward(normed_grad, unit, inverse, gain)
    high, low = two_parts(gain_grad)
    extra = place_of((sent_ref.shape[0] - rows, D), 0)
    sent_ref[:rows] = to_low(own_grad)
    sent_ref[rows:] = to_low(
        jnp.where(
            extra == 0,
            high.astype(jnp.float32),
            jnp.where(extra == 1, low.astype(jnp.float32), 0.0),
        )
    )


def senone_step(length, place, values, turned, targets, tables, gain_row):
    splits, tokens = lax.axis_size("hid"), values.shape[0]
    rows = tokens // splits
    return whole_call(
        functools.partial(senone_kernel, gain_row, splits),
        [
            shaped((tokens, D), jnp.bfloat16),
            shaped((1, 1), jnp.float32),
            shaped((rows + 16, D), jnp.bfloat16),
        ]
        + [shaped((rows, tables.shape[2]), jnp.bfloat16)] * splits,
        [length, place],
        [values, turned, targets, tables],
        1_100_000_000,
        room=60,
    )


def table_grad_kernel(place_ref, low_ref, *refs):
    blocks, out_ref = refs[:-1], refs[-1]
    splits, rows = len(blocks), blocks[0].shape[0]
    total = None
    for step, block in enumerate(blocks):
        begin = pl.multiple_of((place_ref[0] + splits - step) % splits * rows, rows)
        part = dot_left(low_ref[pl.ds(begin, rows)], block[...])
        total = part if total is None else total + part
    out_ref[...] = total


def table_grad(place, low_normed, blocks):
    return whole_call(
        table_grad_kernel,
        [shaped((D, blocks[0].shape[1]), jnp.float32)],
        [place],
        [low_normed, *blocks],
        600_000_000,
    )[0]


def send_back(mixture, grad, plan_ref, gate_ref, rows_ref):
    index = plan_ref[2 * mixture : 2 * mixture + 1]
    chosen = (place_of((rows_ref.shape[0], grad.shape[0]), 0) == index).astype(jnp.float32)
    rows_ref[...] = to_low(dot_low(to_low(chosen), to_low(gate_ref[...] * (0.5 * grad))))


def assemble_kernel(mixture, place_ref, plan_ref, gate_ref, *refs):
    blocks, grad_ref, gain_grad_ref, rows_ref = refs[:-3], refs[-3], refs[-2], refs[-1]
    splits = len(blocks)
    rows = grad_ref.shape[0] // splits
    for step, block in enumerate(blocks):
        begin = pl.multiple_of((place_ref[0] + splits - step) % splits * rows, rows)
        grad_ref[pl.ds(begin, rows)] = block[:rows].astype(jnp.float32)
    gain_grad_ref[...] = sum(
        jnp.sum(block[rows:].astype(jnp.float32), 0, keepdims=True) for block in blocks
    )
    send_back(mixture, grad_ref[...], plan_ref, gate_ref, rows_ref)


def assemble_step(mixture, place, plan, gate, blocks, wide_rows):
    tokens = gate.shape[0]
    return whole_call(
        functools.partial(assemble_kernel, mixture),
        [
            shaped((tokens, D), jnp.float32),
            shaped((1, D), jnp.float32),
            shaped((wide_rows, D), jnp.bfloat16),
        ],
        [place],
        [plan, gate, *blocks],
        200_000_000,
    )


def send_back_kernel(mixture, plan_ref, gate_ref, grad_ref, rows_ref):
    send_back(mixture, grad_ref[...], plan_ref, gate_ref, rows_ref)


def send_back_step(mixture, plan, gate, grad, wide_rows):
    return whole_call(
        functools.partial(send_back_kernel, mixture),
        [shaped((wide_rows, D), jnp.bfloat16)],
        [],
        [plan, gate, grad],
        200_000_000,
    )[0]


def gate_backward_kernel(
    mixture,
    experts,
    gain_row,
    grad_ref,
    expert_out_ref,
    gate_ref,
    chances_ref,
    route_ref,
    values_ref,
    small_ref,
    turned_ref,
    side_ref,
    router_grad_ref,
):
    column = place_of((values_ref.shape[0], LANES), 1) - mixture * experts
    onehot = (column == route_ref[mixture]).astype(jnp.float32)
    gate_grad = jnp.sum(0.5 * grad_ref[...] * expert_out_ref[...], 1, keepdims=True)
    logit_grad = (gate_ref[...] * gate_grad) * (onehot - chances_ref[...])
    normed, _, _ = norm_forward(values_ref[...], turned_ref[gain_row : gain_row + 1])
    router_grad_ref[...] = exact_dot(normed, logit_grad, ((0,), (0,)))
    side_ref[...] = exact_dot(logit_grad, small_ref[:, LANES:], ((1,), (1,)))


def gate_backward(mixture, gain_row, grad, expert_out, gate, chances, routes, values, small, turned):
    return whole_call(
        functools.partial(gate_backward_kernel, mixture, lax.axis_size("dp"), gain_row),
        [shaped(grad.shape, jnp.float32), shaped((D, LANES), jnp.float32)],
        [],
        [grad, expert_out, gate, chances, routes, values, small, turned],
        800_000_000,
    )


def combine_backward_kernel(
    plan_row,
    gain_row,
    plan_ref,
    grad_ref,
    side_ref,
    values_ref,
    turned_ref,
    *refs,
):
    *slots_refs, out_ref, gain_grad_ref = refs
    gain = turned_ref[gain_row : gain_row + 1]
    normed_grad = side_ref[...] + combined(
        plan_ref[plan_row : plan_row + 1], slots_refs
    )
    _, unit, inverse = norm_forward(values_ref[...], gain)
    back, gain_grad_ref[...] = norm_backward(normed_grad, unit, inverse, gain)
    out_ref[...] = grad_ref[...] + back


def combine_backward(plan_row, gain_row, plan, grad, side, values, turned, filled):
    return whole_call(
        functools.partial(combine_backward_kernel, plan_row, gain_row),
        [shaped(grad.shape, jnp.float32), shaped((1, D), jnp.float32)],
        [],
        [plan, grad, side, values, turned, *filled],
        500_000_000,
    )


def pack_grads_kernel(
    owners, grad_ref, features_ref, router_one_ref, router_two_ref, taps_ref, *refs
):
    gain_refs, out_ref, turn_ref = refs[:-2], refs[-2], refs[-1]
    bands, taps = features_ref.shape[0], taps_ref.shape[0]
    turn_ref[...] = jnp.zeros(turn_ref.shape, jnp.float32)
    turn_ref[2 * owners : 2 * owners + taps] = taps_ref[...]
    for number, gain_ref in enumerate(gain_refs):
        at = 2 * owners + taps + number
        turn_ref[at : at + 1] = gain_ref[...]
    out_ref[:, :LANES] = jnp.zeros((D, LANES), jnp.bfloat16)
    out_ref[:, :bands] = to_low(
        lax.dot_general(
            to_low(grad_ref[...]),
            features_ref[...],
            (((0,), (1,)), ((), ())),
            preferred_element_type=jnp.float32,
        )
    )
    out_ref[:, LANES : 2 * LANES] = to_low(
        turn_ref[...].T + router_one_ref[...] + router_two_ref[...]
    )


def pack_grads(grad, features_turned, router_one, router_two, taps_grad, gain_grads):
    return whole_call(
        functools.partial(pack_grads_kernel, lax.axis_size("dp")),
        [shaped((D, 2 * LANES), jnp.bfloat16)],
        [],
        [grad, features_turned, router_one, router_two, taps_grad, *gain_grads],
        60_000_000,
        [pltpu.VMEM((LANES, D), jnp.float32)],
    )[0]


def shares_kernel(place_ref, length_ref, moved_ref, *refs):
    *part_refs, square_ref, loss_ref, share_ref, out_ref = refs
    share = jnp.zeros(share_ref.shape, jnp.float32)
    for owner in range(moved_ref.shape[0]):
        share = share + moved_ref[owner].astype(jnp.float32)
    share_ref[...] = share
    leading = place_ref[0] == 0
    square = jnp.where(leading, jnp.sum(share * share), 0.0) + jnp.sum(square_ref[...])
    for part_ref in part_refs:
        square = square + jnp.sum(part_ref[...] * part_ref[...])
    count = jnp.where(leading, length_ref[0], 0).astype(jnp.float32)
    lane = place_of((1, LANES), 1)
    row = jnp.where(
        lane == 0, square, jnp.where(lane == 1, count, jnp.where(lane == 2, loss_ref[...], 0.0))
    )
    for device in range(out_ref.shape[0]):
        out_ref[device] = row


def shares_step(place, length, moved, parts, squares, loss):
    devices = lax.axis_size("dp") * lax.axis_size("hid")
    return whole_call(
        shares_kernel,
        [shaped(moved.shape[1:], jnp.float32), shaped((devices, 1, LANES), jnp.float32)],
        [place, length],
        [moved, *parts, squares, loss],
        1_000_000,
    )


def summed(moved):
    owners = lax.axis_size("dp")
    return jnp.sum(moved.reshape(owners, D // owners, -1).astype(jnp.float32), 0)


def totals_of(ref):
    rows = jnp.sum(ref[...], 0)
    lane = place_of(rows.shape, 1)
    square, count, loss = (jnp.sum(jnp.where(lane == part, rows, 0.0)) for part in range(3))
    norm = jnp.sqrt(square) / count
    return count, loss, norm, jnp.minimum(1.0, clip_limit / (norm + 1e-06)) / count


def orthogonal_kernel(pieces, experts, place_ref, totals_ref, *refs):
    momentum_refs, grad_refs = refs[:pieces], refs[pieces : 2 * pieces]
    out_refs, matrix_ref = refs[2 * pieces : 3 * pieces], refs[3 * pieces]
    _, _, _, factor = totals_of(totals_ref)
    gram = jnp.zeros((D, D), jnp.float32)
    for piece in range(pieces):
        current = to_low(
            muon_beta * momentum_refs[piece][...].astype(jnp.float32)
            + factor * grad_refs[piece][...].astype(jnp.float32)
        )
        matrix_ref[piece] = current
        gram = gram + dot_right(current, current)
    row, column = place_of((D, D), 0), place_of((D, D), 1)
    square = jnp.sum(jnp.where(row == column, gram, 0.0))
    inverse = 1.0 / (jnp.sqrt(square) + 1e-07)
    gram = gram * (inverse * inverse)
    identity = jnp.where(row == column, newton_first, 0.0)
    total = None
    for turn in range(5):
        parts = two_parts(gram)
        poly = identity + newton_second * gram + newton_third * close_dot(parts, parts)
        poly_parts = two_parts(poly)
        total = poly if total is None else close_dot(poly_parts, two_parts(total))
        if turn < 4:
            gram = close_dot(poly_parts, two_parts(close_dot(poly_parts, parts)))
    kind_scale = jnp.where(
        place_ref[0] % 2 == 0,
        D ** (-0.5) * muon_rate * FF**0.5,
        3 * experts * FF ** (-0.5) * muon_rate * FF**0.5,
    )
    total_parts = two_parts(total * (inverse * kind_scale))
    for piece in range(pieces):
        out_refs[piece][...] = to_low(
            sum(dot_low(part, matrix_ref[piece]) for part in total_parts)
        )


def orthogonal(place, totals, momentum, grads):
    pieces = len(momentum)
    return whole_call(
        functools.partial(orthogonal_kernel, pieces, lax.axis_size("dp")),
        [shaped((D, D), jnp.bfloat16)] * pieces,
        [place],
        [totals, *momentum, *grads],
        17_000_000_000,
        [pltpu.VMEM((pieces, D, D), jnp.bfloat16)],
        60,
    )


def momentum_kernel(totals_ref, momentum_ref, one_ref, two_ref, out_ref):
    _, _, _, factor = totals_of(totals_ref)
    first = pl.program_id(0) < 2
    grad = jnp.where(first, one_ref[0], two_ref[0].astype(jnp.float32))
    out_ref[0] = muon_beta * momentum_ref[0] + factor * grad


def momentum_update(totals, momentum, grads_one, grads_two):
    block = (1,) + momentum.shape[1:]
    return pl.pallas_call(
        momentum_kernel,
        grid=(4,),
        out_shape=shaped(momentum.shape, jnp.float32),
        in_specs=[
            pl.BlockSpec(totals.shape, lambda step: (0, 0, 0)),
            pl.BlockSpec(block, lambda step: (step, 0, 0)),
            pl.BlockSpec(block, lambda step: (jnp.minimum(step, 1), 0, 0)),
            pl.BlockSpec(block, lambda step: (jnp.maximum(step - 2, 0), 0, 0)),
        ],
        out_specs=pl.BlockSpec(block, lambda step: (step, 0, 0)),
        compiler_params=pltpu.CompilerParams(vmem_limit_bytes=32 * 1024 * 1024),
        cost_estimate=pl.CostEstimate(
            flops=3_000_000, bytes_accessed=12_000_000, transcendentals=0
        ),
    )(totals, momentum, grads_one, grads_two)


def update_kernel(place_ref, weight_ref, *refs):
    out_ref, turn = refs[-1], pl.program_id(0)
    for step, update_ref in enumerate(refs[:-1]):

        @pl.when(turn == step)
        def _():
            out_ref[0] = (1.0 - muon_decay) * weight_ref[0] - update_ref[...].astype(jnp.float32)


def expert_update(place, weights, updates):
    count = weights.shape[0]

    def turned(step, place_ref):
        return ((place_ref[0] + step) % count, 0, 0)

    block = (1,) + weights.shape[1:]
    return pl.pallas_call(
        update_kernel,
        out_shape=jax.ShapeDtypeStruct(weights.shape, jnp.float32),
        grid_spec=pltpu.PrefetchScalarGridSpec(
            num_scalar_prefetch=1,
            grid=(count,),
            in_specs=[pl.BlockSpec(block, turned)]
            + [pl.BlockSpec(update.shape, lambda step, place_ref: (0, 0)) for update in updates],
            out_specs=pl.BlockSpec(block, turned),
        ),
        compiler_params=pltpu.CompilerParams(vmem_limit_bytes=32 * 1024 * 1024),
        cost_estimate=pl.CostEstimate(
            flops=3_000_000, bytes_accessed=10_000_000, transcendentals=0
        ),
    )(place, weights, *updates)


def adam_update(weight, grad, first, second, rate, decay):
    first_new = beta_one * first + (1.0 - beta_one) * grad
    second_new = beta_two * second + (1.0 - beta_two) * grad * grad
    corrected = (
        first_new
        / (1.0 - beta_one**STEP)
        / (jnp.sqrt(second_new / (1.0 - beta_two**STEP)) + adam_epsilon)
    )
    return (first_new, second_new, weight - rate * (corrected + decay * weight))


def adam_kernel(owners, splits, place_ref, totals_ref, share_ref, senone_ref, *refs):
    blocks, states = refs[:splits], refs[splits : splits + 24]
    outs, scalars_ref = refs[splits + 24 : splits + 48], refs[splits + 48]
    turn_ref, gather_ref = refs[splits + 49 :]
    count, loss, norm, factor = totals_of(totals_ref)
    lane = place_of((1, LANES), 1)
    scalars_ref[...] = jnp.where(
        lane == 0, loss, jnp.where(lane == 1, count, jnp.where(lane == 2, norm, 0.0))
    )
    width = blocks[0].shape[1] // 7
    for step, block in enumerate(blocks):
        begin = pl.multiple_of((place_ref[0] + splits - step) % splits * width, width)
        for part in range(7):
            gather_ref[part, :, pl.ds(begin, width)] = block[:, part * width : (part + 1) * width]
    own = share_ref.shape[0]
    bands = states[0].shape[1]
    taps, gains = states[4].shape[0], states[7].shape[0]
    turn_ref[...] = jnp.zeros(turn_ref.shape, jnp.float32)
    turn_ref[:own] = share_ref[:, LANES : 2 * LANES]
    turned = turn_ref[...].T
    begin = 2 * owners

    def apply(number, at, grad, rate=adam_rate, decay=weight_decay):
        first, second, weight = (states[number + 8 * part] for part in (1, 2, 0))
        found = adam_update(weight[at], grad * factor, first[at], second[at], rate, decay)
        for ref, value in zip(outs[3 * number : 3 * number + 3], found):
            ref[at] = value

    everything = (slice(None), slice(None))
    apply(0, everything, share_ref[:, :bands])
    for part in range(3):
        apply(1, (slice(None), slice(part * D, (part + 1) * D)), gather_ref[part])
    for part in range(2):
        apply(2, (part,), gather_ref[3 + part])
        apply(3, (slice(None), slice(part * D, (part + 1) * D)), gather_ref[5 + part])
        apply(
            5,
            (part,),
            share_ref[:, LANES + part * owners : LANES + (part + 1) * owners],
        )
    apply(4, everything, turned[begin : begin + taps, :own])
    apply(6, everything, senone_ref[...])
    apply(7, everything, turned[begin + taps : begin + taps + gains, :own], gain_rate, 0.0)


def adam_step(place, totals, share, senone_share, blocks, weights, firsts, seconds):
    rows, splits = share.shape[0], len(blocks)
    outs = [shaped(part.shape, jnp.float32) for part in weights for _ in range(3)]
    return whole_call(
        functools.partial(adam_kernel, lax.axis_size("dp"), splits),
        outs + [shaped((1, LANES), jnp.float32)],
        [place],
        [totals, share, senone_share, *blocks, *weights, *firsts, *seconds],
        4_000_000,
        [
            pltpu.VMEM((LANES, LANES), jnp.float32),
            pltpu.VMEM((7, rows, D), jnp.float32),
        ],
    )


def convolution_forward(values, gains, weight_in, depth, weight_out, valid):
    tokens = values.shape[0]
    normed, unit, inverse = norm_forward(values, gains[2])
    low_normed = to_low(normed)
    linear = dot_low(low_normed, weight_in[0])
    gating = jax.nn.sigmoid(dot_low(low_normed, weight_in[1]))
    mixed = linear * gating * valid[:, None]
    reach = (depth.shape[0] - 1) // 2
    padded = jnp.pad(mixed, ((reach, reach), (0, 0)))
    deep = jnp.zeros_like(mixed)
    for offset in range(depth.shape[0]):
        deep = deep + depth[offset] * padded[offset : offset + tokens]
    count = jnp.sum(valid)
    mask = valid[:, None]
    mean = jnp.sum(mask * deep, 0) / count
    spread = jnp.sum(mask * deep * deep, 0) / count - mean * mean
    scale = lax.rsqrt(spread + 1e-05)
    unit_batch = (deep - mean) * scale
    shifted = unit_batch * gains[5] + gains[6]
    activated = to_low(jax.nn.silu(shifted))
    kept = (
        unit,
        inverse,
        low_normed,
        linear,
        gating,
        padded,
        scale,
        unit_batch,
        shifted,
        activated,
    )
    return (values + dot_low(activated, weight_out), kept)


def convolution_backward(grad, gains, weight_in, depth, weight_out, valid, kept):
    unit, inverse, low_normed, linear, gating, padded, scale, unit_batch, shifted, activated = kept
    tokens = grad.shape[0]
    low_grad = to_low(grad)
    out_grad = dot_left(activated, own_part(low_grad, 1))
    shifted_grad = dot_right(low_grad, weight_out) * silu_slope(shifted)
    gamma_grad = jnp.sum(shifted_grad * unit_batch, 0)
    beta_grad = jnp.sum(shifted_grad, 0)
    unit_grad = shifted_grad * gains[5]
    count = jnp.sum(valid)
    mask = valid[:, None]
    first_sum = jnp.sum(mask * unit_grad, 0) / count
    second_sum = jnp.sum(mask * unit_grad * unit_batch, 0) / count
    deep_grad = scale * (unit_grad - mask * (first_sum + unit_batch * second_sum))
    reach = (depth.shape[0] - 1) // 2
    padded_grad = jnp.pad(deep_grad, ((reach, reach), (0, 0)))
    mixed_grad = jnp.zeros_like(deep_grad)
    depth_rows = []
    for offset in range(depth.shape[0]):
        begin = 2 * reach - offset
        mixed_grad = mixed_grad + depth[offset] * padded_grad[begin : begin + tokens]
        depth_rows.append(jnp.sum(deep_grad * padded[offset : offset + tokens], 0))
    mixed_grad = mixed_grad * mask
    project_grad = [
        to_low(mixed_grad * gating),
        to_low(mixed_grad * linear * gating * (1.0 - gating)),
    ]
    in_grad = [dot_left(low_normed, own_part(part, 1)) for part in project_grad]
    normed_grad = sum(dot_right(part, weight_in[place]) for place, part in enumerate(project_grad))
    values_grad, gain_grad = norm_backward(normed_grad, unit, inverse, gains[2])
    return (
        grad + values_grad,
        gain_grad,
        gamma_grad[None],
        beta_grad[None],
        in_grad,
        jnp.stack(depth_rows),
        out_grad,
    )


def on_device(
    features,
    lengths,
    routes,
    alignments,
    input_weight,
    attention_in,
    branch_out,
    pointwise_in,
    depthwise,
    router,
    senone_table,
    norm_scales,
    expert_weights,
    input_first,
    input_second,
    attention_first,
    attention_second,
    branch_first,
    branch_second,
    pointwise_first,
    pointwise_second,
    depthwise_first,
    depthwise_second,
    router_first,
    router_second,
    senone_first,
    senone_second,
    scales_first,
    scales_second,
    expert_momentum,
):
    owners, splits = lax.axis_size("dp"), lax.axis_size("hid")
    tokens = features.shape[0]
    taps, gains = depthwise.shape[0], norm_scales.shape[0]
    place = lax.axis_index("hid")
    place_array = place[None].astype(jnp.int32)
    gain_begin = 2 * owners + taps
    share = 3 * tokens // (2 * owners) // splits
    wide = -(-share // 8) * 8
    slots, wide_rows = (share, wide), owners * wide

    low_one, low_two = to_low(expert_weights[0, :, 0]), to_low(expert_weights[1, :, 0])
    momentum_pieces = expert_momentum.reshape((2 * 2,) + expert_momentum.shape[3:])
    owned_momentum = spread(
        [to_low(momentum_pieces[(place + step) % splits]) for step in range(splits)]
    )
    small = pack_small(input_weight.T, router, depthwise, norm_scales)
    small = exchange_rows(small.reshape(owners * small.shape[1], -1))
    small, owned_momentum[2] = together(small, owned_momentum[2])
    dense = lax.all_gather(
        pack_dense(attention_in, branch_out, pointwise_in), "dp", axis=1, tiled=True
    )
    valid = (jnp.arange(tokens, dtype=jnp.int32) < lengths[0]).astype(jnp.float32)
    plan = plan_slots(place_array, routes[:, :, 0], share, wide)
    targets = alignments[:, None]
    features_turned = features.T

    start, turned, rows, gate_one, chances_one = start_step(
        small, features_turned, plan, routes, gain_begin, owners * share * splits
    )
    depth_full = turned[2 * owners : gain_begin]
    scales_full = turned[gain_begin : gain_begin + gains]
    rows_one, owned_momentum[1], owned_momentum[3] = together(
        exchange_rows(rows), owned_momentum[1], owned_momentum[3]
    )
    returned, senone_low = together(
        split_forward(rows_one, low_one, slots), to_low(senone_table)
    )
    moved, *senone_rows = together(exchange_all(returned, wide), *gather_near(senone_low))
    tables = lax.all_gather(jnp.stack(senone_rows), "dp", axis=1, tiled=True)
    expert_out_one, first = combine_step(0, plan, gate_one, start, gather_sums(moved, slots))

    first, low_two = together(first, low_two)
    weights_two = gather_near(low_two)
    second, *kept_attend = attention_forward(lengths, first, turned, dense, gain_begin + 1)
    third, kept_convolve = convolution_forward(
        second, scales_full, dense[5:7], depth_full, dense[4], valid
    )

    rows, gate_two, chances_two = dispatch_step(
        1, third, small, turned, plan, routes, gain_begin + 3, wide_rows
    )
    forward_two, returned = expert_forward(place_array, exchange_rows(rows), weights_two, slots)
    filled = exchange_all(returned, wide)
    expert_out_two, fourth = combine_step(1, plan, gate_two, third, [filled])

    low_normed, loss_local, sent, *logit_grad = senone_step(
        lengths, place_array, fourth, turned, targets, tables, gain_begin + 4
    )
    grad, gain_five, rows = assemble_step(
        1, place_array, plan, gate_two, gather_near(sent), wide_rows
    )

    rows_grad = exchange_rows(rows)
    side, router_two = gate_backward(
        1,
        gain_begin + 3,
        grad,
        expert_out_two,
        gate_two,
        chances_two,
        routes,
        third,
        small,
        turned,
    )
    logit_grad = spread(logit_grad)
    rows_grad, side, *logit_grad[1:] = together(rows_grad, side, *logit_grad[1:])
    backward_two, returned = expert_backward(
        place_array, forward_two[0], rows_grad, weights_two, slots
    )
    filled = exchange_all(returned, wide)
    experts_two = lax.psum_scatter(
        expert_grads(place_array, forward_two, backward_two), "hid", scatter_dimension=0
    )
    grad, gain_four = combine_backward(
        3, gain_begin + 3, plan, grad, side, third, turned, [filled]
    )
    senone_share = lax.psum_scatter(
        table_grad(place_array, low_normed, logit_grad), "dp", scatter_dimension=0, tiled=True
    )
    grad, gain_three, gamma_grad, beta_grad, pointwise_grad, depth_grad, conv_out_grad = (
        convolution_backward(
            grad, scales_full, dense[5:7], depth_full, dense[4], valid, kept_convolve
        )
    )
    grad, gain_two, attend_grad = attention_backward(
        lengths,
        place_array,
        grad,
        first,
        turned,
        dense,
        kept_attend,
        [conv_out_grad] + pointwise_grad,
        gain_begin + 1,
    )

    rows_grad = exchange_rows(
        send_back_step(0, plan, gate_one, grad, owners * share * splits)
    )
    hidden, active_grad, returned = split_backward(rows_one, rows_grad, low_one, slots)
    moved = exchange_all(returned, wide)
    side, router_one = gate_backward(
        0, gain_begin, grad, expert_out_one, gate_one, chances_one, routes, start, small, turned
    )
    experts_one, squares, sent = last_expert_grads(
        place_array, rows_one, rows_grad, hidden, active_grad, experts_two
    )
    moved, side, early = together(moved, side, attend_grad)
    early_moved = exchange_rows(early)
    *filled, squares = together(*gather_sums(moved, slots), squares)
    grad, gain_one = combine_backward(1, gain_begin, plan, grad, side, start, turned, filled)
    last = pack_grads(
        grad,
        features_turned,
        router_one,
        router_two,
        depth_grad,
        [gain_one, gain_two, gain_three, gain_four, gain_five, gamma_grad, beta_grad],
    )
    early_share = summed(early_moved)
    last, sent = together(last, tuple(sent))
    blocks = gather_near(early_share)
    owned_grad = spread(sent)
    moved = exchange_rows(last)
    last_share, totals = shares_step(
        place_array,
        lengths,
        moved.reshape(owners, D // owners, -1),
        [senone_share, early_share],
        squares,
        loss_local,
    )
    totals = lax.all_to_all(totals, ("dp", "hid"), split_axis=0, concat_axis=0, tiled=True)

    totals, blocks = together(totals, tuple(blocks))
    orth = orthogonal(place_array, totals, owned_momentum, owned_grad)
    returned = [orth[0]] + [shift(orth[step], -step) for step in range(1, splits)]
    momentum_new = momentum_update(totals, momentum_pieces, experts_one, experts_two)
    *updated, scalars = adam_step(
        place_array,
        totals,
        last_share,
        senone_share,
        blocks,
        [
            input_weight.T,
            attention_in,
            branch_out,
            pointwise_in,
            depthwise,
            router,
            senone_table,
            norm_scales,
        ],
        [
            input_first.T,
            attention_first,
            branch_first,
            pointwise_first,
            depthwise_first,
            router_first,
            senone_first,
            scales_first,
        ],
        [
            input_second.T,
            attention_second,
            branch_second,
            pointwise_second,
            depthwise_second,
            router_second,
            senone_second,
            scales_second,
        ],
    )
    experts_new = expert_update(
        place_array, expert_weights.reshape(momentum_pieces.shape), returned
    )
    return (
        scalars[0, 0],
        scalars[0, 1],
        scalars[0, 2],
        *[part.T for part in updated[:3]],
        *updated[3:],
        momentum_new.reshape(expert_momentum.shape),
        experts_new.reshape(expert_weights.shape),
    )


def solution(mesh):
    return jax.shard_map(
        on_device,
        mesh=mesh,
        in_specs=(
            P("dp", None),
            P("dp"),
            P(None, "dp", None),
            P("dp"),
            P(None, "dp"),
            P("dp", None),
            P(None, "dp", None),
            P("dp", None),
            P(None, "dp"),
            P(None, "dp", None),
            P("dp", "hid"),
            P(None, "dp"),
            P(None, None, "dp", None, "hid"),
            P(None, "dp"),
            P(None, "dp"),
            P("dp", None),
            P("dp", None),
            P(None, "dp", None),
            P(None, "dp", None),
            P("dp", None),
            P("dp", None),
            P(None, "dp"),
            P(None, "dp"),
            P(None, "dp", None),
            P(None, "dp", None),
            P("dp", "hid"),
            P("dp", "hid"),
            P(None, "dp"),
            P(None, "dp"),
            P(None, None, "dp", None, "hid"),
        ),
        out_specs=(
            P(),
            P(),
            P(),
            P(None, "dp"),
            P(None, "dp"),
            P(None, "dp"),
            P("dp", None),
            P("dp", None),
            P("dp", None),
            P(None, "dp", None),
            P(None, "dp", None),
            P(None, "dp", None),
            P("dp", None),
            P("dp", None),
            P("dp", None),
            P(None, "dp"),
            P(None, "dp"),
            P(None, "dp"),
            P(None, "dp", None),
            P(None, "dp", None),
            P(None, "dp", None),
            P("dp", "hid"),
            P("dp", "hid"),
            P("dp", "hid"),
            P(None, "dp"),
            P(None, "dp"),
            P(None, "dp"),
            P(None, None, "dp", None, "hid"),
            P(None, None, "dp", None, "hid"),
        ),
        check_vma=False,
    )
```
